32 devices in a mesh: rows: 8 (over z, y), seq: 4 (over x, core).
Axes of the slice: x: 2, y: 2, z: 4, core: 2. Of those that a mesh axis runs over, the one named last changes fastest.
Arguments:
- block_in: bfloat16 [16, 2048, 768], P('rows', 'seq'), may hold values from -6 to 6
- lengths: int32 [16, 8], P('rows'), may hold values from 1 to 1536, 2048 in all within a row
- attn_gain: float32 [768], replicated, may hold values from 0.1 to 1.9
- attn_bias: float32 [768], replicated, may hold values from -1.75 to 1.75
- feed_gain: float32 [768], replicated, may hold values from 0.1 to 1.9
- feed_bias: float32 [768], replicated, may hold values from -1.75 to 1.75
- joint_weight: bfloat16 [768, 2304], replicated, may hold values from -0.21875 to 0.21875
- joint_bias: float32 [2304], replicated, may hold values from -1.75 to 1.75
- dense_weight: bfloat16 [768, 768], replicated, may hold values from -1.25 to 1.25
- dense_bias: float32 [768], replicated, may hold values from -1.75 to 1.75
- expand_weight: bfloat16 [768, 3072], replicated, may hold values from -0.21875 to 0.21875
- expand_bias: float32 [3072], replicated, may hold values from -1.75 to 1.75
- contract_weight: bfloat16 [3072, 768], replicated, may hold values from -0.109375 to 0.109375
- contract_bias: float32 [768], replicated, may hold values from -1.75 to 1.75
- out_cotangent: bfloat16 [16, 2048, 768], P('rows', 'seq'), may hold values from -6 to 6
Outputs:
- block_out: bfloat16 [16, 2048, 768], P('rows', 'seq')
- input_grad: bfloat16 [16, 2048, 768], P('rows', 'seq')
- grad_attn_gain: float32 [768], replicated
- grad_attn_bias: float32 [768], replicated
- grad_feed_gain: float32 [768], replicated
- grad_feed_bias: float32 [768], replicated
- grad_joint_weight: float32 [768, 2304], replicated
- grad_joint_bias: float32 [2304], replicated
- grad_dense_weight: float32 [768, 768], replicated
- grad_dense_bias: float32 [768], replicated
- grad_expand_weight: float32 [768, 3072], replicated
- grad_expand_bias: float32 [3072], replicated
- grad_contract_weight: float32 [3072, 768], replicated
- grad_contract_bias: float32 [768], replicated
The draws below stay inside these ranges and needn't reach their ends.
Inputs may be any that keep to these rules, and one draw needn't show every extreme that they name: In each row the 8 lengths add up to 2048, and one of them is exactly 1536.
All inputs are finite; a program needn't handle non-finite values.
Results may differ from the reference program's by a relative error of at most 0.0095.
Values may be sent and summed in bfloat16 or wider, within the bound.
No kernel may reach another device: no remote copies, remote signals or barrier semaphores. Data moves between devices by JAX's collectives and lax.ppermute only.
A program may use at most 256 MiB of HBM per device.

```python
import math
import jax
import jax.numpy as jnp
import numpy as np
from jax import lax

D = 768
H = 12
FF = 3072
HD = 64
RD = 16
LENGTH = 2048
SEGS = 8
ROWS = 16


def shard_levels(rng, dims, split, smallest, largest):
    level = 1.0
    for dim, parts in split:
        heights = jax.random.uniform(jax.random.fold_in(jax.random.fold_in(rng, 6), dim), (parts,), jnp.float32, smallest / len(split), largest / len(split))
        level = level * jnp.repeat(jnp.exp(heights), dims[dim] // parts).reshape((-1,) + (1,) * (len(dims) - 1 - dim))
    return level


def split_up(amount, total, bound, skew):
    portions = [(1 << 20) // math.isqrt(rank ** skew) + 1 for rank in range(2, amount + 1)]
    rest, given = total - bound - (amount - 1), [1] * (amount - 1)
    while rest > 0:
        movable = [i for i in range(amount - 1) if given[i] < bound]
        whole, remaining = sum([portions[i] for i in movable]), rest
        for i in movable:
            more = min(bound - given[i], max(1, remaining * portions[i] // whole), rest)
            given[i] = given[i] + more
            rest = rest - more
    return np.array([bound] + given)


def uneven(stream_key, amount, total, reach, lean):
    if amount == 2:
        one = jax.random.randint(stream_key, (), max(1, total - reach), min(reach, total - 1) + 1)
        return jnp.stack([one, total - one])
    tallies = jnp.asarray(split_up(amount, total, reach, lean), jnp.int32)
    pairs = (amount - 1) // 2
    source_of, receiver = tallies[1:1 + 2 * pairs:2], tallies[2:2 + 2 * pairs:2]
    margin = jnp.minimum(source_of - 1, reach - receiver)
    passed = jax.random.randint(jax.random.fold_in(stream_key, 1), (pairs,), 0, 1 << 20) % (margin + 1)
    tallies = tallies.at[1:1 + 2 * pairs:2].set(source_of - passed).at[2:2 + 2 * pairs:2].set(receiver + passed)
    return tallies[jax.random.permutation(jax.random.fold_in(stream_key, 2), amount)]


def noise(stream_key, shape, scale, bound, cuts=(), held_as=jnp.bfloat16):
    array = jax.random.normal(stream_key, shape, jnp.float32) * scale
    if len(cuts) > 0:
        array = shard_levels(stream_key, shape, cuts, -0.22, 0.18) * array
    return jnp.clip(array, min=-bound, max=bound).astype(held_as)


def setup_inputs(seed: int = 0) -> dict:
    key_of = jax.random.split(jax.random.key(seed), 16)
    block_in = noise(key_of[0], (ROWS, LENGTH, D), 1.0, 6.0, ((0, 8), (1, 4)))
    lengths = jax.vmap(lambda own: uneven(own, SEGS, LENGTH, 3 * LENGTH // 4, 2))(jax.random.split(key_of[1], ROWS)).reshape((ROWS, SEGS)).astype(jnp.int32)
    attn_gain = jnp.clip(1.0 + 0.18 * jax.random.normal(key_of[2], (D,), jnp.float32), 0.1, 1.9)
    attn_bias = noise(key_of[3], (D,), 0.3, 1.75, (), jnp.float32)
    feed_gain = jnp.clip(1.0 + 0.18 * jax.random.normal(key_of[4], (D,), jnp.float32), 0.1, 1.9)
    feed_bias = noise(key_of[5], (D,), 0.3, 1.75, (), jnp.float32)
    joint_weight = noise(key_of[6], (D, 3 * D), D ** -0.5, 0.21875)
    joint_bias = noise(key_of[7], (3 * D,), 0.3, 1.75, (), jnp.float32)
    dense_weight = noise(key_of[8], (D, D), (D // 32) ** -0.5, 1.25)
    dense_bias = noise(key_of[9], (D,), 0.3, 1.75, (), jnp.float32)
    expand_weight = noise(key_of[10], (D, FF), D ** -0.5, 0.21875)
    expand_bias = noise(key_of[11], (FF,), 0.3, 1.75, (), jnp.float32)
    contract_weight = noise(key_of[12], (FF, D), FF ** -0.5, 0.109375)
    contract_bias = noise(key_of[13], (D,), 0.3, 1.75, (), jnp.float32)
    out_cotangent = noise(key_of[14], (ROWS, LENGTH, D), 1.0, 6.0, ((0, 8), (1, 4)))
    return dict(block_in=block_in, lengths=lengths, attn_gain=attn_gain, attn_bias=attn_bias, feed_gain=feed_gain, feed_bias=feed_bias, joint_weight=joint_weight, joint_bias=joint_bias, dense_weight=dense_weight, dense_bias=dense_bias, expand_weight=expand_weight, expand_bias=expand_bias, contract_weight=contract_weight, contract_bias=contract_bias, out_cotangent=out_cotangent)


@jax.custom_vjp
def low(v):
    return lax.optimization_barrier(v.astype(jnp.bfloat16)).astype(jnp.float32)

@jax.custom_vjp
def low_back(v):
    return v

def low_keep(v):
    return (low(v), None)

def low_pass(kept, grad):
    return (grad,)

def back_keep(v):
    return (v, None)

def back_low(kept, grad):
    return (low(grad),)
low.defvjp(low_keep, low_pass)
low_back.defvjp(back_keep, back_low)
EPSILON = 1e-05
BASE_FREQ = 10000.0
NEGATIVE = -1e+30
HIGHEST = lax.Precision.HIGHEST

def layer_norm(values, gain_vector, bias_vector):
    centered = values - lax.optimization_barrier(jnp.mean(values, axis=-1, keepdims=True))
    spread = lax.optimization_barrier(jnp.mean(centered * centered, axis=-1, keepdims=True))
    return centered * lax.rsqrt(spread + EPSILON) * gain_vector + bias_vector

def rotate(values, places, direction):
    halfway = RD // 2
    inverse = BASE_FREQ ** (-2.0 * jnp.arange(halfway).astype(jnp.float32) / RD)
    angles = direction * places.astype(jnp.float32)[:, None] * inverse[None, :]
    cosine = jnp.cos(angles)[:, None, :]
    sine_part = jnp.sin(angles)[:, None, :]
    first_half = values[..., :halfway]
    second = values[..., halfway:RD]
    return jnp.concatenate([first_half * cosine - second * sine_part, second * cosine + first_half * sine_part, values[..., RD:]], axis=-1)

def segment_ids(row_lengths, total_len):
    bounds = jnp.cumsum(row_lengths[..., :-1], axis=-1).astype(jnp.int32)
    places = jnp.arange(total_len, dtype=jnp.int32)
    return lax.optimization_barrier(jnp.sum((places[:, None] >= bounds[..., None, :]).astype(jnp.int32), axis=-1)).astype(jnp.int32)

def forward(row_in, row_seg, attn_gain, attn_bias, feed_gain, feed_bias, joint_weight, joint_bias, dense_weight, dense_bias, expand_weight, expand_bias, contract_weight, contract_bias):
    total_len = row_in.shape[0]
    score_scale = HD ** (-0.5)
    normed_attn = low(layer_norm(row_in, attn_gain, attn_bias))
    normed_feed = low(layer_norm(row_in, feed_gain, feed_bias))
    joint_all = low_back(jnp.dot(normed_attn, joint_weight, precision=HIGHEST) + joint_bias).reshape(total_len, 3, H, HD)
    places = jnp.arange(total_len, dtype=jnp.int32)
    queries = low(rotate(joint_all[:, 0], places, 1.0))
    key_rows = low(rotate(joint_all[:, 1], places, 1.0))
    value_rows = low(joint_all[:, 2])
    query_block = min(512, total_len)
    block_count = total_len // query_block

    def attend(pieces):
        query_part, place_part, seg_part = pieces
        scores = low_back(jnp.einsum('qhd,khd->hqk', query_part, key_rows, precision=HIGHEST) * score_scale)
        allowed = (places[None, :] <= place_part[:, None]) & (row_seg[None, :] == seg_part[:, None])
        scores = jnp.where(allowed[None], scores, NEGATIVE)
        prob_low = low(jax.nn.softmax(scores, axis=-1))
        return jnp.einsum('hqk,khd->qhd', prob_low, value_rows, precision=HIGHEST)
    outputs = lax.map(jax.checkpoint(attend), (queries.reshape(block_count, query_block, H, HD), places.reshape(block_count, query_block), row_seg.reshape(block_count, query_block)))
    mixed_out = low(low_back(outputs.reshape(total_len, D)))
    hidden = low_back(jnp.dot(normed_feed, expand_weight, precision=HIGHEST) + expand_bias)
    activated = low(jax.nn.gelu(hidden, approximate=False))
    attn_branch = jnp.dot(mixed_out, dense_weight, precision=HIGHEST) + dense_bias
    feed_branch = jnp.dot(activated, contract_weight, precision=HIGHEST) + contract_bias
    return row_in + attn_branch + feed_branch

def reference(block_in, lengths, attn_gain, attn_bias, feed_gain, feed_bias, joint_weight, joint_bias, dense_weight, dense_bias, expand_weight, expand_bias, contract_weight, contract_bias, out_cotangent):
    params = tuple((item.astype(jnp.float32) for item in (attn_gain, attn_bias, feed_gain, feed_bias, joint_weight, joint_bias, dense_weight, dense_bias, expand_weight, expand_bias, contract_weight, contract_bias)))
    seg_all = segment_ids(lengths, LENGTH)
    starting = tuple((jnp.zeros(item.shape, jnp.float32) for item in params))

    def per_row(totals, pieces):
        row_in, row_seg, row_cot = pieces
        result, backward = jax.vjp(lambda given, *weights: forward(given, row_seg, *weights), row_in.astype(jnp.float32), *params)
        gradients = backward(row_cot.astype(jnp.float32))
        updated = tuple((total + gradient for total, gradient in zip(totals, gradients[1:])))
        return (updated, (result.astype(jnp.bfloat16), gradients[0].astype(jnp.bfloat16)))
    totals, (outputs, in_grads) = lax.scan(per_row, starting, (block_in, seg_all, out_cotangent))
    return (outputs, in_grads, totals[0], totals[1], totals[2], totals[3], totals[4], totals[5], totals[6], totals[7], totals[8], totals[9], totals[10], totals[11])
```

```python
import functools

import jax
import jax.numpy as jnp
from jax import lax
from jax.experimental import pallas as pl
from jax.experimental.pallas import tpu as pltpu
from jax.sharding import Mesh, PartitionSpec as P

H = 12
RD = 16
HALF = RD // 2
EPSILON = 1e-05
BASE_FREQ = 10000.0
NEGATIVE = -1e30
F32 = jnp.float32
BF16 = jnp.bfloat16
VMEM_BYTES = 60 * 2**20
CHIP = ("rows", "x", "core")
NT = (((1,), (1,)), ((), ()))


def dot(a, b):
    return jnp.dot(a, b, preferred_element_type=F32)


def dot_nt(a, b):
    return lax.dot_general(a, b, NT, preferred_element_type=F32)


def params():
    return pltpu.CompilerParams(vmem_limit_bytes=VMEM_BYTES)


def lasting(microseconds):
    return pl.CostEstimate(flops=int(microseconds * 1e9), bytes_accessed=0, transcendentals=0)


def whole(shape):
    return pl.BlockSpec(shape, lambda *_: (0,) * len(shape))


def shaped(shape, dtype):
    return jax.ShapeDtypeStruct(shape, dtype)


def after(kernel, inputs, deps):
    return lambda *refs: kernel(*refs[:inputs], *refs[inputs + deps :])


ANYWHERE = pl.BlockSpec(memory_space=pl.ANY)


def norm_stats(x):
    centered = x - jnp.mean(x, axis=-1, keepdims=True)
    spread = jnp.mean(centered * centered, axis=-1, keepdims=True)
    inverse = lax.rsqrt(spread + EPSILON)
    return centered * inverse, inverse


def gelu_both(h):
    e = jnp.exp2(h * h * (-0.5 * 1.4426950408889634))
    t = pl.reciprocal(1.0 + jnp.abs(h) * (0.3275911 * 0.7071067811865476), approx=False)
    poly = t * (
        0.5 * 0.254829592
        + t * (0.5 * -0.284496736 + t * (0.5 * 1.421413741 + t * (0.5 * -1.453152027 + t * (0.5 * 1.061405429))))
    )
    tail = poly * e
    phi = jnp.where(h >= 0.0, 1.0 - tail, tail)
    return h * phi, phi + h * e * 0.3989422804014327


def feed_kernel(
    base, x_own, x_sib, dy_own, dy_sib, gain, bias, we, wc, be,
    grads, act, hid, be_grad, out_bias, nf, nf_t, dy_t,
):
    step = pl.program_id(0)
    tokens = x_own.shape[0]
    width = we.shape[1]

    @pl.when(step == 0)
    def _():
        tile = 256
        for half, (x_ref, dy_ref) in enumerate(((x_own, dy_own), (x_sib, dy_sib))):
            def one(i, total):
                here = pl.ds(pl.multiple_of(i * tile, tile), tile)
                there = pl.ds(pl.multiple_of(half * tokens + i * tile, tile), tile)
                hat, _ = norm_stats(x_ref[here, :].astype(F32))
                normed = (hat * gain[...] + bias[...]).astype(BF16)
                nf[there, :] = normed
                nf_t[:, there] = normed.T
                dy = dy_ref[here, :]
                dy_t[:, there] = dy.T
                return total + jnp.sum(dy.astype(F32), axis=0, keepdims=True)

            total = lax.fori_loop(0, tokens // tile, one, jnp.zeros((1, x_own.shape[1]), F32))
            if half == 0:
                out_bias[...] = total

    tile = 512
    per = tokens // tile
    count = 2 * per
    hidden, back = [None] * count, [None] * count

    def finish(n):
        value, slope = gelu_both(hidden[n])
        rows = slice(n * tile, (n + 1) * tile)
        act[rows, :] = value.astype(BF16)
        hid[rows, :] = (back[n] * slope).astype(BF16)

    for n in range(count):
        dy_ref = dy_own if n < per else dy_sib
        hidden[n] = dot(nf[n * tile : (n + 1) * tile, :], we[...]) + be[...]
        back[n] = dot_nt(dy_ref[(n % per) * tile : (n % per + 1) * tile, :], wc[...])
        if n > 0:
            finish(n - 1)
    finish(count - 1)
    there = pl.ds(pl.multiple_of(step * width, width), width)
    grads[0, there, :] = dot(dy_t[...], act[...]).T.astype(BF16)
    grads[1, :, there] = dot(nf_t[...], hid[...]).astype(BF16)
    be_grad[...] = jnp.sum(hid[...].astype(F32), axis=0, keepdims=True)


def feed_part(base, x_own, x_sib, dy_own, dy_sib, gain, bias, we, wc, be, units, deps=()):
    tokens, features = x_own.shape
    width = 256
    steps = units // width
    return pl.pallas_call(
        after(feed_kernel, 10, len(deps)),
        out_shape=(
            shaped((2, units, features), BF16),
            shaped((2 * tokens, units), BF16),
            shaped((2 * tokens, units), BF16),
            shaped((1, units), F32),
            shaped((1, features), F32),
        ),
        grid_spec=pltpu.PrefetchScalarGridSpec(
            num_scalar_prefetch=1,
            grid=(steps,),
            in_specs=[whole((tokens, features))] * 4
            + [whole((1, features))] * 2
            + [
                pl.BlockSpec((features, width), lambda t, b: (0, b[0] + t)),
                pl.BlockSpec((width, features), lambda t, b: (b[0] + t, 0)),
                pl.BlockSpec((1, width), lambda t, b: (0, b[0] + t)),
            ]
            + [ANYWHERE] * len(deps),
            out_specs=(
                whole((2, units, features)),
                pl.BlockSpec((2 * tokens, width), lambda t, b: (0, t)),
                pl.BlockSpec((2 * tokens, width), lambda t, b: (0, t)),
                pl.BlockSpec((1, width), lambda t, b: (0, t)),
                whole((1, features)),
            ),
            scratch_shapes=[
                pltpu.VMEM((2 * tokens, features), BF16),
                pltpu.VMEM((features, 2 * tokens), BF16),
                pltpu.VMEM((features, 2 * tokens), BF16),
            ],
        ),
        cost_estimate=lasting(23),
        compiler_params=params(),
    )(base, x_own, x_sib, dy_own, dy_sib, gain, bias, we, wc, be, *deps)


def project_kernel(
    places, x_own, x_near, x_sib, x_far, dy_own, dy_near, dy_sib, dy_far, gain, bias, wq, wk, wv, jb, wd,
    cos, sin, normed_t, qkv, mix_t, w_t, x_here, dy_here,
):
    step = pl.program_id(0)
    part = wq.shape[1]
    heads, size = qkv.shape[1], qkv.shape[2]

    @pl.when(step == 0)
    def _():
        for n, w in enumerate((wq, wk, wv)):
            w_t[n * part : (n + 1) * part, :] = w[...].T

    sources = ((x_own, dy_own), (x_near, dy_near), (x_sib, dy_sib), (x_far, dy_far))
    for number, (x_ref, dy_ref) in enumerate(sources):

        @pl.when(step == number)
        def _():
            x_here[...] = x_ref[...].reshape(x_here.shape)
            dy_here[...] = dy_ref[...].reshape(dy_here.shape)

    hat, _ = norm_stats(x_here[...].astype(F32))
    turned = (hat * gain[...] + bias[...]).astype(BF16).T
    normed_t[...] = turned
    mix = dot_nt(wd[...], dy_here[...])
    c, s = cos[...], sin[...]
    for n in range(3):
        rows = slice(n * part, (n + 1) * part)
        joint = dot(w_t[rows, :], turned) + jb[rows, :]
        for h in range(heads):
            one = joint[h * size : (h + 1) * size]
            if n < 2:
                a, b = one[:HALF], one[HALF:RD]
                one = jnp.concatenate([a * c - b * s, b * c + a * s, one[RD:]], axis=0)
            if n == 0:
                one = one * size**-0.5
            qkv[n, h] = one.astype(BF16)
    for h in range(heads):
        mix_t[h] = mix[h * size : (h + 1) * size].astype(BF16)


def row_specs(tile, width, number, column=lambda *_: 0):
    flat = pl.BlockSpec((tile, width), lambda *g: (g[-1][3], column(*g)))
    stacked = pl.BlockSpec((1, tile, width), lambda *g: (number, 0, column(*g)))
    return [flat, stacked, flat, stacked]


def project(places, x_own, x_sib, dy_own, dy_sib, near, far, gain, bias, joint_w, jb, dense_w, cos, sin,
            heads, deps=()):
    tokens, features = x_own.shape
    tile = tokens // 2
    part = features // 2
    size = part // heads
    weight = lambda n: pl.BlockSpec((features, part), lambda g, p: (0, 2 * n + p[2]))
    lane = pl.BlockSpec((HALF, tile), lambda g, p: (0, g))
    return pl.pallas_call(
        after(project_kernel, 18, len(deps)),
        out_shape=(
            shaped((features, 2 * tokens), BF16),
            shaped((3, heads, size, 2 * tokens), BF16),
            shaped((heads, size, 2 * tokens), BF16),
        ),
        grid_spec=pltpu.PrefetchScalarGridSpec(
            num_scalar_prefetch=1,
            grid=(4,),
            in_specs=row_specs(tile, features, 0) + row_specs(tile, features, 1)
            + [whole((1, features)), whole((1, features)),
               weight(0), weight(1), weight(2), whole((3 * part, 1)),
               pl.BlockSpec((part, features), lambda g, p: (p[2], 0)), lane, lane]
            + [ANYWHERE] * len(deps),
            out_specs=(
                pl.BlockSpec((features, tile), lambda g, p: (0, g)),
                pl.BlockSpec((3, heads, size, tile), lambda g, p: (0, 0, 0, g)),
                pl.BlockSpec((heads, size, tile), lambda g, p: (0, 0, g)),
            ),
            scratch_shapes=[pltpu.VMEM((3 * part, features), BF16),
                            pltpu.VMEM((tile, features), BF16), pltpu.VMEM((tile, features), BF16)],
        ),
        cost_estimate=lasting(12),
        compiler_params=params(),
    )(places, x_own, near, x_sib, far, dy_own, near, dy_sib, far, gain, bias,
      joint_w, joint_w, joint_w, jb, dense_w, cos, sin, *deps)


def placing(bounds, segs, block, chunk, total):
    per_chunk = chunk // block
    tag = bounds[segs - 1]

    def place(b):
        k = (b // per_chunk) ^ tag
        slot = 2 * (k & 1) + (k >> 1)
        return pl.multiple_of(slot * chunk + (b % per_chunk) * block, block)

    def halved(offset):
        half = offset // (total // 2)
        return half, pl.ds(pl.multiple_of(offset - half * (total // 2), block), block)

    def first_of(position):
        start = jnp.int32(0)
        for m in range(segs - 1):
            start = jnp.where(bounds[m] <= position, bounds[m], start)
        return start

    def last_of(position):
        end = jnp.int32(total)
        for m in range(segs - 2, -1, -1):
            end = jnp.where(bounds[m] > position, bounds[m], end)
        return end - 1

    return place, halved, first_of, last_of


def sentence_rows(bounds, segs, pos):
    seg = jnp.zeros_like(pos)
    for m in range(segs - 1):
        seg = seg + (pos >= bounds[m]).astype(jnp.int32)
    rows = lax.broadcasted_iota(jnp.int32, (16, pos.shape[1]), 0)
    same = rows == seg
    onehot = jnp.where(same, 1.0, 0.0).astype(BF16)
    away = jnp.where(same | (rows >= segs), 0.0, NEGATIVE).astype(BF16)
    return onehot, away


def causal_bias(block):
    key = lax.broadcasted_iota(jnp.int32, (block, block), 0)
    query = lax.broadcasted_iota(jnp.int32, (block, block), 1)
    return jnp.where(key <= query, 0.0, NEGATIVE)


def forward_kernel(
    bounds, q, k, v, mix, pos, out_near, out_far, stats, qa, kn, acc, top, low,
    *, heads, block, chunk, segs,
):
    total = q.shape[-1]
    size = q.shape[2]
    place, halved, first_of, _ = placing(bounds, segs, block, chunk, total)
    hs = range(heads)
    onehot, away = sentence_rows(bounds, segs, pos[...])
    for h in hs:
        qa[h, :size, :] = q[0, h]
        qa[h, size:, :] = away
        kn[h] = jnp.concatenate([k[0, h], onehot], axis=0).T
    bias = causal_bias(block)

    def queries(i, _):
        half, lanes = halved(place(i))
        qs = pl.ds(place(i), block)
        s = [dot(kn[h, qs, :], qa[h, :, qs]) + bias for h in hs]
        m = [jnp.max(s[h], axis=0, keepdims=True) for h in hs]
        p = [jnp.exp(s[h] - m[h]) for h in hs]
        o = [dot(v[0, h, :, qs], p[h].astype(BF16)) for h in hs]
        l = [jnp.sum(p[h], axis=0, keepdims=True) for h in hs]
        for h in hs:
            top[h] = m[h]
            low[h] = l[h]
            acc[h] = o[h]

        def keys(j, _):
            ks = pl.ds(place(j), block)
            s = [dot(kn[h, ks, :], qa[h, :, qs]) for h in hs]
            m_old = [top[h] for h in hs]
            l_old = [low[h] for h in hs]
            m = [jnp.maximum(m_old[h], jnp.max(s[h], axis=0, keepdims=True)) for h in hs]
            p = [jnp.exp(s[h] - m[h]) for h in hs]
            f = [jnp.exp(m_old[h] - m[h]) for h in hs]
            o = [dot(v[0, h, :, ks], p[h].astype(BF16)) for h in hs]
            l = [l_old[h] * f[h] + jnp.sum(p[h], axis=0, keepdims=True) for h in hs]
            a = [acc[h] * f[h] + o[h] for h in hs]
            for h in hs:
                top[h] = m[h]
                low[h] = l[h]
                acc[h] = a[h]
            return 0

        lax.fori_loop(first_of(i * block) // block, i, keys, 0)
        result = [acc[h] / low[h] for h in hs]
        for number, out in enumerate((out_near, out_far)):

            @pl.when(half == number)
            def _():
                for h in hs:
                    out[h, :, lanes] = result[h].astype(BF16)

        for h in hs:
            o = result[h]
            stats[h, 0:1, qs] = top[h] + jnp.log(low[h])
            stats[h, 1:2, qs] = jnp.sum(o * mix[h, :, qs].astype(F32), axis=0, keepdims=True)
        return 0

    lax.fori_loop(0, total // block, queries, 0)


def attend(bounds, qkv, mix, pos, chunk, segs, deps=(), block=256):
    _, heads, size, total = qkv.shape
    part = lambda n: pl.BlockSpec((1, heads, size, total), lambda g, b: (n, 0, 0, 0))
    kernel = functools.partial(forward_kernel, heads=heads, block=block, chunk=chunk, segs=segs)
    return pl.pallas_call(
        after(kernel, 6, len(deps)),
        out_shape=(shaped((heads, size, total // 2), BF16),) * 2 + (shaped((heads, 2, total), F32),),
        grid_spec=pltpu.PrefetchScalarGridSpec(
            num_scalar_prefetch=1,
            grid=(1,),
            in_specs=[part(0), part(1), part(2), whole((heads, size, total)), whole((1, total))]
            + [ANYWHERE] * len(deps),
            out_specs=(whole((heads, size, total // 2)),) * 2 + (whole((heads, 2, total)),),
            scratch_shapes=[
                pltpu.VMEM((heads, size + 16, total), BF16),
                pltpu.VMEM((heads, total, size + 16), BF16),
                pltpu.VMEM((heads, size, block), F32),
                pltpu.VMEM((heads, 1, block), F32),
                pltpu.VMEM((heads, 1, block), F32),
            ],
        ),
        cost_estimate=lasting(30),
        compiler_params=params(),
    )(bounds, qkv, qkv, qkv, mix, pos, *deps)


def backward_kernel(
    bounds, q, k, v, mix, stats, pos, cos, sin, out_near, out_far, qa, kn, vn, qn, mn, dq, dk, dv,
    *, heads, block, chunk, segs,
):
    total = q.shape[-1]
    size = q.shape[2]
    place, halved, _, last_of = placing(bounds, segs, block, chunk, total)
    hs = range(heads)
    onehot, away = sentence_rows(bounds, segs, pos[...])
    for h in hs:
        qa[h, :size, :] = q[0, h]
        qa[h, size:, :] = away
        kn[h] = jnp.concatenate([k[0, h], onehot], axis=0).T
        vn[h] = v[0, h].T
        qn[h] = q[0, h].T
        mn[h] = mix[h].T
    bias = causal_bias(block)
    dq[...] = jnp.zeros_like(dq)

    def grads(qs, ks, add):
        s = [dot(kn[h, ks, :], qa[h, :, qs]) for h in hs]
        dp = [dot(vn[h, ks, :], mix[h, :, qs]) for h in hs]
        if add is not None:
            s = [x + add for x in s]
        p = [jnp.exp(s[h] - stats[h, 0:1, qs]) for h in hs]
        ds = [(p[h] * (dp[h] - stats[h, 1:2, qs])).astype(BF16) for h in hs]
        a = [dot(p[h].astype(BF16), mn[h, qs, :]) for h in hs]
        b = [dot(ds[h], qn[h, qs, :]) for h in hs]
        c = [dot(k[0, h, :, ks], ds[h]) for h in hs]
        return a, b, c

    def turned_back(g, c, s):
        a, b = g[:HALF], g[HALF:RD]
        return jnp.concatenate([a * c + b * s, b * c - a * s, g[RD:]], axis=0).astype(BF16)

    def keys(j, _):
        ks = pl.ds(place(j), block)
        a, b, c = grads(ks, ks, bias)
        for h in hs:
            dv[h] = a[h]
            dk[h] = b[h]
            dq[h, :, ks] += c[h]

        def queries(i, _):
            qs = pl.ds(place(i), block)
            a, b, c = grads(qs, ks, None)
            a = [dv[h] + a[h] for h in hs]
            b = [dk[h] + b[h] for h in hs]
            c = [dq[h, :, qs] + c[h] for h in hs]
            for h in hs:
                dv[h] = a[h]
                dk[h] = b[h]
                dq[h, :, qs] = c[h]
            return 0

        lax.fori_loop(j + 1, last_of((j + 1) * block - 1) // block + 1, queries, 0)
        half, lanes = halved(place(j))
        c, s = cos[:, ks], sin[:, ks]
        g = [(turned_back(dk[h].T, c, s), dv[h].T.astype(BF16)) for h in hs]
        for number, out in enumerate((out_near, out_far)):

            @pl.when(half == number)
            def _():
                for h in hs:
                    out[1, h, :, lanes] = g[h][0]
                    out[2, h, :, lanes] = g[h][1]

        return 0

    lax.fori_loop(0, total // block, keys, 0)
    c, s = cos[...], sin[...]
    for h in hs:
        g = turned_back(dq[h] * size**-0.5, c, s)
        out_near[0, h] = g[:, : total // 2]
        out_far[0, h] = g[:, total // 2 :]


def attend_back(bounds, qkv, mix, stats, pos, cos, sin, chunk, segs, deps=(), block=256):
    _, heads, size, total = qkv.shape
    part = lambda n: pl.BlockSpec((1, heads, size, total), lambda g, b: (n, 0, 0, 0))
    kernel = functools.partial(backward_kernel, heads=heads, block=block, chunk=chunk, segs=segs)
    return pl.pallas_call(
        after(kernel, 9, len(deps)),
        out_shape=(shaped((3, heads, size, total // 2), BF16),) * 2,
        grid_spec=pltpu.PrefetchScalarGridSpec(
            num_scalar_prefetch=1,
            grid=(1,),
            in_specs=[part(0), part(1), part(2), whole((heads, size, total)),
                      whole((heads, 2, total)), whole((1, total)), whole((HALF, total)), whole((HALF, total))]
            + [ANYWHERE] * len(deps),
            out_specs=(whole((3, heads, size, total // 2)),) * 2,
            scratch_shapes=[
                pltpu.VMEM((heads, size + 16, total), BF16),
                pltpu.VMEM((heads, total, size + 16), BF16),
                pltpu.VMEM((heads, total, size), BF16),
                pltpu.VMEM((heads, total, size), BF16),
                pltpu.VMEM((heads, total, size), BF16),
                pltpu.VMEM((heads, size, total), F32),
                pltpu.VMEM((heads, block, size), F32),
                pltpu.VMEM((heads, block, size), F32),
            ],
        ),
        cost_estimate=lasting(45),
        compiler_params=params(),
    )(bounds, qkv, qkv, qkv, mix, stats, pos, cos, sin, *deps)


def joint_grads_kernel(places, normed_t, near, far, mixed, mixed_far, dy_own, dy_near, dy_sib, dy_far, out, bias):
    step = pl.program_id(0)
    tokens = near.shape[2]
    tile = tokens // 2

    @pl.when(step < 3)
    def _():
        a, b = near[0], far[0]
        out[...] = (dot_nt(normed_t[:, :tokens], a) + dot_nt(normed_t[:, tokens:], b)).astype(BF16)
        ones = jnp.ones((8, tokens), BF16)
        bias[0] = dot_nt(ones, a) + dot_nt(ones, b)

    @pl.when(step == 3)
    def _():
        out[...] = (
            dot(mixed[:, :tile], dy_own[...]) + dot(mixed[:, tile:], dy_near[0])
            + dot(mixed_far[:, :tile], dy_sib[...]) + dot(mixed_far[:, tile:], dy_far[0])
        ).astype(BF16)


def joint_grads(places, which, normed_t, grads, mixed, dy_own, dy_sib, near, far, deps=()):
    features, total = normed_t.shape
    part = features // 2
    tokens = total // 2
    clamp = lambda n: jnp.minimum(n, 2)
    piece = pl.BlockSpec((1, part, tokens), lambda n, p: (clamp(n), 0, 0))
    half = lambda p: p[4 + which]
    return pl.pallas_call(
        after(joint_grads_kernel, 10, len(deps)),
        out_shape=(shaped((part, 4 * part), BF16), shaped((3, 8, part), F32)),
        grid_spec=pltpu.PrefetchScalarGridSpec(
            num_scalar_prefetch=1,
            grid=(4,),
            in_specs=[pl.BlockSpec((part, total), lambda n, p: (half(p), 0)), piece, piece,
                      whole((part, tokens)), whole((part, tokens))]
            + row_specs(tokens // 2, part, 1, lambda n, p: half(p))
            + [ANYWHERE] * len(deps),
            out_specs=(pl.BlockSpec((part, part), lambda n, p: (0, n)),
                       pl.BlockSpec((1, 8, part), lambda n, p: (clamp(n), 0, 0))),
        ),
        cost_estimate=lasting(9),
        compiler_params=params(),
    )(places, normed_t, grads[0], grads[1], mixed[0], mixed[1], dy_own, near, dy_sib, far, *deps)


def norm_back_of(grad, x, gain):
    hat, inverse = norm_stats(x)
    scaled = grad * gain
    dx = inverse * (
        scaled
        - jnp.mean(scaled, axis=-1, keepdims=True)
        - hat * jnp.mean(scaled * hat, axis=-1, keepdims=True)
    )
    return dx, jnp.sum(grad * hat, axis=0, keepdims=True), jnp.sum(grad, axis=0, keepdims=True)


def norm_back_kernel(places, own, sib, w, x, x_near, gain, dx_own, dx_far, gain_grad, bias_grad, x_here):
    step = pl.program_id(0)
    part = own.shape[1]
    core = places[2]

    @pl.when(step == 0)
    def _():
        x_here[...] = x_near[0]

    @pl.when(step == 1)
    def _():
        x_here[...] = x[...]

    total = None
    for n in range(3):
        mine = pl.ds(pl.multiple_of((2 * n + core) * part, 128), part)
        other = pl.ds(pl.multiple_of((2 * n + 1 - core) * part, 128), part)
        one = dot(w[:, mine], own[n]) + dot(w[:, other], sib[n])
        total = one if n == 0 else total + one
    dx, g, b = norm_back_of(total.T, x_here[...].astype(F32), gain[...])

    @pl.when(step == 0)
    def _():
        dx_far[...] = dx.astype(BF16)
        gain_grad[...] = g
        bias_grad[...] = b

    @pl.when(step == 1)
    def _():
        dx_own[...] = dx
        gain_grad[...] += g
        bias_grad[...] += b


def norm_back(places, own, sib, w, x, near, gain, deps=()):
    part = own.shape[1]
    tokens, features = x.shape
    tile = tokens // 2
    piece = pl.BlockSpec((3, part, tile), lambda g, p: (0, 0, 1 - g))
    return pl.pallas_call(
        after(norm_back_kernel, 7, len(deps)),
        out_shape=(shaped((tile, features), F32), shaped((tile, features), BF16),
                   shaped((1, features), F32), shaped((1, features), F32)),
        grid_spec=pltpu.PrefetchScalarGridSpec(
            num_scalar_prefetch=1,
            grid=(2,),
            in_specs=[piece, piece, whole(w.shape)] + row_specs(tile, features, 0)[:2]
            + [whole((1, features))] + [ANYWHERE] * len(deps),
            out_specs=(whole((tile, features)), whole((tile, features)),
                       whole((1, features)), whole((1, features))),
            scratch_shapes=[pltpu.VMEM((tile, features), BF16)],
        ),
        cost_estimate=lasting(12),
        compiler_params=params(),
    )(places, own, sib, w, x, near, gain, *deps)


def partial_kernel(places, act_a, act_b, hid_a, hid_b, wc_a, wc_b, we_a, we_b, out, back):
    out[...] = (dot(act_a[...], wc_a[...]) + dot(act_b[...], wc_b[...])).astype(BF16)
    back[...] = (dot_nt(hid_a[...], we_a[...]) + dot_nt(hid_b[...], we_b[...])).astype(BF16)


def feed_specs(tile, units, features, first):
    token = pl.BlockSpec((tile, units), first)
    row = lambda n: pl.BlockSpec((units, features), lambda g, p: (p[n], 0))
    column = lambda n: pl.BlockSpec((features, units), lambda g, p: (0, p[n]))
    return [token] * 4 + [row(0), row(1), column(0), column(1)]


def sibling_part(places, sent, kept, wc, we, deps=()):
    tokens, units = sent[1].shape[0] // 2, sent[1].shape[1]
    features = wc.shape[1]
    tile = tokens // 2
    spec = pl.BlockSpec((tile, features), lambda g, p: (g, 0))
    return pl.pallas_call(
        after(partial_kernel, 9, len(deps)),
        out_shape=(shaped((tokens, features), BF16),) * 2,
        grid_spec=pltpu.PrefetchScalarGridSpec(
            num_scalar_prefetch=1,
            grid=(2,),
            in_specs=feed_specs(tile, units, features, lambda g, p: (2 + g, 0)) + [ANYWHERE] * len(deps),
            out_specs=(spec, spec),
        ),
        cost_estimate=lasting(10),
        compiler_params=params(),
    )(places, sent[1], kept[1], sent[2], kept[2], wc, wc, we, we, *deps)


def results_kernel(
    places, act_a, act_b, hid_a, hid_b, wc_a, wc_b, we_a, we_b, out_sib, back_sib, x, dy,
    mixed, mixed_sib, mixed_near, wd, dx_own, dx_near, add_bias, gain,
    block_out, input_grad, gain_grad, bias_grad, acc,
):
    step = pl.program_id(0)
    part = mixed.shape[0]
    tile = x.shape[0]
    core = places[2]
    mine = pl.ds(pl.multiple_of(core * part, 128), part)
    other = pl.ds(pl.multiple_of((1 - core) * part, 128), part)

    @pl.when(step == 0)
    def _():
        acc[...] = dot(mixed[:, :tile].T, wd[mine, :]) + dot(mixed_sib[:, :tile].T, wd[other, :])

    @pl.when(step == 1)
    def _():
        acc[...] = dot(mixed_near[:part, :].T, wd[mine, :]) + dot(mixed_near[part:, :].T, wd[other, :])

    x_float = x[...].astype(F32)
    out = dot(act_a[...], wc_a[...]) + dot(act_b[...], wc_b[...])
    back = dot_nt(hid_a[...], we_a[...]) + dot_nt(hid_b[...], we_b[...]) + back_sib[...].astype(F32)
    block_out[...] = (x_float + acc[...] + out + out_sib[...].astype(F32) + add_bias[...]).astype(BF16)
    dx, g, b = norm_back_of(back, x_float, gain[...])
    total = dy[...].astype(F32) + dx

    @pl.when(step == 0)
    def _():
        input_grad[...] = (total + dx_own[...]).astype(BF16)
        gain_grad[...] = g
        bias_grad[...] = b

    @pl.when(step == 1)
    def _():
        input_grad[...] = (total + dx_near[...].astype(F32)).astype(BF16)
        gain_grad[...] += g
        bias_grad[...] += b


def results(places, sent, kept, wc, we, out_sib, back_sib, x, dy, mixed, mixed_sib, mixed_near,
            wd, dx_own, dx_near, add_bias, gain, deps=()):
    tokens, features = x.shape
    units = sent[1].shape[1]
    tile = tokens // 2
    part = features // 2
    token = pl.BlockSpec((tile, features), lambda g, p: (p[3] ^ g, 0))
    return pl.pallas_call(
        after(results_kernel, 21, len(deps)),
        out_shape=(shaped((tokens, features), BF16),) * 2 + (shaped((1, features), F32),) * 2,
        grid_spec=pltpu.PrefetchScalarGridSpec(
            num_scalar_prefetch=1,
            grid=(2,),
            in_specs=feed_specs(tile, units, features, lambda g, p: (p[3] ^ g, 0))
            + [token] * 4
            + [whole((part, tokens)), whole((part, tokens)),
               whole((features, tile)), whole((features, features)), whole((tile, features)),
               whole((tile, features)), whole((1, features)), whole((1, features))]
            + [ANYWHERE] * len(deps),
            out_specs=(token, token, whole((1, features)), whole((1, features))),
            scratch_shapes=[pltpu.VMEM((tile, features), F32)],
        ),
        cost_estimate=lasting(17),
        compiler_params=params(),
    )(places, sent[1], kept[1], sent[2], kept[2], wc, wc, we, we, out_sib, back_sib, x, dy,
      mixed, mixed_sib, mixed_near, wd, dx_own, dx_near, add_bias, gain, *deps)


class Links:
    def __init__(self, row_count):
        self.row_count = row_count
        self.row_bits = row_count.bit_length() - 1
        dims = ["x", *range(self.row_bits)]
        other = list(dims)
        for n in range(0, len(dims) - 1, 2):
            other[n], other[n + 1] = other[n + 1], other[n]
        self.orders = (dims, other)
        self.rounds = len(dims)

    def bit(self, number, sibling=False):
        def of(dim):
            if dim == "x":
                return lax.axis_index("x")
            return (lax.axis_index("rows") >> dim) & 1

        return jnp.where(
            lax.axis_index("core") == int(sibling), of(self.orders[0][number]), of(self.orders[1][number])
        )

    def swap(self, array, number):
        pairs = []
        for row in range(self.row_count):
            for x in range(2):
                for core in range(2):
                    dim = self.orders[core][number]
                    there = (row, 1 - x) if dim == "x" else (row ^ (1 << dim), x)
                    pairs.append(((row * 2 + x) * 2 + core, (there[0] * 2 + there[1]) * 2 + core))
        return lax.ppermute(array, CHIP, pairs)


def swap_core(array):
    return lax.ppermute(array, "core", [(0, 1), (1, 0)])


def swap_x(array):
    return lax.ppermute(array, "x", [(0, 1), (1, 0)])


def add(a, b):
    return (a.astype(F32) + b.astype(F32)).astype(BF16)


def halve_kernel(bit, a_go, b_go, a_stay, b_stay, go, stay):
    go[...] = add(a_go[...], b_go[...])
    stay[...] = add(a_stay[...], b_stay[...])


def halve(bit, a, b, deps=()):
    rows, width = a.shape
    rows = rows // 2
    if rows % 16:
        pick = lambda array, n: lax.dynamic_slice_in_dim(array, n * rows, rows, 0)
        return add(pick(a, 1 - bit), pick(b, 1 - bit)), add(pick(a, bit), pick(b, bit))
    tile = min(rows, 384)
    steps = rows // tile
    going = pl.BlockSpec((tile, width), lambda t, b: ((1 - b[0]) * steps + t, 0))
    staying = pl.BlockSpec((tile, width), lambda t, b: (b[0] * steps + t, 0))
    spec = pl.BlockSpec((tile, width), lambda t, b: (t, 0))
    return pl.pallas_call(
        after(halve_kernel, 5, len(deps)),
        out_shape=(shaped((rows, width), BF16),) * 2,
        grid_spec=pltpu.PrefetchScalarGridSpec(
            num_scalar_prefetch=1,
            grid=(steps,),
            in_specs=[going, going, staying, staying] + [ANYWHERE] * len(deps),
            out_specs=(spec, spec),
        ),
        cost_estimate=lasting(1),
        compiler_params=params(),
    )(bit.reshape(1), a, b, a, b, *deps)


def two_parts(vector):
    high = lax.reduce_precision(vector, 8, 7)
    low = lax.reduce_precision(vector - high, 8, 7)
    return jnp.concatenate([high, low], axis=0).astype(BF16), high + low


def one_part(pair):
    rows = pair.shape[0] // 2
    return pair[:rows].astype(F32) + pair[rows:].astype(F32)


def spread_kernel(first, second, contract, expand):
    contract[...] = first[...].astype(F32)
    expand[...] = second[...].astype(F32)


def spread(gathered, links, features, units, deps=()):
    piece = features >> (links.rounds - 2)
    parts = features // piece

    def rank(core, half, which, quarter):
        def one(order):
            place = 0
            bits = {order[0]: half, order[1]: which}
            for n, dim in enumerate(order[2:]):
                bits[dim] = (quarter >> (links.rounds - 3 - n)) & 1
            for dim, value in bits.items():
                place = place + (value * 2 if dim == "x" else value * (4 << dim))
            return place

        return jnp.where(core == 0, one(links.orders[0]), one(links.orders[1])) + core

    source = lambda which: pl.BlockSpec((piece, features), lambda c, h, q: (rank(c, h, which, q), 0))
    return pl.pallas_call(
        after(spread_kernel, 2, len(deps)),
        out_shape=(shaped((4 * units, features), F32), shaped((features, 4 * units), F32)),
        grid=(2, 2, parts),
        in_specs=[source(0), source(1)] + [ANYWHERE] * len(deps),
        out_specs=(
            pl.BlockSpec((piece, features), lambda c, h, q: ((c * 2 + h) * parts + q, 0)),
            pl.BlockSpec((piece, features), lambda c, h, q: (q, c * 2 + h)),
        ),
        cost_estimate=lasting(14),
        compiler_params=params(),
    )(gathered, gathered, *deps)


def spread_joint_kernel(places, own, own_far, sib, sib_far, joint, dense):
    step = pl.program_id(0)
    half = step // 2
    part = dense.shape[2]
    for ref, core, wanted in (
        (own, places[0], places[1]), (own_far, places[0], 1 - places[1]),
        (sib, 1 - places[0], places[2]), (sib_far, 1 - places[0], 1 - places[2]),
    ):
        @pl.when(half == wanted)
        def _():
            for n in range(3):
                there = pl.ds(pl.multiple_of((2 * n + core) * part, 128), part)
                joint[:, there] = ref[:, n * part : (n + 1) * part].astype(F32)
            dense[core] = ref[:, 3 * part :].astype(F32)


def spread_joint(places, own, own_far, sib, sib_far, features):
    part = features // 2
    tile = part // 2
    source = pl.BlockSpec((tile, 4 * part), lambda q, p: (q % 2, 0))
    return pl.pallas_call(
        spread_joint_kernel,
        out_shape=(shaped((features, 3 * features), F32), shaped((2, part, features), F32)),
        grid_spec=pltpu.PrefetchScalarGridSpec(
            num_scalar_prefetch=1,
            grid=(4,),
            in_specs=[source] * 4,
            out_specs=(pl.BlockSpec((tile, 3 * features), lambda q, p: (q, 0)),
                       pl.BlockSpec((2, tile, part), lambda q, p: (0, q % 2, q // 2))),
        ),
        cost_estimate=lasting(8),
        compiler_params=params(),
    )(places, own, own_far, sib, sib_far)


def per_device(
    links, block_in, lengths, attn_gain, attn_bias, feed_gain, feed_bias, joint_weight, joint_bias,
    dense_weight, dense_bias, expand_weight, expand_bias, contract_weight, contract_bias, out_cotangent,
):
    rows_here, chunk, features = block_in.shape
    tokens = rows_here * chunk
    total = 2 * tokens
    segs = lengths.shape[1]
    heads = H // 2
    part = features // 2
    units = expand_weight.shape[1] // 4
    x_at, core_at = lax.axis_index("x"), lax.axis_index("core")
    chunk_at = x_at * 2 + core_at
    row = lambda vector: vector.reshape(1, -1)

    x_own, dy_own = block_in.reshape(tokens, features), out_cotangent.reshape(tokens, features)
    x_sib, dy_sib = swap_core(x_own), swap_core(dy_own)
    away = jnp.stack([
        lax.dynamic_index_in_dim(block_in, 1 - x_at, 0, keepdims=False),
        lax.dynamic_index_in_dim(out_cotangent, 1 - x_at, 0, keepdims=False),
    ])
    near = swap_x(away)
    far = swap_core(near)

    mine = lax.dynamic_index_in_dim(lengths, x_at, 0, keepdims=False)
    before = jnp.tril(jnp.ones((segs, segs), jnp.int32))
    bounds = jnp.sum(before * mine[None, :], axis=1)
    bounds = jnp.where(jnp.arange(segs) == segs - 1, chunk_at, bounds).astype(jnp.int32)
    slots = jnp.arange(4, dtype=jnp.int32)
    starts = (((slots & 1) * 2 + (slots >> 1)) ^ chunk_at) * chunk
    pos = (starts[:, None] + jnp.arange(chunk, dtype=jnp.int32)[None, :]).reshape(1, total)
    inverse = BASE_FREQ ** (-2.0 * jnp.arange(HALF).astype(F32) / RD)
    angles = inverse[:, None] * pos.astype(F32)
    cos, sin = jnp.cos(angles), jnp.sin(angles)

    bits = [links.bit(n) for n in range(links.rounds)]

    def feed(half, deps=()):
        base = ((core_at * 2 + half) * (units // 256)).astype(jnp.int32).reshape(1)
        return feed_part(
            base, x_own, x_sib, dy_own, dy_sib, row(feed_gain), row(feed_bias),
            expand_weight, contract_weight, row(expand_bias), units, deps,
        )

    places = jnp.stack(
        [core_at * 2 + 1 - bits[0], core_at * 2 + bits[0], core_at, x_at, 1 - bits[0], bits[0]]
    ).astype(jnp.int32)
    sent = feed(1 - bits[0], (away,))
    arriving = links.swap(sent[0], 0)
    kept = feed(bits[0], (sent[0],))

    flat = lambda a: a.reshape(2 * units, features)
    bias_here = lax.dynamic_index_in_dim(joint_bias.reshape(3, 2, part), core_at, 1, keepdims=False)
    outgoing, stay = halve(bits[1], flat(kept[0]), flat(arriving))
    arriving = links.swap(outgoing, 1)
    normed_t, qkv, mix_t = project(
        places, x_own, x_sib, dy_own, dy_sib, near, far, row(attn_gain), row(attn_bias), joint_weight,
        bias_here.reshape(3 * part, 1), dense_weight, cos, sin, heads, (outgoing,),
    )
    outgoing, stay = halve(bits[2], stay, arriving, (normed_t,))
    arriving = links.swap(outgoing, 2)
    mixed_own, mixed_far, stats = attend(bounds, qkv, mix_t, pos, chunk, segs, (outgoing,))
    mixed_own, mixed_far = mixed_own.reshape(part, tokens), mixed_far.reshape(part, tokens)
    mixed_sib = swap_core(mixed_far)
    ready = stats
    for number in range(3, links.rounds):
        outgoing, stay = halve(bits[number], stay, arriving, (ready,))
        arriving = links.swap(outgoing, number)
        ready = outgoing
    out_sib, back_sib = sibling_part(places, sent, kept, contract_weight, expand_weight, (ready, mixed_own))
    stay, arriving, out_sib = lax.optimization_barrier((stay, arriving, out_sib))
    last = add(stay, arriving)
    gathered = lax.all_gather(last, CHIP, axis=0, tiled=True)
    away = jnp.concatenate([mixed_own[:, chunk:], mixed_sib[:, chunk:]], axis=0)
    mixed_near = swap_x(away)
    grads = attend_back(bounds, qkv, mix_t, stats, pos, cos, sin, chunk, segs, (last, away))
    grads = [g.reshape(3, part, tokens) for g in grads]
    out_sib, back_sib = swap_core(out_sib), swap_core(back_sib)

    grads_sib = swap_core(grads[1])
    mixed = (mixed_own, mixed_far)
    outgoing, joint_b = joint_grads(places, 0, normed_t, grads, mixed, dy_own, dy_sib, near, far)
    arriving = links.swap(outgoing, 0)
    current, _ = joint_grads(places, 1, normed_t, grads, mixed, dy_own, dy_sib, near, far, (outgoing,))
    dx_own, dx_far, gain_attn, bias_attn = norm_back(
        places, grads[0], grads_sib, joint_weight, x_own, near, row(attn_gain), (current,)
    )
    dx_near = swap_x(dx_far)
    ready = dx_own
    for number in range(1, links.rounds):
        outgoing, current = halve(bits[number], current, arriving, (ready,))
        arriving = links.swap(outgoing, number)
        if number == 1:
            grad_contract_w, grad_expand_w = spread(gathered, links, features, units, (outgoing,))
            ready = grad_contract_w
        elif number == 2:
            results_after = outgoing
    block_out, input_grad, gain_feed, bias_feed = results(
        places, sent, kept, contract_weight, expand_weight, out_sib, back_sib, x_own, dy_own,
        mixed_own, mixed_sib, mixed_near, dense_weight, dx_own, dx_near, row(dense_bias + contract_bias),
        row(feed_gain), (results_after,),
    )
    current = add(current, arriving)

    expand_b = jnp.where(
        bits[0] == 0,
        jnp.concatenate([kept[3], sent[3]], axis=1),
        jnp.concatenate([sent[3], kept[3]], axis=1),
    )
    width = current.shape[1]
    small = jnp.concatenate([
        vector.reshape(-1)
        for vector in (gain_attn, bias_attn, gain_feed, bias_feed, sent[4], joint_b[:, 0], expand_b)
    ])
    shared = 5 * features
    small = jnp.pad(small, (0, 8 * width - small.shape[0])).reshape(8, width)
    for number in reversed(range(links.rounds)):
        pair, small = two_parts(small)
        outgoing = jnp.concatenate([current, pair], axis=0)
        arrived = links.swap(outgoing, number)
        rows_now = current.shape[0]
        small = small + one_part(arrived[rows_now:])
        if number > 0:
            current = jnp.where(
                bits[number] == 0,
                jnp.concatenate([current, arrived[:rows_now]], axis=0),
                jnp.concatenate([arrived[:rows_now], current], axis=0),
            )
    from_sib, far_sib = swap_core(outgoing), swap_core(arrived)
    small_sib = (one_part(from_sib[part:]) + one_part(far_sib[part:])).reshape(-1)
    small = small.reshape(-1)
    sums = (small + small_sib)[:shared].reshape(5, features)
    ordered = lambda a, b: jnp.where(core_at == 0, jnp.stack([a, b]), jnp.stack([b, a]))
    single = ordered(small[shared:], small_sib[shared:])
    grad_joint_b = single[:, : 3 * part].reshape(2, 3, part).transpose(1, 0, 2).reshape(-1)
    grad_expand_b = single[:, 3 * part : 3 * part + 2 * units].reshape(-1)
    kinds = jnp.stack([core_at, bits[0], links.bit(0, True)]).astype(jnp.int32)
    grad_joint_w, grad_dense_w = spread_joint(kinds, outgoing, arrived, from_sib, far_sib, features)
    return (
        block_out.reshape(block_in.shape),
        input_grad.reshape(block_in.shape),
        sums[0],
        sums[1],
        sums[2],
        sums[3],
        grad_joint_w,
        grad_joint_b,
        grad_dense_w.reshape(features, features),
        sums[4],
        grad_expand_w,
        grad_expand_b,
        grad_contract_w,
        sums[4],
    )


def solution(mesh):
    row_count, seq_count = mesh.devices.shape
    chips = Mesh(mesh.devices.reshape(row_count, seq_count // 2, 2), CHIP)
    links = Links(row_count)
    tokens = P("rows", ("x", "core"), None)
    in_specs = (tokens, P("rows", None)) + (P(),) * 12 + (tokens,)
    out_specs = (tokens, tokens) + (P(),) * 12
    return jax.shard_map(
        functools.partial(per_device, links), mesh=chips, in_specs=in_specs, out_specs=out_specs,
        check_vma=False,
    )
```

```python
import functools

import jax
import jax.numpy as jnp
from jax import lax
from jax.experimental import pallas as pl
from jax.experimental.pallas import tpu as pltpu
from jax.sharding import Mesh, PartitionSpec as P

H = 12
RD = 16
HALF = RD // 2
EPSILON = 1e-05
BASE_FREQ = 10000.0
NEGATIVE = -1e30
F32 = jnp.float32
BF16 = jnp.bfloat16
VMEM_BYTES = 63 * 2**20
CHIP = ("rows", "x", "core")
NT = (((1,), (1,)), ((), ()))


def dot(a, b):
    return jnp.dot(a, b, preferred_element_type=F32)


def dot_nt(a, b):
    return lax.dot_general(a, b, NT, preferred_element_type=F32)


def params():
    return pltpu.CompilerParams(vmem_limit_bytes=VMEM_BYTES)


def lasting(microseconds):
    return pl.CostEstimate(flops=int(microseconds * 1e9), bytes_accessed=0, transcendentals=0)


def whole(shape):
    return pl.BlockSpec(shape, lambda *_: (0,) * len(shape))


def shaped(shape, dtype):
    return jax.ShapeDtypeStruct(shape, dtype)


def after(kernel, inputs, deps):
    return lambda *refs: kernel(*refs[:inputs], *refs[inputs + deps :])


ANYWHERE = pl.BlockSpec(memory_space=pl.ANY)


def once(array, deps):
    return pl.pallas_call(
        lambda *refs: None,
        out_shape=shaped(array.shape, array.dtype),
        in_specs=[ANYWHERE] * (1 + len(deps)),
        out_specs=ANYWHERE,
        input_output_aliases={0: 0},
        cost_estimate=lasting(0.1),
    )(array, *deps)


def norm_stats(x):
    centered = x - jnp.mean(x, axis=-1, keepdims=True)
    spread = jnp.mean(centered * centered, axis=-1, keepdims=True)
    inverse = lax.rsqrt(spread + EPSILON)
    return centered * inverse, inverse


def gelu_both(h):
    e = jnp.exp2(h * h * (-0.5 * 1.4426950408889634))
    t = pl.reciprocal(1.0 + jnp.abs(h) * (0.3275911 * 0.7071067811865476), approx=False)
    poly = t * (
        0.5 * 0.254829592
        + t * (0.5 * -0.284496736 + t * (0.5 * 1.421413741 + t * (0.5 * -1.453152027 + t * (0.5 * 1.061405429))))
    )
    tail = poly * e
    phi = jnp.where(h >= 0.0, 1.0 - tail, tail)
    return h * phi, phi + h * e * 0.3989422804014327


def feed_kernel(
    base, x_own, x_sib, dy_own, dy_sib, pack, we, wc,
    grads, act, hid, be_grad, out_bias, normed, nf, act_t, hid_t, gone,
):
    tokens = x_own.shape[0]
    features = x_own.shape[1]
    copy = pltpu.make_async_copy(nf, normed, gone)

    @pl.when(pl.program_id(0) == 0)
    def _():
        tile = 256
        for half, (x_ref, dy_ref) in enumerate(((x_own, dy_own), (x_sib, dy_sib))):
            def one(i, total):
                here = pl.ds(pl.multiple_of(i * tile, tile), tile)
                there = pl.ds(pl.multiple_of(half * tokens + i * tile, tile), tile)
                hat, _ = norm_stats(x_ref[here, :].astype(F32))
                nf[there, :] = (hat * pack[2:3, :] + pack[3:4, :]).astype(BF16)
                if half == 0:
                    total = total + jnp.sum(dy_ref[here, :].astype(F32), axis=0, keepdims=True)
                return total

            total = lax.fori_loop(0, tokens // tile, one, jnp.zeros((1, features), F32))
            if half == 0:
                out_bias[...] = total
        copy.start()

    feed_tile(base, nf, dy_own, dy_sib, pack, we, wc, grads, act, hid, be_grad, act_t, hid_t)

    @pl.when(pl.program_id(0) == pl.num_programs(0) - 1)
    def _():
        copy.wait()


def feed_tile(base, nf, dy_own, dy_sib, pack, we, wc, grads, act, hid, be_grad, act_t, hid_t):
    step = pl.program_id(0)
    tokens, features = dy_own.shape
    width = we.shape[1]
    first = (base[0] + step) * width
    be = pack[
        pl.ds(5 + first // features, 1), pl.ds(pl.multiple_of(first % features, width), width)
    ]
    tile = 512
    per = tokens // tile
    count = 2 * per
    hidden, back = [None] * count, [None] * count

    def finish(n):
        value, slope = gelu_both(hidden[n])
        rows = slice(n * tile, (n + 1) * tile)
        value, slope = value.astype(BF16), (back[n] * slope).astype(BF16)
        act[rows, :] = value
        hid[rows, :] = slope
        act_t[:, rows] = value.T
        hid_t[:, rows] = slope.T

    for n in range(count):
        dy_ref = dy_own if n < per else dy_sib
        hidden[n] = dot(nf[n * tile : (n + 1) * tile, :], we[...]) + be
        back[n] = dot_nt(dy_ref[(n % per) * tile : (n % per + 1) * tile, :], wc[...])
        if n > 0:
            finish(n - 1)
    finish(count - 1)
    there = pl.ds(pl.multiple_of(step * width, width), width)
    grads[0, there, :] = (
        dot(act_t[:, :tokens], dy_own[...]) + dot(act_t[:, tokens:], dy_sib[...])
    ).astype(BF16)
    grads[1, :, there] = dot(hid_t[...], nf[...]).T.astype(BF16)
    be_grad[...] = jnp.sum(hid[...].astype(F32), axis=0, keepdims=True)


def feed_part(base, x, dy_own, dy_sib, pack, we, wc, units, deps=()):
    tokens, features = dy_own.shape
    width = 256
    prepared = len(x) == 1
    token = pl.BlockSpec((2 * tokens, width), lambda t, b: (0, t))
    out_shape = (
        shaped((2, units, features), BF16), shaped((2 * tokens, units), BF16),
        shaped((2 * tokens, units), BF16), shaped((1, units), F32),
    )
    out_specs = (whole((2, units, features)), token, token, pl.BlockSpec((1, width), lambda t, b: (0, t)))
    scratch = [pltpu.VMEM((width, 2 * tokens), BF16), pltpu.VMEM((width, 2 * tokens), BF16)]
    if not prepared:
        out_shape += (shaped((1, features), F32), shaped((2 * tokens, features), BF16))
        out_specs += (whole((1, features)), ANYWHERE)
        scratch = [pltpu.VMEM((2 * tokens, features), BF16), *scratch, pltpu.SemaphoreType.DMA]
    return pl.pallas_call(
        after(feed_tile if prepared else feed_kernel, 6 + len(x), len(deps)),
        out_shape=out_shape,
        grid_spec=pltpu.PrefetchScalarGridSpec(
            num_scalar_prefetch=1,
            grid=(units // width,),
            in_specs=[whole(a.shape) for a in x] + [whole((tokens, features))] * 2
            + [
                whole(pack.shape),
                pl.BlockSpec((features, width), lambda t, b: (0, b[0] + t)),
                pl.BlockSpec((width, features), lambda t, b: (b[0] + t, 0)),
            ]
            + [ANYWHERE] * len(deps),
            out_specs=out_specs,
            scratch_shapes=scratch,
        ),
        cost_estimate=lasting(22),
        compiler_params=params(),
    )(base, *x, dy_own, dy_sib, pack, we, wc, *deps)


def row_pieces(places, own, sib, near, far, number, tile, columns=None):
    rows = pl.ds(pl.multiple_of(places[3] * tile, tile), tile)
    if columns is None:
        return own.at[rows], near.at[number], sib.at[rows], far.at[number]
    return own.at[rows, columns], near.at[number, :, columns], sib.at[rows, columns], far.at[number, :, columns]


def project_kernel(
    places, x_own, x_sib, dy_own, dy_sib, near, far, pack, wq, wk, wv, wd,
    cos, sin, normed_t, qkv, mix_t, w_t, jb, x_here, dy_here, arrived,
):
    step = pl.program_id(0)
    part = wq.shape[1]
    heads, size = qkv.shape[1], qkv.shape[2]
    tile = x_here.shape[1]
    copies = [
        [pltpu.make_async_copy(piece, there.at[n], arrived.at[which, n]) for n, piece in enumerate(pieces)]
        for which, (there, pieces) in enumerate((
            (x_here, row_pieces(places, x_own, x_sib, near, far, 0, tile)),
            (dy_here, row_pieces(places, dy_own, dy_sib, near, far, 1, tile)),
        ))
    ]

    @pl.when(step == 0)
    def _():
        for pair in zip(*copies):
            for copy in pair:
                copy.start()
        lanes = pl.ds(pl.multiple_of(places[2] * part, 128), part)
        for n, w in enumerate((wq, wk, wv)):
            rows = slice(n * part, (n + 1) * part)
            w_t[rows, :] = w[...].T
            jb[rows, :] = jnp.broadcast_to(pack[9 + n : 10 + n, lanes], (128, part)).T

    for number in range(4):

        @pl.when(step == number)
        def _():
            copies[0][number].wait()
            copies[1][number].wait()

    hat, _ = norm_stats(x_here[step].astype(F32))
    turned = (hat * pack[0:1, :] + pack[1:2, :]).astype(BF16).T
    normed_t[...] = turned
    mix = dot_nt(wd[...], dy_here[step])
    c, s = cos[...], sin[...]
    for n in range(3):
        rows = slice(n * part, (n + 1) * part)
        joint = dot(w_t[rows, :], turned) + jnp.concatenate([jb[rows, :]] * (c.shape[1] // 128), axis=1)
        for h in range(heads):
            one = joint[h * size : (h + 1) * size]
            if n < 2:
                a, b = one[:HALF], one[HALF:RD]
                one = jnp.concatenate([a * c - b * s, b * c + a * s, one[RD:]], axis=0)
            if n == 0:
                one = one * size**-0.5
            qkv[n, h] = one.astype(BF16)
    for h in range(heads):
        mix_t[h] = mix[h * size : (h + 1) * size].astype(BF16)


def project(places, x_own, x_sib, dy_own, dy_sib, near, far, pack, joint_w, dense_w, cos, sin,
            heads, deps=()):
    tokens, features = x_own.shape
    tile = tokens // 2
    part = features // 2
    size = part // heads
    weight = lambda n: pl.BlockSpec((features, part), lambda g, p: (0, 2 * n + p[2]))
    lane = pl.BlockSpec((HALF, tile), lambda g, p: (0, g))
    return pl.pallas_call(
        after(project_kernel, 14, len(deps)),
        out_shape=(
            shaped((features, 2 * tokens), BF16),
            shaped((3, heads, size, 2 * tokens), BF16),
            shaped((heads, size, 2 * tokens), BF16),
        ),
        grid_spec=pltpu.PrefetchScalarGridSpec(
            num_scalar_prefetch=1,
            grid=(4,),
            in_specs=[ANYWHERE] * 6
            + [whole(pack.shape), weight(0), weight(1), weight(2),
               pl.BlockSpec((part, features), lambda g, p: (p[2], 0)), lane, lane]
            + [ANYWHERE] * len(deps),
            out_specs=(
                pl.BlockSpec((features, tile), lambda g, p: (0, g)),
                pl.BlockSpec((3, heads, size, tile), lambda g, p: (0, 0, 0, g)),
                pl.BlockSpec((heads, size, tile), lambda g, p: (0, 0, g)),
            ),
            scratch_shapes=[pltpu.VMEM((3 * part, features), BF16), pltpu.VMEM((3 * part, 128), F32),
                            pltpu.VMEM((4, tile, features), BF16), pltpu.VMEM((4, tile, features), BF16),
                            pltpu.SemaphoreType.DMA((2, 4))],
        ),
        cost_estimate=lasting(12),
        compiler_params=params(),
    )(places, x_own, x_sib, dy_own, dy_sib, near, far, pack,
      joint_w, joint_w, joint_w, dense_w, cos, sin, *deps)


def placing(bounds, segs, block, chunk, total):
    per_chunk = chunk // block
    tag = bounds[segs - 1]

    def place(b):
        k = (b // per_chunk) ^ tag
        slot = 2 * (k & 1) + (k >> 1)
        return pl.multiple_of(slot * chunk + (b % per_chunk) * block, block)

    def halved(offset):
        half = offset // (total // 2)
        return half, pl.ds(pl.multiple_of(offset - half * (total // 2), block), block)

    def first_of(position):
        start = jnp.int32(0)
        for m in range(segs - 1):
            start = jnp.where(bounds[m] <= position, bounds[m], start)
        return start

    def last_of(position):
        end = jnp.int32(total)
        for m in range(segs - 2, -1, -1):
            end = jnp.where(bounds[m] > position, bounds[m], end)
        return end - 1

    return place, halved, first_of, last_of


def sentence_rows(bounds, segs, pos):
    seg = jnp.zeros_like(pos)
    for m in range(segs - 1):
        seg = seg + (pos >= bounds[m]).astype(jnp.int32)
    rows = lax.broadcasted_iota(jnp.int32, (16, pos.shape[1]), 0)
    same = rows == seg
    onehot = jnp.where(same, 1.0, 0.0).astype(BF16)
    away = jnp.where(same | (rows >= segs), 0.0, NEGATIVE).astype(BF16)
    return onehot, away


def causal_bias(block):
    key = lax.broadcasted_iota(jnp.int32, (block, block), 0)
    query = lax.broadcasted_iota(jnp.int32, (block, block), 1)
    return jnp.where(key <= query, 0.0, NEGATIVE)


def staged(heads, *steps):
    for turn in range(len(heads) + len(steps) - 1):
        for number, step in enumerate(steps):
            if 0 <= turn - number < len(heads):
                step(heads[turn - number])


def in_runs(start, end, body, run=2):
    runs = (end - start) // run

    def several(n, _):
        body([start + n * run + r for r in range(run)])
        return 0

    def single(n, _):
        body([n])
        return 0

    lax.fori_loop(0, runs, several, 0)
    if run > 1:
        lax.fori_loop(start + runs * run, end, single, 0)


def forward_kernel(
    bounds, q, k, v, mix, pos, out_near, out_far, stats, qa, kn, acc, top, low,
    *, heads, block, chunk, segs,
):
    total = q.shape[-1]
    size = q.shape[2]
    place, halved, first_of, _ = placing(bounds, segs, block, chunk, total)
    hs = range(heads)
    onehot, away = sentence_rows(bounds, segs, pos[...])
    for h in hs:
        qa[h, :size, :] = q[0, h]
        qa[h, size:, :] = away
        kn[h] = jnp.concatenate([k[0, h], onehot], axis=0).T
    bias = causal_bias(block)

    def queries(i, _):
        half, lanes = halved(place(i))
        qs = pl.ds(place(i), block)
        s = [dot(kn[h, qs, :], qa[h, :, qs]) + bias for h in hs]
        m = [jnp.max(s[h], axis=0, keepdims=True) for h in hs]
        p = [jnp.exp(s[h] - m[h]) for h in hs]
        o = [dot(v[0, h, :, qs], p[h].astype(BF16)) for h in hs]
        l = [jnp.sum(p[h], axis=0, keepdims=True) for h in hs]
        for h in hs:
            top[h] = m[h]
            low[h] = l[h]
            acc[h] = o[h]

        def keys(blocks):
            parts = [pl.ds(place(j), block) for j in blocks]
            s, p, f = {}, {}, {}

            def score(h):
                s[h] = [dot(kn[h, ks, :], qa[h, :, qs]) for ks in parts]

            def soften(h):
                m_old = top[h]
                m = m_old
                for one in s[h]:
                    m = jnp.maximum(m, jnp.max(one, axis=0, keepdims=True))
                e = [jnp.exp(one - m) for one in s[h]]
                f[h] = jnp.exp(m_old - m)
                top[h] = m
                low[h] = low[h] * f[h] + sum(jnp.sum(one, axis=0, keepdims=True) for one in e)
                p[h] = [one.astype(BF16) for one in e]

            def gather(h):
                acc[h] = acc[h] * f[h] + sum(dot(v[0, h, :, ks], one) for ks, one in zip(parts, p[h]))

            staged(hs, score, soften, gather)

        in_runs(first_of(i * block) // block, i, keys)
        result = [acc[h] / low[h] for h in hs]
        for number, out in enumerate((out_near, out_far)):

            @pl.when(half == number)
            def _():
                for h in hs:
                    out[h, :, lanes] = result[h].astype(BF16)

        for h in hs:
            o = result[h]
            stats[h, 0:1, qs] = top[h] + jnp.log(low[h])
            stats[h, 1:2, qs] = jnp.sum(o * mix[h, :, qs].astype(F32), axis=0, keepdims=True)
        return 0

    lax.fori_loop(0, total // block, queries, 0)


def attend(bounds, qkv, mix, pos, chunk, segs, deps=(), block=256):
    _, heads, size, total = qkv.shape
    part = lambda n: pl.BlockSpec((1, heads, size, total), lambda g, b: (n, 0, 0, 0))
    kernel = functools.partial(forward_kernel, heads=heads, block=block, chunk=chunk, segs=segs)
    return pl.pallas_call(
        after(kernel, 6, len(deps)),
        out_shape=(shaped((heads, size, total // 2), BF16),) * 2 + (shaped((heads, 2, total), F32),),
        grid_spec=pltpu.PrefetchScalarGridSpec(
            num_scalar_prefetch=1,
            grid=(1,),
            in_specs=[part(0), part(1), part(2), whole((heads, size, total)), whole((1, total))]
            + [ANYWHERE] * len(deps),
            out_specs=(whole((heads, size, total // 2)),) * 2 + (whole((heads, 2, total)),),
            scratch_shapes=[
                pltpu.VMEM((heads, size + 16, total), BF16),
                pltpu.VMEM((heads, total, size + 16), BF16),
                pltpu.VMEM((heads, size, block), F32),
                pltpu.VMEM((heads, 1, block), F32),
                pltpu.VMEM((heads, 1, block), F32),
            ],
        ),
        cost_estimate=lasting(30),
        compiler_params=params(),
    )(bounds, qkv, qkv, qkv, mix, pos, *deps)


def backward_kernel(
    bounds, q, k, v, mix, stats, pos, cos, sin, out_near, out_far, qa, kn, vn, dq, dk, dv,
    *, heads, block, chunk, segs,
):
    total = q.shape[-1]
    size = q.shape[2]
    place, halved, _, last_of = placing(bounds, segs, block, chunk, total)
    hs = range(heads)
    onehot, away = sentence_rows(bounds, segs, pos[...])
    for h in hs:
        qa[h, :size, :] = q[0, h]
        qa[h, size:, :] = away
        kn[h] = jnp.concatenate([k[0, h], onehot], axis=0).T
        vn[h] = v[0, h].T
    bias = causal_bias(block)
    dq[...] = jnp.zeros_like(dq)

    def pairs(parts, ks, add, fresh):
        p, ds, s, dp = {}, {}, {}, {}

        def score(h):
            s[h] = [dot(kn[h, ks, :], qa[h, :, qs]) for qs in parts]
            dp[h] = [dot(vn[h, ks, :], mix[h, :, qs]) for qs in parts]

        def soften(h):
            p[h], ds[h] = [], []
            for qs, one, back in zip(parts, s[h], dp[h]):
                e = jnp.exp((one if add is None else one + add) - stats[h, 0:1, qs])
                p[h].append(e.astype(BF16))
                ds[h].append((e * (back - stats[h, 1:2, qs])).astype(BF16))

        def gather(h):
            a = sum(dot_nt(mix[h, :, qs], one) for qs, one in zip(parts, p[h]))
            b = sum(dot_nt(q[0, h, :, qs], one) for qs, one in zip(parts, ds[h]))
            dv[h] = a if fresh else dv[h] + a
            dk[h] = b if fresh else dk[h] + b
            for qs, one in zip(parts, ds[h]):
                dq[h, :, qs] += dot(k[0, h, :, ks], one)

        staged(hs, score, soften, gather)

    def turned_back(g, c, s):
        a, b = g[:HALF], g[HALF:RD]
        return jnp.concatenate([a * c + b * s, b * c - a * s, g[RD:]], axis=0).astype(BF16)

    def keys(j, _):
        ks = pl.ds(place(j), block)
        pairs([ks], ks, bias, True)
        in_runs(
            j + 1,
            last_of((j + 1) * block - 1) // block + 1,
            lambda blocks: pairs([pl.ds(place(i), block) for i in blocks], ks, None, False),
            1,
        )
        half, lanes = halved(place(j))
        c, s = cos[:, ks], sin[:, ks]
        g = [(turned_back(dk[h], c, s), dv[h].astype(BF16)) for h in hs]
        for number, out in enumerate((out_near, out_far)):

            @pl.when(half == number)
            def _():
                for h in hs:
                    out[1, h, :, lanes] = g[h][0]
                    out[2, h, :, lanes] = g[h][1]

        return 0

    lax.fori_loop(0, total // block, keys, 0)
    c, s = cos[...], sin[...]
    for h in hs:
        g = turned_back(dq[h] * size**-0.5, c, s)
        out_near[0, h] = g[:, : total // 2]
        out_far[0, h] = g[:, total // 2 :]


def attend_back(bounds, qkv, mix, stats, pos, cos, sin, chunk, segs, deps=(), block=256):
    _, heads, size, total = qkv.shape
    part = lambda n: pl.BlockSpec((1, heads, size, total), lambda g, b: (n, 0, 0, 0))
    kernel = functools.partial(backward_kernel, heads=heads, block=block, chunk=chunk, segs=segs)
    return pl.pallas_call(
        after(kernel, 9, len(deps)),
        out_shape=(shaped((3, heads, size, total // 2), BF16),) * 2,
        grid_spec=pltpu.PrefetchScalarGridSpec(
            num_scalar_prefetch=1,
            grid=(1,),
            in_specs=[part(0), part(1), part(2), whole((heads, size, total)),
                      whole((heads, 2, total)), whole((1, total)), whole((HALF, total)), whole((HALF, total))]
            + [ANYWHERE] * len(deps),
            out_specs=(whole((3, heads, size, total // 2)),) * 2,
            scratch_shapes=[
                pltpu.VMEM((heads, size + 16, total), BF16),
                pltpu.VMEM((heads, total, size + 16), BF16),
                pltpu.VMEM((heads, total, size), BF16),
                pltpu.VMEM((heads, size, total), F32),
                pltpu.VMEM((heads, size, block), F32),
                pltpu.VMEM((heads, size, block), F32),
            ],
        ),
        cost_estimate=lasting(45),
        compiler_params=params(),
    )(bounds, qkv, qkv, qkv, mix, stats, pos, cos, sin, *deps)


def joint_grads_kernel(
    places, normed_t, near, far, mixed, mixed_far, dy_own, dy_sib, dy_near, dy_far, out, bias,
    nt, g, mx, dy, made, arrived, gone, *, which,
):
    part, tokens = mixed.shape
    tile = tokens // 2
    lanes = pl.ds(pl.multiple_of(places[4 + which] * part, 128), part)
    copy = pltpu.make_async_copy
    first = copy(normed_t.at[lanes], nt, arrived.at[3, 0])
    first.start()
    later = []
    for n in range(3):
        later.append([copy(near.at[n], g.at[n, 0], arrived.at[n, 0]), copy(far.at[n], g.at[n, 1], arrived.at[n, 1])])
    last = [copy(mixed, mx.at[0], arrived.at[3, 1]), copy(mixed_far, mx.at[1], arrived.at[3, 2])]
    pieces = row_pieces(places, dy_own, dy_sib, dy_near, dy_far, 1, tile, lanes)
    last += [copy(piece, dy.at[n], arrived.at[4, n]) for n, piece in enumerate(pieces)]
    later.append(last)
    for copies in later:
        for one in copies:
            one.start()
    first.wait()
    leaving = []
    for n in range(4):
        for one in later[n]:
            one.wait()
        if n < 3:
            made[n] = (dot_nt(nt[:, :tokens], g[n, 0]) + dot_nt(nt[:, tokens:], g[n, 1])).astype(BF16)
        else:
            made[n] = (
                dot(mx[0, :, :tile], dy[0]) + dot(mx[0, :, tile:], dy[1])
                + dot(mx[1, :, :tile], dy[2]) + dot(mx[1, :, tile:], dy[3])
            ).astype(BF16)
        leaving.append(copy(made.at[n], out.at[:, n * part : (n + 1) * part], gone.at[n]))
        leaving[-1].start()
        if n < 3:
            total = None
            for half in range(2):
                for at in range(0, tokens, 128):
                    one = g[n, half, :, at : at + 128].astype(F32)
                    total = one if total is None else total + one
            bias[n] = jnp.sum(total.T, axis=0, keepdims=True)
    for one in leaving:
        one.wait()


def joint_grads(places, which, normed_t, grads, mixed, dy_own, dy_sib, near, far, deps=()):
    features, total = normed_t.shape
    part = features // 2
    tokens = total // 2
    return pl.pallas_call(
        after(functools.partial(joint_grads_kernel, which=which), 10, len(deps)),
        out_shape=(shaped((part, 4 * part), BF16), shaped((3, 1, part), F32)),
        grid_spec=pltpu.PrefetchScalarGridSpec(
            num_scalar_prefetch=1,
            grid=(1,),
            in_specs=[ANYWHERE] * (9 + len(deps)),
            out_specs=(ANYWHERE, whole((3, 1, part))),
            scratch_shapes=[
                pltpu.VMEM((part, total), BF16), pltpu.VMEM((3, 2, part, tokens), BF16),
                pltpu.VMEM((2, part, tokens), BF16), pltpu.VMEM((4, tokens // 2, part), BF16),
                pltpu.VMEM((4, part, part), BF16), pltpu.SemaphoreType.DMA((5, 4)),
                pltpu.SemaphoreType.DMA((4,)),
            ],
        ),
        cost_estimate=lasting(7),
        compiler_params=params(),
    )(places, normed_t, grads[0], grads[1], mixed[0], mixed[1], dy_own, dy_sib, near, far, *deps)


def norm_back_of(grad, x, gain):
    hat, inverse = norm_stats(x)
    scaled = grad * gain
    dx = inverse * (
        scaled
        - jnp.mean(scaled, axis=-1, keepdims=True)
        - hat * jnp.mean(scaled * hat, axis=-1, keepdims=True)
    )
    return dx, jnp.sum(grad * hat, axis=0, keepdims=True), jnp.sum(grad, axis=0, keepdims=True)


def norm_back_kernel(places, own, sib, w, x, pack, *refs):
    *before, dx_out, gain_grad, bias_grad = refs
    part = own.shape[1]
    core = places[2]
    total = None
    for n in range(3):
        mine = pl.ds(pl.multiple_of((2 * n + core) * part, 128), part)
        other = pl.ds(pl.multiple_of((2 * n + 1 - core) * part, 128), part)
        one = dot(w[:, mine], own[n]) + dot(w[:, other], sib[n])
        total = one if n == 0 else total + one
    x_here = x[...].reshape(dx_out.shape)
    dx, g, b = norm_back_of(total.T, x_here.astype(F32), pack[0:1, :])
    dx_out[...] = dx.astype(dx_out.dtype)
    gain_grad[...] = before[0][...] + g if before else g
    bias_grad[...] = before[1][...] + b if before else b


def norm_back(places, own, sib, w, x, pack, far, before=(), deps=()):
    part = own.shape[1]
    features = w.shape[0]
    tile = own.shape[2] // 2
    piece = pl.BlockSpec((3, part, tile), lambda g, p: (0, 0, int(far)))
    token = (
        pl.BlockSpec((1, tile, features), lambda g, p: (0, 0, 0))
        if far
        else pl.BlockSpec((tile, features), lambda g, p: (p[3], 0))
    )
    vector = whole((1, features))
    return pl.pallas_call(
        after(norm_back_kernel, 6 + len(before), len(deps)),
        out_shape=(shaped((tile, features), BF16 if far else F32),
                   shaped((1, features), F32), shaped((1, features), F32)),
        grid_spec=pltpu.PrefetchScalarGridSpec(
            num_scalar_prefetch=1,
            grid=(1,),
            in_specs=[piece, piece, whole(w.shape), token, whole(pack.shape)] + [vector] * len(before)
            + [ANYWHERE] * len(deps),
            out_specs=(whole((tile, features)), vector, vector),
        ),
        cost_estimate=lasting(6),
        compiler_params=params(),
    )(places, own, sib, w, x, pack, *before, *deps)


def products_kernel(places, act_a, act_b, hid_a, hid_b, wc_a, wc_b, we_a, we_b, out, back):
    out[...] = (dot(act_a[...], wc_a[...]) + dot(act_b[...], wc_b[...])).astype(out.dtype)
    back[...] = (dot_nt(hid_a[...], we_a[...]) + dot_nt(hid_b[...], we_b[...])).astype(back.dtype)


def products(places, sent, kept, wc, we, sibling, deps=()):
    tokens, units = sent[1].shape[0] // 2, sent[1].shape[1]
    features = wc.shape[1]
    tile = tokens // 2
    token = pl.BlockSpec((tile, units), lambda g, p: (2 * int(sibling) + g, 0))
    row = lambda n: pl.BlockSpec((units, features), lambda g, p: (p[n], 0))
    column = lambda n: pl.BlockSpec((features, units), lambda g, p: (0, p[n]))
    spec = pl.BlockSpec((tile, features), lambda g, p: (g, 0))
    return pl.pallas_call(
        after(products_kernel, 9, len(deps)),
        out_shape=(shaped((tokens, features), BF16 if sibling else F32),) * 2,
        grid_spec=pltpu.PrefetchScalarGridSpec(
            num_scalar_prefetch=1,
            grid=(2,),
            in_specs=[token] * 4 + [row(0), row(1), column(0), column(1)] + [ANYWHERE] * len(deps),
            out_specs=(spec, spec),
        ),
        cost_estimate=lasting(10),
        compiler_params=params(),
    )(places, sent[1], kept[1], sent[2], kept[2], wc, wc, we, we, *deps)


def block_out_kernel(places, x, out, out_sib, mixed, mixed_sib, mixed_near, wd, pack, block_out):
    step = pl.program_id(0)
    part, tile = mixed.shape[0], x.shape[0]
    core = places[2]
    mine = pl.ds(pl.multiple_of(core * part, 128), part)
    other = pl.ds(pl.multiple_of((1 - core) * part, 128), part)

    def finish(ours, siblings):
        attn = dot(ours.T, wd[mine, :]) + dot(siblings.T, wd[other, :])
        feed = out[...] + out_sib[...].astype(F32)
        block_out[...] = (x[...].astype(F32) + attn + feed + pack[4:5, :]).astype(BF16)

    @pl.when(step == 0)
    def _():
        finish(mixed[:, :tile], mixed_sib[:, :tile])

    @pl.when(step == 1)
    def _():
        finish(mixed_near[:part, :], mixed_near[part:, :])


def block_result(places, x, out, out_sib, mixed, mixed_sib, mixed_near, wd, pack, deps=()):
    tokens, features = out.shape
    tile = tokens // 2
    part = features // 2
    token = pl.BlockSpec((tile, features), lambda g, p: (p[3] ^ g, 0))
    return pl.pallas_call(
        after(block_out_kernel, 9, len(deps)),
        out_shape=shaped((tokens, features), BF16),
        grid_spec=pltpu.PrefetchScalarGridSpec(
            num_scalar_prefetch=1,
            grid=(2,),
            in_specs=[token] * 3 + [whole((part, tokens)), whole((part, tokens)), whole((features, tile)),
                      whole((features, features)), whole(pack.shape)] + [ANYWHERE] * len(deps),
            out_specs=token,
        ),
        cost_estimate=lasting(8),
        compiler_params=params(),
    )(places, x, out, out_sib, mixed, mixed_sib, mixed_near, wd, pack, *deps)


def input_grad_kernel(
    places, x, dy, back, back_sib, dx_own, dx_near, pack, gain_attn, bias_attn, out_bias, be_sent, be_kept,
    joint_b, input_grad, small, gain_sum, bias_sum,
):
    step = pl.program_id(0)
    features = x.shape[1]
    dx_feed, g, b = norm_back_of(
        back[...] + back_sib[...].astype(F32), x[...].astype(F32), pack[2:3, :]
    )

    @pl.when(step == 0)
    def _():
        input_grad[...] = (dy[...].astype(F32) + dx_own[...] + dx_feed).astype(BF16)
        gain_sum[...] = g
        bias_sum[...] = b

    @pl.when(step == 1)
    def _():
        input_grad[...] = (dy[...].astype(F32) + dx_near[...].astype(F32) + dx_feed).astype(BF16)
        small[...] = jnp.zeros_like(small)
        small[0:1, :features] = gain_attn[...]
        small[0:1, features:] = bias_attn[...]
        small[1:2, :features] = gain_sum[...] + g
        small[1:2, features:] = bias_sum[...] + b
        small[2:3, :features] = out_bias[...]
        first = places[5] == 0
        small[2:3, features:] = jnp.where(first, be_kept[...], be_sent[...])
        small[3:4, :features] = jnp.where(first, be_sent[...], be_kept[...])
        half = features // 2
        small[3:4, features : features + half] = joint_b[0]
        small[3:4, features + half :] = joint_b[1]
        small[4:5, :half] = joint_b[2]


def input_result(places, x, dy, back, back_sib, dx_own, dx_near, pack, sums, joint_b, deps=()):
    tokens, features = x.shape
    tile = tokens // 2
    token = pl.BlockSpec((tile, features), lambda g, p: (p[3] ^ g, 0))
    return pl.pallas_call(
        after(input_grad_kernel, 14, len(deps)),
        out_shape=(shaped((tokens, features), BF16), shaped((8, 2 * features), F32)),
        grid_spec=pltpu.PrefetchScalarGridSpec(
            num_scalar_prefetch=1,
            grid=(2,),
            in_specs=[token] * 4 + [whole((tile, features))] * 2 + [whole(pack.shape)]
            + [whole((1, features))] * 5 + [whole(joint_b.shape)] + [ANYWHERE] * len(deps),
            out_specs=(token, whole((8, 2 * features))),
            scratch_shapes=[pltpu.VMEM((1, features), F32), pltpu.VMEM((1, features), F32)],
        ),
        cost_estimate=lasting(8),
        compiler_params=params(),
    )(places, x, dy, back, back_sib, dx_own, dx_near, pack, *sums, joint_b, *deps)


class Links:
    def __init__(self, row_count):
        self.row_count = row_count
        self.row_bits = row_count.bit_length() - 1
        dims = [0, 1, "x", *range(2, self.row_bits)]
        other = list(dims)
        for n in range(0, len(dims) - 1, 2):
            other[n], other[n + 1] = other[n + 1], other[n]
        self.orders = (dims, other)
        self.rounds = len(dims)
        self.groups = [(n,) for n in range(self.rounds)]

    def bit(self, number, sibling=False):
        def of(dim):
            if dim == "x":
                return lax.axis_index("x")
            return (lax.axis_index("rows") >> dim) & 1

        return jnp.where(
            lax.axis_index("core") == int(sibling), of(self.orders[0][number]), of(self.orders[1][number])
        )

    def swap(self, array, *numbers):
        pairs = []
        for row in range(self.row_count):
            for x in range(2):
                for core in range(2):
                    there = [row, x]
                    for number in numbers:
                        dim = self.orders[core][number]
                        if dim == "x":
                            there[1] = 1 - there[1]
                        else:
                            there[0] ^= 1 << dim
                    pairs.append(((row * 2 + x) * 2 + core, (there[0] * 2 + there[1]) * 2 + core))
        return lax.ppermute(array, CHIP, pairs)

    def others(self, group):
        return [group] if len(group) == 1 else [group[1:], group[:1], group]

    def swap_group(self, arrays, group):
        return [self.swap(array, *numbers) for array, numbers in zip(arrays, self.others(group))]


def swap_core(array):
    return lax.ppermute(array, "core", [(0, 1), (1, 0)])


def swap_x(array):
    return lax.ppermute(array, "x", [(0, 1), (1, 0)])


def add(a, b):
    return (a.astype(F32) + b.astype(F32)).astype(BF16)


def total_of(terms):
    total = terms[0].astype(F32)
    for term in terms[1:]:
        total = total + term.astype(F32)
    return total.astype(BF16)


def divide_kernel(place, *refs, terms, pieces):
    for n in range(pieces):
        refs[terms * pieces + n][...] = total_of([refs[t * pieces + n][...] for t in range(terms)])


def divide(bits, terms, deps=()):
    place = bits[0] if len(bits) == 1 else bits[0] * 2 + bits[1]
    pieces = 2 ** len(bits)
    rows, width = terms[0].shape
    rows = rows // pieces
    if rows % 16:
        return [
            total_of([lax.dynamic_slice_in_dim(t, (place ^ n) * rows, rows, 0) for t in terms])
            for n in range(pieces)
        ]
    tile = min(rows, 384)
    steps = rows // tile
    source = lambda n: pl.BlockSpec((tile, width), lambda t, p: ((p[0] ^ n) * steps + t, 0))
    kernel = functools.partial(divide_kernel, terms=len(terms), pieces=pieces)
    return pl.pallas_call(
        after(kernel, 1 + len(terms) * pieces, len(deps)),
        out_shape=(shaped((rows, width), BF16),) * pieces,
        grid_spec=pltpu.PrefetchScalarGridSpec(
            num_scalar_prefetch=1,
            grid=(steps,),
            in_specs=[source(n) for n in range(pieces)] * len(terms) + [ANYWHERE] * len(deps),
            out_specs=(pl.BlockSpec((tile, width), lambda t, p: (t, 0)),) * pieces,
        ),
        cost_estimate=lasting(1),
        compiler_params=params(),
    )(place.astype(jnp.int32).reshape(1), *[t for t in terms for _ in range(pieces)], *deps)


def in_order(bits, pieces):
    if len(pieces) == 2:
        mine, other = pieces
        forward, back = jnp.concatenate([mine, other], axis=0), jnp.concatenate([other, mine], axis=0)
        return jnp.where(bits[-1] == 0, forward, back)
    low, high = in_order(bits[1:], pieces[:2]), in_order(bits[1:], pieces[2:])
    return in_order(bits[:1], [low, high])


def two_parts(vector):
    high = lax.reduce_precision(vector, 8, 7)
    low = lax.reduce_precision(vector - high, 8, 7)
    return jnp.concatenate([high, low], axis=0).astype(BF16), high + low


def one_part(pair):
    rows = pair.shape[0] // 2
    return pair[:rows].astype(F32) + pair[rows:].astype(F32)


def spread_kernel(*refs, parts):
    contract, expand = refs[2 * parts :]
    rows = contract.shape[0] // parts
    for q in range(parts):
        contract[q * rows : (q + 1) * rows, :] = refs[q][...].astype(F32)
        expand[q * rows : (q + 1) * rows, :] = refs[parts + q][...].astype(F32)


def spread(gathered, links, features, units, deps=()):
    piece = features >> (links.rounds - 2)
    parts = features // piece

    def rank(core, half, which, quarter):
        def one(order):
            place = 0
            bits = {order[0]: half, order[1]: which}
            for n, dim in enumerate(order[2:]):
                bits[dim] = (quarter >> (links.rounds - 3 - n)) & 1
            for dim, value in bits.items():
                place = place + (value * 2 if dim == "x" else value * (4 << dim))
            return place

        return jnp.where(core == 0, one(links.orders[0]), one(links.orders[1])) + core

    source = lambda which, q: pl.BlockSpec((piece, features), lambda c, h: (rank(c, h, which, q), 0))
    return pl.pallas_call(
        after(functools.partial(spread_kernel, parts=parts), 2 * parts, len(deps)),
        out_shape=(shaped((4 * units, features), F32), shaped((features, 4 * units), F32)),
        grid=(2, 2),
        in_specs=[source(which, q) for which in range(2) for q in range(parts)] + [ANYWHERE] * len(deps),
        out_specs=(
            pl.BlockSpec((features, features), lambda c, h: (c * 2 + h, 0)),
            pl.BlockSpec((features, features), lambda c, h: (0, c * 2 + h)),
        ),
        cost_estimate=lasting(12),
        compiler_params=params(),
    )(*[gathered] * (2 * parts), *deps)


def spread_joint_kernel(places, own, sib, *refs, which):
    joint, dense, wide, arrived = refs[-4:]
    part = own.shape[0]
    copies = []
    for g, ref in enumerate((own, sib)):
        core = places[2] ^ g
        rows = pl.ds(pl.multiple_of(places[4 + 2 * g + which] * part, part), part)
        for n in range(4):
            wide[g, n] = ref[:, n * part : (n + 1) * part].astype(F32)
            if n < 3:
                there = joint.at[rows, pl.ds(pl.multiple_of((2 * n + core) * part, part), part)]
            else:
                there = dense.at[pl.ds(pl.multiple_of(core * part, part), part), rows]
            copies.append(pltpu.make_async_copy(wide.at[g, n], there, arrived.at[g, n]))
            copies[-1].start()
    for copy in copies:
        copy.wait()


def spread_joint(places, own, sib, features, which, into=(), deps=()):
    part = features // 2
    return pl.pallas_call(
        functools.partial(spread_joint_kernel, which=which),
        out_shape=(shaped((features, 3 * features), F32), shaped((features, features), F32)),
        grid_spec=pltpu.PrefetchScalarGridSpec(
            num_scalar_prefetch=1,
            grid=(1,),
            in_specs=[whole(own.shape), whole(sib.shape)] + [ANYWHERE] * (len(into) + len(deps)),
            out_specs=(ANYWHERE, ANYWHERE),
            scratch_shapes=[pltpu.VMEM((2, 4, part, part), F32), pltpu.SemaphoreType.DMA((2, 4))],
        ),
        input_output_aliases={3: 0, 4: 1} if into else {},
        cost_estimate=lasting(4),
        compiler_params=params(),
    )(places, own, sib, *into, *deps)


def per_device(
    links, block_in, lengths, attn_gain, attn_bias, feed_gain, feed_bias, joint_weight, joint_bias,
    dense_weight, dense_bias, expand_weight, expand_bias, contract_weight, contract_bias, out_cotangent,
):
    rows_here, chunk, features = block_in.shape
    tokens = rows_here * chunk
    total = 2 * tokens
    segs = lengths.shape[1]
    heads = H // 2
    part = features // 2
    units = expand_weight.shape[1] // 4
    x_at, core_at = lax.axis_index("x"), lax.axis_index("core")
    chunk_at = x_at * 2 + core_at

    x_own, dy_own = block_in.reshape(tokens, features), out_cotangent.reshape(tokens, features)
    x_sib, dy_sib = swap_core(x_own), swap_core(dy_own)
    away = jnp.stack([
        lax.dynamic_index_in_dim(block_in, 1 - x_at, 0, keepdims=False),
        lax.dynamic_index_in_dim(out_cotangent, 1 - x_at, 0, keepdims=False),
    ])
    near = swap_x(away)

    mine = lax.dynamic_index_in_dim(lengths, x_at, 0, keepdims=False)
    before = jnp.tril(jnp.ones((segs, segs), jnp.int32))
    bounds = jnp.sum(before * mine[None, :], axis=1)
    bounds = jnp.where(jnp.arange(segs) == segs - 1, chunk_at, bounds).astype(jnp.int32)
    slots = jnp.arange(4, dtype=jnp.int32)
    starts = (((slots & 1) * 2 + (slots >> 1)) ^ chunk_at) * chunk
    pos = (starts[:, None] + jnp.arange(chunk, dtype=jnp.int32)[None, :]).reshape(1, total)
    inverse = BASE_FREQ ** (-2.0 * jnp.arange(HALF).astype(F32) / RD)
    angles = inverse[:, None] * pos.astype(F32)
    cos, sin = jnp.cos(angles), jnp.sin(angles)

    pack = jnp.concatenate([
        attn_gain, attn_bias, feed_gain, feed_bias, dense_bias + contract_bias, expand_bias, joint_bias,
    ]).reshape(-1, features)
    pack = jnp.pad(pack, ((0, 16 - pack.shape[0]), (0, 0)))

    bits = [links.bit(n) for n in range(links.rounds)]
    of = lambda group: [bits[n] for n in group]
    sib_bit = links.bit(0, True)
    places = jnp.stack(
        [core_at * 2 + 1 - bits[0], core_at * 2 + bits[0], core_at, x_at, 1 - bits[0], bits[0],
         1 - sib_bit, sib_bit]
    ).astype(jnp.int32)

    def feed(number, x, deps):
        base = (places[number] * (units // 256)).reshape(1)
        return feed_part(base, x, dy_own, dy_sib, pack, expand_weight, contract_weight, units, deps)

    sent = feed(0, (x_own, x_sib), (away,))
    arrived = links.swap(sent[0], 0)
    kept = feed(1, sent[5:], (sent[0],))
    near = once(near, (kept[0],))
    far = swap_core(near)

    flat = lambda a: a.reshape(2 * units, features)
    first, second, *rest = links.groups
    stay, outgoing = divide(of(second), [flat(kept[0]), flat(arrived)])
    terms = [stay, links.swap(outgoing, *second)]
    normed_t, qkv, mix_t = project(
        places, x_own, x_sib, dy_own, dy_sib, near, far, pack, joint_weight, dense_weight, cos, sin,
        heads, (outgoing,),
    )
    ready = normed_t
    for number, group in enumerate(rest):
        stay, *outgoing = divide(of(group), terms, (ready,))
        terms = [stay, *links.swap_group(outgoing, group)]
        ready = stay
        if number == 0:
            out_sib, back_sib = products(places, sent, kept, contract_weight, expand_weight, True, (stay,))
            ready = out_sib
    out_own, back_own = products(places, sent, kept, contract_weight, expand_weight, False, (stay,))
    out_sib, back_sib = swap_core(out_sib), swap_core(back_sib)
    terms[-1] = once(terms[-1], (out_own,))
    last = total_of(terms)
    gathered = lax.all_gather(last, CHIP, axis=0, tiled=True)
    mixed_own, mixed_far, stats = attend(bounds, qkv, mix_t, pos, chunk, segs, (last,))
    mixed_own, mixed_far = mixed_own.reshape(part, tokens), mixed_far.reshape(part, tokens)
    grads = attend_back(bounds, qkv, mix_t, stats, pos, cos, sin, chunk, segs)
    grads = [g.reshape(3, part, tokens) for g in grads]
    grads_sib = swap_core(grads[1])
    mixed = (mixed_own, mixed_far)
    outgoing, joint_b = joint_grads(places, 0, normed_t, grads, mixed, dy_own, dy_sib, near, far)
    arrived = links.swap(outgoing, *first)
    current, _ = joint_grads(places, 1, normed_t, grads, mixed, dy_own, dy_sib, near, far, (outgoing,))
    mixed_sib = swap_core(once(mixed_far, (grads[0],)))
    mixed_near = swap_x(jnp.concatenate([mixed_own[:, chunk:], mixed_sib[:, chunk:]], axis=0))
    dx_far, *before = norm_back(
        places, grads[0], grads_sib, joint_weight, near, pack, True, (), (current,)
    )
    dx_near = swap_x(dx_far)
    dx_own, gain_attn, bias_attn = norm_back(
        places, grads[0], grads_sib, joint_weight, x_own, pack, False, before, (dx_far,)
    )
    stay, outgoing = divide(of(second), [current, arrived], (dx_own,))
    terms = [stay, links.swap(outgoing, *second)]
    block_out = block_result(
        places, x_own, out_own, out_sib, mixed_own, mixed_sib, mixed_near, dense_weight, pack, (stay,)
    )
    ready = block_out
    for number, group in enumerate(rest):
        stay, *outgoing = divide(of(group), terms, (ready,))
        terms = [stay, *links.swap_group(outgoing, group)]
        ready = stay
        if number == 0:
            input_grad, small = input_result(
                places, x_own, dy_own, back_own, back_sib, dx_own, dx_near, pack,
                (gain_attn, bias_attn, sent[4], sent[3], kept[3]), joint_b, (stay,),
            )
            ready = input_grad
    current = total_of(terms)

    shared = 5 * features

    def summed(group, small):
        pair, small = two_parts(small)
        outgoing = jnp.concatenate([current, pair], axis=0)
        rows_now = current.shape[0]
        arrived = [links.swap(outgoing, *numbers) for numbers in links.others(group)]
        parts = [small] + [one_part(array[rows_now:]) for array in arrived]
        while len(parts) > 1:
            parts = [a + b for a, b in zip(parts[::2], parts[1::2])]
        return in_order(of(group), [current] + [array[:rows_now] for array in arrived]), parts[0]

    for group in reversed(rest):
        current, small = summed(group, small)
    pair, small = two_parts(small)
    rows_now = current.shape[0]
    outgoing = jnp.concatenate([current, pair], axis=0)
    arrived = links.swap(outgoing, *second)
    one, both = links.swap(pair, *first), links.swap(pair, *first, *second)
    small = (small + one_part(arrived[rows_now:])) + (one_part(one) + one_part(both))
    current = in_order(of(second), [current, arrived[:rows_now]])
    arrived = links.swap(current, *first)
    sib_current = swap_core(current)
    pair, small = two_parts(small)
    small_sib = one_part(swap_core(pair)).reshape(-1)
    small = small.reshape(-1)
    sums = (small + small_sib)[:shared].reshape(5, features)
    ordered = lambda a, b: jnp.where(core_at == 0, jnp.stack([a, b]), jnp.stack([b, a]))
    single = ordered(small[shared:], small_sib[shared:])
    grad_expand_b = single[:, : 2 * units].reshape(-1)
    grad_joint_b = single[:, 2 * units : 2 * units + 3 * part].reshape(2, 3, part).transpose(1, 0, 2).reshape(-1)
    grad_contract_w, grad_expand_w = spread(gathered, links, features, units, (current,))
    into = spread_joint(places, current, sib_current, features, 1)
    arrived = once(arrived, (into[0], grad_contract_w, sums, grad_joint_b, grad_expand_b))
    sib_arrived = swap_core(arrived)
    grad_joint_w, grad_dense_w = spread_joint(places, arrived, sib_arrived, features, 0, into)
    return (
        block_out.reshape(block_in.shape),
        input_grad.reshape(block_in.shape),
        sums[0],
        sums[1],
        sums[2],
        sums[3],
        grad_joint_w,
        grad_joint_b,
        grad_dense_w,
        sums[4],
        grad_expand_w,
        grad_expand_b,
        grad_contract_w,
        sums[4],
    )


def solution(mesh):
    row_count, seq_count = mesh.devices.shape
    chips = Mesh(mesh.devices.reshape(row_count, seq_count // 2, 2), CHIP)
    links = Links(row_count)
    tokens = P("rows", ("x", "core"), None)
    in_specs = (tokens, P("rows", None)) + (P(),) * 12 + (tokens,)
    out_specs = (tokens, tokens) + (P(),) * 12
    return jax.shard_map(
        functools.partial(per_device, links), mesh=chips, in_specs=in_specs, out_specs=out_specs,
        check_vma=False,
    )
```

```python
import functools

import jax
import jax.numpy as jnp
from jax import lax
from jax.experimental import pallas as pl
from jax.experimental.pallas import tpu as pltpu
from jax.sharding import Mesh, PartitionSpec as P

H = 12
RD = 16
HALF = RD // 2
EPSILON = 1e-05
BASE_FREQ = 10000.0
NEGATIVE = -1e30
F32 = jnp.float32
BF16 = jnp.bfloat16
VMEM_BYTES = 63 * 2**20
CHIP = ("rows", "x", "core")
NT = (((1,), (1,)), ((), ()))


def dot(a, b):
    return jnp.dot(a, b, preferred_element_type=F32)


def dot_nt(a, b):
    return lax.dot_general(a, b, NT, preferred_element_type=F32)


def params():
    return pltpu.CompilerParams(vmem_limit_bytes=VMEM_BYTES)


def lasting(microseconds):
    return pl.CostEstimate(flops=int(microseconds * 1e9), bytes_accessed=0, transcendentals=0)


def whole(shape):
    return pl.BlockSpec(shape, lambda *_: (0,) * len(shape))


def shaped(shape, dtype):
    return jax.ShapeDtypeStruct(shape, dtype)


def after(kernel, inputs, deps):
    return lambda *refs: kernel(*refs[:inputs], *refs[inputs + deps :])


ANYWHERE = pl.BlockSpec(memory_space=pl.ANY)


def once(array, deps):
    return pl.pallas_call(
        lambda *refs: None,
        out_shape=shaped(array.shape, array.dtype),
        in_specs=[ANYWHERE] * (1 + len(deps)),
        out_specs=ANYWHERE,
        input_output_aliases={0: 0},
        cost_estimate=lasting(0.1),
    )(array, *deps)


def norm_stats(x):
    centered = x - jnp.mean(x, axis=-1, keepdims=True)
    spread = jnp.mean(centered * centered, axis=-1, keepdims=True)
    inverse = lax.rsqrt(spread + EPSILON)
    return centered * inverse, inverse


def gelu_both(h):
    e = jnp.exp2(h * h * (-0.5 * 1.4426950408889634))
    t = pl.reciprocal(1.0 + jnp.abs(h) * (0.3275911 * 0.7071067811865476), approx=False)
    poly = t * (
        0.5 * 0.254829592
        + t * (0.5 * -0.284496736 + t * (0.5 * 1.421413741 + t * (0.5 * -1.453152027 + t * (0.5 * 1.061405429))))
    )
    tail = poly * e
    phi = jnp.where(h >= 0.0, 1.0 - tail, tail)
    return h * phi, phi + h * e * 0.3989422804014327


def feed_kernel(
    base, x_own, x_sib, dy_own, dy_sib, pack, we, wc,
    grads, act, hid, be_grad, out_bias, normed, nf, act_t, hid_t, x_here, dy_here, gone, arrived,
):
    tokens, features = dy_own.shape
    copy = pltpu.make_async_copy(nf, normed, gone)

    @pl.when(pl.program_id(0) == 0)
    def _():
        tile = 256
        sources = (x_own, x_sib, dy_own, dy_sib)
        places = (x_here.at[0], x_here.at[1], dy_here.at[0], dy_here.at[1])
        copies = [
            pltpu.make_async_copy(a, b, arrived.at[n]) for n, (a, b) in enumerate(zip(sources, places))
        ]
        for one in copies:
            one.start()
        for half in range(2):
            copies[half].wait()

            def norm(i, _):
                here = pl.ds(pl.multiple_of(i * tile, tile), tile)
                there = pl.ds(pl.multiple_of(half * tokens + i * tile, tile), tile)
                hat, _ = norm_stats(x_here[half, here, :].astype(F32))
                nf[there, :] = (hat * pack[2:3, :] + pack[3:4, :]).astype(BF16)
                return 0

            lax.fori_loop(0, tokens // tile, norm, 0)
        copy.start()
        copies[2].wait()
        copies[3].wait()

        def add_up(i, total):
            here = pl.ds(pl.multiple_of(i * tile, tile), tile)
            return total + jnp.sum(dy_here[0, here, :].astype(F32), axis=0, keepdims=True)

        out_bias[...] = lax.fori_loop(0, tokens // tile, add_up, jnp.zeros((1, features), F32))

    feed_tile(base, nf, dy_here.at[0], dy_here.at[1], pack, we, wc, grads, act, hid, be_grad, act_t, hid_t)

    @pl.when(pl.program_id(0) == pl.num_programs(0) - 1)
    def _():
        copy.wait()


def feed_tile(base, nf, dy_own, dy_sib, pack, we, wc, grads, act, hid, be_grad, act_t, hid_t):
    step = pl.program_id(0)
    tokens, features = dy_own.shape
    width = we.shape[1]
    first = (base[0] + step) * width
    be = pack[
        pl.ds(5 + first // features, 1), pl.ds(pl.multiple_of(first % features, width), width)
    ]
    tile = 512
    per = tokens // tile
    count = 2 * per
    hidden, back = [None] * count, [None] * count

    def finish(n):
        value, slope = gelu_both(hidden[n])
        rows = slice(n * tile, (n + 1) * tile)
        value, slope = value.astype(BF16), (back[n] * slope).astype(BF16)
        act[rows, :] = value
        hid[rows, :] = slope
        act_t[:, rows] = value.T
        hid_t[:, rows] = slope.T

    for n in range(count):
        dy_ref = dy_own if n < per else dy_sib
        hidden[n] = dot(nf[n * tile : (n + 1) * tile, :], we[...]) + be
        back[n] = dot_nt(dy_ref[(n % per) * tile : (n % per + 1) * tile, :], wc[...])
        if n > 0:
            finish(n - 1)
    finish(count - 1)
    there = pl.ds(pl.multiple_of(step * width, width), width)
    grads[0, there, :] = (
        dot(act_t[:, :tokens], dy_own[...]) + dot(act_t[:, tokens:], dy_sib[...])
    ).astype(BF16)
    grads[1, :, there] = dot(hid_t[...], nf[...]).T.astype(BF16)
    be_grad[...] = jnp.sum(hid[...].astype(F32), axis=0, keepdims=True)


def feed_part(base, x, dy_own, dy_sib, pack, we, wc, units, deps=()):
    tokens, features = dy_own.shape
    width = 256
    prepared = len(x) == 1
    token = pl.BlockSpec((2 * tokens, width), lambda t, b: (0, t))
    out_shape = (
        shaped((2, units, features), BF16), shaped((2 * tokens, units), BF16),
        shaped((2 * tokens, units), BF16), shaped((1, units), F32),
    )
    out_specs = (whole((2, units, features)), token, token, pl.BlockSpec((1, width), lambda t, b: (0, t)))
    scratch = [pltpu.VMEM((width, 2 * tokens), BF16), pltpu.VMEM((width, 2 * tokens), BF16)]
    if not prepared:
        out_shape += (shaped((1, features), F32), shaped((2 * tokens, features), BF16))
        out_specs += (whole((1, features)), ANYWHERE)
        both = pltpu.VMEM((2, tokens, features), BF16)
        scratch = [pltpu.VMEM((2 * tokens, features), BF16), *scratch, both, both,
                   pltpu.SemaphoreType.DMA, pltpu.SemaphoreType.DMA((4,))]
    return pl.pallas_call(
        after(feed_tile if prepared else feed_kernel, 6 + len(x), len(deps)),
        out_shape=out_shape,
        grid_spec=pltpu.PrefetchScalarGridSpec(
            num_scalar_prefetch=1,
            grid=(units // width,),
            in_specs=([whole(a.shape) for a in (*x, dy_own, dy_sib)] if prepared else [ANYWHERE] * 4)
            + [
                whole(pack.shape),
                pl.BlockSpec((features, width), lambda t, b: (0, b[0] + t)),
                pl.BlockSpec((width, features), lambda t, b: (b[0] + t, 0)),
            ]
            + [ANYWHERE] * len(deps),
            out_specs=out_specs,
            scratch_shapes=scratch,
        ),
        cost_estimate=lasting(22),
        compiler_params=params(),
    )(base, *x, dy_own, dy_sib, pack, we, wc, *deps)


def row_pieces(places, own, sib, near, far, number, tile):
    rows = pl.ds(pl.multiple_of(places[3] * tile, tile), tile)
    return own.at[rows], near.at[number], sib.at[rows], far.at[number]


def project_kernel(
    places, x_own, x_sib, dy_own, dy_sib, near, far, pack, wq, wk, wv, wd,
    cos, sin, normed_t, qkv, mix_t, w_t, jb, x_here, dy_here, arrived,
):
    step = pl.program_id(0)
    part = wq.shape[1]
    heads, size = qkv.shape[1], qkv.shape[2]
    tile = x_here.shape[1]
    copies = [
        [pltpu.make_async_copy(piece, there.at[n], arrived.at[which, n]) for n, piece in enumerate(pieces)]
        for which, (there, pieces) in enumerate((
            (x_here, row_pieces(places, x_own, x_sib, near, far, 0, tile)),
            (dy_here, row_pieces(places, dy_own, dy_sib, near, far, 1, tile)),
        ))
    ]

    @pl.when(step == 0)
    def _():
        for pair in zip(*copies):
            for copy in pair:
                copy.start()
        lanes = pl.ds(pl.multiple_of(places[2] * part, 128), part)
        for n, w in enumerate((wq, wk, wv)):
            rows = slice(n * part, (n + 1) * part)
            w_t[rows, :] = w[...].T
            jb[rows, :] = jnp.broadcast_to(pack[9 + n : 10 + n, lanes], (128, part)).T

    for number in range(4):

        @pl.when(step == number)
        def _():
            copies[0][number].wait()
            copies[1][number].wait()

    hat, _ = norm_stats(x_here[step].astype(F32))
    turned = (hat * pack[0:1, :] + pack[1:2, :]).astype(BF16).T
    normed_t[...] = turned
    mix = dot_nt(wd[...], dy_here[step])
    c, s = cos[...], sin[...]
    for n in range(3):
        rows = slice(n * part, (n + 1) * part)
        joint = dot(w_t[rows, :], turned) + jnp.concatenate([jb[rows, :]] * (c.shape[1] // 128), axis=1)
        for h in range(heads):
            one = joint[h * size : (h + 1) * size]
            if n < 2:
                a, b = one[:HALF], one[HALF:RD]
                one = jnp.concatenate([a * c - b * s, b * c + a * s, one[RD:]], axis=0)
            if n == 0:
                one = one * size**-0.5
            qkv[n, h] = one.astype(BF16)
    for h in range(heads):
        mix_t[h] = mix[h * size : (h + 1) * size].astype(BF16)


def project(places, x_own, x_sib, dy_own, dy_sib, near, far, pack, joint_w, dense_w, cos, sin,
            heads, deps=()):
    tokens, features = x_own.shape
    tile = tokens // 2
    part = features // 2
    size = part // heads
    weight = lambda n: pl.BlockSpec((features, part), lambda g, p: (0, 2 * n + p[2]))
    lane = pl.BlockSpec((HALF, tile), lambda g, p: (0, g))
    return pl.pallas_call(
        after(project_kernel, 14, len(deps)),
        out_shape=(
            shaped((features, 2 * tokens), BF16),
            shaped((3, heads, size, 2 * tokens), BF16),
            shaped((heads, size, 2 * tokens), BF16),
        ),
        grid_spec=pltpu.PrefetchScalarGridSpec(
            num_scalar_prefetch=1,
            grid=(4,),
            in_specs=[ANYWHERE] * 6
            + [whole(pack.shape), weight(0), weight(1), weight(2),
               pl.BlockSpec((part, features), lambda g, p: (p[2], 0)), lane, lane]
            + [ANYWHERE] * len(deps),
            out_specs=(
                pl.BlockSpec((features, tile), lambda g, p: (0, g)),
                pl.BlockSpec((3, heads, size, tile), lambda g, p: (0, 0, 0, g)),
                pl.BlockSpec((heads, size, tile), lambda g, p: (0, 0, g)),
            ),
            scratch_shapes=[pltpu.VMEM((3 * part, features), BF16), pltpu.VMEM((3 * part, 128), F32),
                            pltpu.VMEM((4, tile, features), BF16), pltpu.VMEM((4, tile, features), BF16),
                            pltpu.SemaphoreType.DMA((2, 4))],
        ),
        cost_estimate=lasting(12),
        compiler_params=params(),
    )(places, x_own, x_sib, dy_own, dy_sib, near, far, pack,
      joint_w, joint_w, joint_w, dense_w, cos, sin, *deps)


def placing(bounds, segs, block, chunk, total):
    per_chunk = chunk // block
    tag = bounds[segs - 1]

    def place(b):
        k = (b // per_chunk) ^ tag
        slot = 2 * (k & 1) + (k >> 1)
        return pl.multiple_of(slot * chunk + (b % per_chunk) * block, block)

    def halved(offset):
        half = offset // (total // 2)
        return half, pl.ds(pl.multiple_of(offset - half * (total // 2), block), block)

    def first_of(position):
        start = jnp.int32(0)
        for m in range(segs - 1):
            start = jnp.where(bounds[m] <= position, bounds[m], start)
        return start

    def last_of(position):
        end = jnp.int32(total)
        for m in range(segs - 2, -1, -1):
            end = jnp.where(bounds[m] > position, bounds[m], end)
        return end - 1

    return place, halved, first_of, last_of


def sentence_rows(bounds, segs, pos):
    seg = jnp.zeros_like(pos)
    for m in range(segs - 1):
        seg = seg + (pos >= bounds[m]).astype(jnp.int32)
    rows = lax.broadcasted_iota(jnp.int32, (16, pos.shape[1]), 0)
    same = rows == seg
    onehot = jnp.where(same, 1.0, 0.0).astype(BF16)
    away = jnp.where(same | (rows >= segs), 0.0, NEGATIVE).astype(BF16)
    return onehot, away


def causal_bias(block):
    key = lax.broadcasted_iota(jnp.int32, (block, block), 0)
    query = lax.broadcasted_iota(jnp.int32, (block, block), 1)
    return jnp.where(key <= query, 0.0, NEGATIVE)


def staged(heads, *steps):
    for turn in range(len(heads) + len(steps) - 1):
        for number, step in enumerate(steps):
            if 0 <= turn - number < len(heads):
                step(heads[turn - number])


def in_runs(start, end, body, run=2):
    runs = (end - start) // run

    def several(n, _):
        body([start + n * run + r for r in range(run)])
        return 0

    def single(n, _):
        body([n])
        return 0

    lax.fori_loop(0, runs, several, 0)
    if run > 1:
        lax.fori_loop(start + runs * run, end, single, 0)


def attention_kernel(
    bounds, q, k, v, mix, pos, cos, sin, out_near, out_far, grad_near, grad_far,
    stats, qa, kn, vn, acc, top, low, dq, dk, dv, *, heads, block, chunk, segs,
):
    total = q.shape[-1]
    size = q.shape[2]
    place, halved, first_of, last_of = placing(bounds, segs, block, chunk, total)
    hs = range(heads)
    onehot, away = sentence_rows(bounds, segs, pos[...])
    for h in hs:
        qa[h, :size, :] = q[0, h]
        qa[h, size:, :] = away
        kn[h] = jnp.concatenate([k[0, h], onehot], axis=0).T
        vn[h] = v[0, h].T
    bias = causal_bias(block)

    def queries(i, _):
        half, lanes = halved(place(i))
        qs = pl.ds(place(i), block)
        s = [dot(kn[h, qs, :], qa[h, :, qs]) + bias for h in hs]
        m = [jnp.max(s[h], axis=0, keepdims=True) for h in hs]
        p = [jnp.exp(s[h] - m[h]) for h in hs]
        o = [dot(v[0, h, :, qs], p[h].astype(BF16)) for h in hs]
        l = [jnp.sum(p[h], axis=0, keepdims=True) for h in hs]
        for h in hs:
            top[h] = m[h]
            low[h] = l[h]
            acc[h] = o[h]

        def keys(blocks):
            parts = [pl.ds(place(j), block) for j in blocks]
            s, p, f = {}, {}, {}

            def score(h):
                s[h] = [dot(kn[h, ks, :], qa[h, :, qs]) for ks in parts]

            def soften(h):
                m_old = top[h]
                m = m_old
                for one in s[h]:
                    m = jnp.maximum(m, jnp.max(one, axis=0, keepdims=True))
                e = [jnp.exp(one - m) for one in s[h]]
                f[h] = jnp.exp(m_old - m)
                top[h] = m
                low[h] = low[h] * f[h] + sum(jnp.sum(one, axis=0, keepdims=True) for one in e)
                p[h] = [one.astype(BF16) for one in e]

            def gather(h):
                acc[h] = acc[h] * f[h] + sum(dot(v[0, h, :, ks], one) for ks, one in zip(parts, p[h]))

            staged(hs, score, soften, gather)

        in_runs(first_of(i * block) // block, i, keys)
        result = [acc[h] / low[h] for h in hs]
        for number, out in enumerate((out_near, out_far)):

            @pl.when(half == number)
            def _():
                for h in hs:
                    out[h, :, lanes] = result[h].astype(BF16)

        for h in hs:
            o = result[h]
            stats[h, 0:1, qs] = top[h] + jnp.log(low[h])
            stats[h, 1:2, qs] = jnp.sum(o * mix[h, :, qs].astype(F32), axis=0, keepdims=True)
        return 0

    lax.fori_loop(0, total // block, queries, 0)

    dq[...] = jnp.zeros_like(dq)

    def pairs(parts, ks, add, fresh):
        p, ds, s, dp = {}, {}, {}, {}

        def score(h):
            s[h] = [dot(kn[h, ks, :], qa[h, :, qs]) for qs in parts]
            dp[h] = [dot(vn[h, ks, :], mix[h, :, qs]) for qs in parts]

        def soften(h):
            p[h], ds[h] = [], []
            for qs, one, back in zip(parts, s[h], dp[h]):
                e = jnp.exp((one if add is None else one + add) - stats[h, 0:1, qs])
                p[h].append(e.astype(BF16))
                ds[h].append((e * (back - stats[h, 1:2, qs])).astype(BF16))

        def gather(h):
            a = sum(dot_nt(mix[h, :, qs], one) for qs, one in zip(parts, p[h]))
            b = sum(dot_nt(q[0, h, :, qs], one) for qs, one in zip(parts, ds[h]))
            dv[h] = a if fresh else dv[h] + a
            dk[h] = b if fresh else dk[h] + b
            for qs, one in zip(parts, ds[h]):
                dq[h, :, qs] += dot(k[0, h, :, ks], one)

        staged(hs, score, soften, gather)

    def turned_back(g, c, s):
        a, b = g[:HALF], g[HALF:RD]
        return jnp.concatenate([a * c + b * s, b * c - a * s, g[RD:]], axis=0).astype(BF16)

    def key_block(j, _):
        ks = pl.ds(place(j), block)
        pairs([ks], ks, bias, True)
        in_runs(
            j + 1,
            last_of((j + 1) * block - 1) // block + 1,
            lambda blocks: pairs([pl.ds(place(i), block) for i in blocks], ks, None, False),
            1,
        )
        half, lanes = halved(place(j))
        c, s = cos[:, ks], sin[:, ks]
        g = [(turned_back(dk[h], c, s), dv[h].astype(BF16)) for h in hs]
        for number, out in enumerate((grad_near, grad_far)):

            @pl.when(half == number)
            def _():
                for h in hs:
                    out[1, h, :, lanes] = g[h][0]
                    out[2, h, :, lanes] = g[h][1]

        return 0

    lax.fori_loop(0, total // block, key_block, 0)
    c, s = cos[...], sin[...]
    for h in hs:
        g = turned_back(dq[h] * size**-0.5, c, s)
        grad_near[0, h] = g[:, : total // 2]
        grad_far[0, h] = g[:, total // 2 :]


def attention(bounds, qkv, mix, pos, cos, sin, chunk, segs, deps=(), block=256):
    _, heads, size, total = qkv.shape
    part = lambda n: pl.BlockSpec(
        (1, heads, size, total), lambda g, b: (n, 0, 0, 0), pipeline_mode=pl.Buffered(1)
    )
    kernel = functools.partial(attention_kernel, heads=heads, block=block, chunk=chunk, segs=segs)
    mixed, grads = (heads, size, total // 2), (3, heads, size, total // 2)
    return pl.pallas_call(
        after(kernel, 8, len(deps)),
        out_shape=(shaped(mixed, BF16),) * 2 + (shaped(grads, BF16),) * 2,
        grid_spec=pltpu.PrefetchScalarGridSpec(
            num_scalar_prefetch=1,
            grid=(1,),
            in_specs=[part(0), part(1), part(2), whole((heads, size, total)), whole((1, total)),
                      whole((HALF, total)), whole((HALF, total))] + [ANYWHERE] * len(deps),
            out_specs=(whole(mixed),) * 2 + (whole(grads),) * 2,
            scratch_shapes=[
                pltpu.VMEM((heads, 2, total), F32),
                pltpu.VMEM((heads, size + 16, total), BF16),
                pltpu.VMEM((heads, total, size + 16), BF16),
                pltpu.VMEM((heads, total, size), BF16),
                pltpu.VMEM((heads, size, block), F32),
                pltpu.VMEM((heads, 1, block), F32),
                pltpu.VMEM((heads, 1, block), F32),
                pltpu.VMEM((heads, size, total), F32),
                pltpu.VMEM((heads, size, block), F32),
                pltpu.VMEM((heads, size, block), F32),
            ],
        ),
        cost_estimate=lasting(60),
        compiler_params=params(),
    )(bounds, qkv, qkv, qkv, mix, pos, cos, sin, *deps)


def joint_grads_kernel(
    places, normed_t, near, far, mixed, mixed_far, dy_own, dy_sib, dy_near, dy_far, going, staying, bias,
    nt, g, mx, dy, made, arrived, gone,
):
    part, tokens = mixed.shape
    tile = tokens // 2
    copy = pltpu.make_async_copy
    first = copy(normed_t, nt, arrived.at[3, 0])
    first.start()
    later = []
    for n in range(3):
        later.append([copy(near.at[n], g.at[n, 0], arrived.at[n, 0]), copy(far.at[n], g.at[n, 1], arrived.at[n, 1])])
    last = [copy(mixed, mx.at[0], arrived.at[3, 1]), copy(mixed_far, mx.at[1], arrived.at[3, 2])]
    pieces = row_pieces(places, dy_own, dy_sib, dy_near, dy_far, 1, tile)
    last += [copy(piece, dy.at[n], arrived.at[4, n]) for n, piece in enumerate(pieces)]
    later.append(last)
    for copies in later:
        for one in copies:
            one.start()
    first.wait()
    leaving = []
    for n in range(4):
        for one in later[n]:
            one.wait()
        for which, out in enumerate((going, staying)):
            half = pl.ds(pl.multiple_of(places[4 + which] * part, 128), part)
            if n < 3:
                value = dot_nt(nt[half, :tokens], g[n, 0]) + dot_nt(nt[half, tokens:], g[n, 1])
            else:
                value = (
                    dot(mx[0, :, :tile], dy[0, :, half]) + dot(mx[0, :, tile:], dy[1, :, half])
                    + dot(mx[1, :, :tile], dy[2, :, half]) + dot(mx[1, :, tile:], dy[3, :, half])
                )
            made[which, n] = value.astype(BF16)
            there = out.at[:, n * part : (n + 1) * part]
            leaving.append(copy(made.at[which, n], there, gone.at[which, n]))
            leaving[-1].start()
        if n < 3:
            total = None
            for half in range(2):
                for at in range(0, tokens, 128):
                    one = g[n, half, :, at : at + 128].astype(F32)
                    total = one if total is None else total + one
            bias[n] = jnp.sum(total.T, axis=0, keepdims=True)
    for one in leaving:
        one.wait()


def joint_grads(places, normed_t, grads, mixed, dy_own, dy_sib, near, far, deps=()):
    features, total = normed_t.shape
    part = features // 2
    tokens = total // 2
    return pl.pallas_call(
        after(joint_grads_kernel, 10, len(deps)),
        out_shape=(shaped((part, 4 * part), BF16),) * 2 + (shaped((3, 1, part), F32),),
        grid_spec=pltpu.PrefetchScalarGridSpec(
            num_scalar_prefetch=1,
            grid=(1,),
            in_specs=[ANYWHERE] * (9 + len(deps)),
            out_specs=(ANYWHERE, ANYWHERE, whole((3, 1, part))),
            scratch_shapes=[
                pltpu.VMEM((features, total), BF16), pltpu.VMEM((3, 2, part, tokens), BF16),
                pltpu.VMEM((2, part, tokens), BF16), pltpu.VMEM((4, tokens // 2, features), BF16),
                pltpu.VMEM((2, 4, part, part), BF16), pltpu.SemaphoreType.DMA((5, 4)),
                pltpu.SemaphoreType.DMA((2, 4)),
            ],
        ),
        cost_estimate=lasting(11),
        compiler_params=params(),
    )(places, normed_t, grads[0], grads[1], mixed[0], mixed[1], dy_own, dy_sib, near, far, *deps)


def norm_back_of(grad, x, gain):
    hat, inverse = norm_stats(x)
    scaled = grad * gain
    dx = inverse * (
        scaled
        - jnp.mean(scaled, axis=-1, keepdims=True)
        - hat * jnp.mean(scaled * hat, axis=-1, keepdims=True)
    )
    return dx, jnp.sum(grad * hat, axis=0, keepdims=True), jnp.sum(grad, axis=0, keepdims=True)


def norm_back_kernel(places, own, sib, w, x, x_near, pack, dx_own, dx_far, gain_grad, bias_grad, x_here):
    step = pl.program_id(0)
    part = own.shape[1]
    core = places[2]

    @pl.when(step == 0)
    def _():
        x_here[...] = x_near[0]

    @pl.when(step == 1)
    def _():
        x_here[...] = x[...]

    total = None
    for n in range(3):
        mine = pl.ds(pl.multiple_of((2 * n + core) * part, 128), part)
        other = pl.ds(pl.multiple_of((2 * n + 1 - core) * part, 128), part)
        one = dot(w[:, mine], own[n]) + dot(w[:, other], sib[n])
        total = one if n == 0 else total + one
    dx, g, b = norm_back_of(total.T, x_here[...].astype(F32), pack[0:1, :])

    @pl.when(step == 0)
    def _():
        dx_far[...] = dx.astype(BF16)
        gain_grad[...] = g
        bias_grad[...] = b

    @pl.when(step == 1)
    def _():
        dx_own[...] = dx
        gain_grad[...] += g
        bias_grad[...] += b


def norm_back(places, own, sib, w, x, near, pack, deps=()):
    part = own.shape[1]
    tokens, features = x.shape
    tile = tokens // 2
    piece = pl.BlockSpec((3, part, tile), lambda g, p: (0, 0, 1 - g))
    return pl.pallas_call(
        after(norm_back_kernel, 7, len(deps)),
        out_shape=(shaped((tile, features), F32), shaped((tile, features), BF16),
                   shaped((1, features), F32), shaped((1, features), F32)),
        grid_spec=pltpu.PrefetchScalarGridSpec(
            num_scalar_prefetch=1,
            grid=(2,),
            in_specs=[piece, piece, whole(w.shape),
                      pl.BlockSpec((tile, features), lambda g, p: (p[3], 0)),
                      pl.BlockSpec((1, tile, features), lambda g, p: (0, 0, 0)),
                      whole(pack.shape)] + [ANYWHERE] * len(deps),
            out_specs=(whole((tile, features)), whole((tile, features)),
                       whole((1, features)), whole((1, features))),
            scratch_shapes=[pltpu.VMEM((tile, features), BF16)],
        ),
        cost_estimate=lasting(12),
        compiler_params=params(),
    )(places, own, sib, w, x, near, pack, *deps)


def products_kernel(places, act_a, act_b, hid_a, hid_b, wc_a, wc_b, we_a, we_b, out, back):
    out[...] = (dot(act_a[...], wc_a[...]) + dot(act_b[...], wc_b[...])).astype(out.dtype)
    back[...] = (dot_nt(hid_a[...], we_a[...]) + dot_nt(hid_b[...], we_b[...])).astype(back.dtype)


def products(places, sent, kept, wc, we, sibling, deps=()):
    tokens, units = sent[1].shape[0] // 2, sent[1].shape[1]
    features = wc.shape[1]
    tile = tokens // 2
    token = pl.BlockSpec((tile, units), lambda g, p: (2 * int(sibling) + g, 0))
    row = lambda n: pl.BlockSpec((units, features), lambda g, p: (p[n], 0))
    column = lambda n: pl.BlockSpec((features, units), lambda g, p: (0, p[n]))
    spec = pl.BlockSpec((tile, features), lambda g, p: (g, 0))
    return pl.pallas_call(
        after(products_kernel, 9, len(deps)),
        out_shape=(shaped((tokens, features), BF16 if sibling else F32),) * 2,
        grid_spec=pltpu.PrefetchScalarGridSpec(
            num_scalar_prefetch=1,
            grid=(2,),
            in_specs=[token] * 4 + [row(0), row(1), column(0), column(1)] + [ANYWHERE] * len(deps),
            out_specs=(spec, spec),
        ),
        cost_estimate=lasting(10),
        compiler_params=params(),
    )(places, sent[1], kept[1], sent[2], kept[2], wc, wc, we, we, *deps)


def block_out_kernel(places, x, out, out_sib, mixed, mixed_sib, mixed_near, wd, pack, block_out):
    step = pl.program_id(0)
    part, tile = mixed.shape[0], x.shape[0]
    core = places[2]
    mine = pl.ds(pl.multiple_of(core * part, 128), part)
    other = pl.ds(pl.multiple_of((1 - core) * part, 128), part)

    def finish(ours, siblings):
        attn = dot(ours.T, wd[mine, :]) + dot(siblings.T, wd[other, :])
        feed = out[...] + out_sib[...].astype(F32)
        block_out[...] = (x[...].astype(F32) + attn + feed + pack[4:5, :]).astype(BF16)

    @pl.when(step == 0)
    def _():
        finish(mixed[:, :tile], mixed_sib[:, :tile])

    @pl.when(step == 1)
    def _():
        finish(mixed_near[:part, :], mixed_near[part:, :])


def block_result(places, x, out, out_sib, mixed, mixed_sib, mixed_near, wd, pack, deps=()):
    tokens, features = out.shape
    tile = tokens // 2
    part = features // 2
    token = pl.BlockSpec((tile, features), lambda g, p: (p[3] ^ g, 0))
    return pl.pallas_call(
        after(block_out_kernel, 9, len(deps)),
        out_shape=shaped((tokens, features), BF16),
        grid_spec=pltpu.PrefetchScalarGridSpec(
            num_scalar_prefetch=1,
            grid=(2,),
            in_specs=[token] * 3 + [whole((part, tokens)), whole((part, tokens)), whole((features, tile)),
                      whole((features, features)), whole(pack.shape)] + [ANYWHERE] * len(deps),
            out_specs=token,
        ),
        cost_estimate=lasting(8),
        compiler_params=params(),
    )(places, x, out, out_sib, mixed, mixed_sib, mixed_near, wd, pack, *deps)


def input_grad_kernel(
    places, x, dy, back, back_sib, dx_own, dx_near, pack, gain_attn, bias_attn, out_bias, be_sent, be_kept,
    joint_b, input_grad, small, gain_sum, bias_sum,
):
    step = pl.program_id(0)
    features = x.shape[1]
    dx_feed, g, b = norm_back_of(
        back[...] + back_sib[...].astype(F32), x[...].astype(F32), pack[2:3, :]
    )

    @pl.when(step == 0)
    def _():
        input_grad[...] = (dy[...].astype(F32) + dx_own[...] + dx_feed).astype(BF16)
        gain_sum[...] = g
        bias_sum[...] = b

    @pl.when(step == 1)
    def _():
        input_grad[...] = (dy[...].astype(F32) + dx_near[...].astype(F32) + dx_feed).astype(BF16)
        small[...] = jnp.zeros_like(small)
        small[0:1, :features] = gain_attn[...]
        small[0:1, features:] = bias_attn[...]
        small[1:2, :features] = gain_sum[...] + g
        small[1:2, features:] = bias_sum[...] + b
        small[2:3, :features] = out_bias[...]
        first = places[5] == 0
        small[2:3, features:] = jnp.where(first, be_kept[...], be_sent[...])
        small[3:4, :features] = jnp.where(first, be_sent[...], be_kept[...])
        half = features // 2
        small[3:4, features : features + half] = joint_b[0]
        small[3:4, features + half :] = joint_b[1]
        small[4:5, :half] = joint_b[2]


def input_result(places, x, dy, back, back_sib, dx_own, dx_near, pack, sums, joint_b, deps=()):
    tokens, features = x.shape
    tile = tokens // 2
    token = pl.BlockSpec((tile, features), lambda g, p: (p[3] ^ g, 0))
    return pl.pallas_call(
        after(input_grad_kernel, 14, len(deps)),
        out_shape=(shaped((tokens, features), BF16), shaped((8, 2 * features), F32)),
        grid_spec=pltpu.PrefetchScalarGridSpec(
            num_scalar_prefetch=1,
            grid=(2,),
            in_specs=[token] * 4 + [whole((tile, features))] * 2 + [whole(pack.shape)]
            + [whole((1, features))] * 5 + [whole(joint_b.shape)] + [ANYWHERE] * len(deps),
            out_specs=(token, whole((8, 2 * features))),
            scratch_shapes=[pltpu.VMEM((1, features), F32), pltpu.VMEM((1, features), F32)],
        ),
        cost_estimate=lasting(8),
        compiler_params=params(),
    )(places, x, dy, back, back_sib, dx_own, dx_near, pack, *sums, joint_b, *deps)


class Links:
    def __init__(self, row_count, x_together=False):
        self.row_count = row_count
        self.row_bits = row_count.bit_length() - 1
        rest = range(2, self.row_bits)
        if x_together:
            self.orders = ([0, 1, "x", *rest], [1, 0, "x", *rest])
        else:
            dims = [0, 1, "x", *rest]
            other = list(dims)
            for n in range(0, len(dims) - 1, 2):
                other[n], other[n + 1] = other[n + 1], other[n]
            self.orders = (dims, other)
        dims = self.orders[0]
        self.rounds = len(dims)
        self.groups = [(n,) for n in range(self.rounds)]

    def bit(self, number, sibling=False):
        def of(dim):
            if dim == "x":
                return lax.axis_index("x")
            return (lax.axis_index("rows") >> dim) & 1

        return jnp.where(
            lax.axis_index("core") == int(sibling), of(self.orders[0][number]), of(self.orders[1][number])
        )

    def swap(self, array, *numbers):
        pairs = []
        for row in range(self.row_count):
            for x in range(2):
                for core in range(2):
                    there = [row, x]
                    for number in numbers:
                        dim = self.orders[core][number]
                        if dim == "x":
                            there[1] = 1 - there[1]
                        else:
                            there[0] ^= 1 << dim
                    pairs.append(((row * 2 + x) * 2 + core, (there[0] * 2 + there[1]) * 2 + core))
        return lax.ppermute(array, CHIP, pairs)

    def others(self, group):
        return [group] if len(group) == 1 else [group[1:], group[:1], group]

    def swap_group(self, arrays, group):
        return [self.swap(array, *numbers) for array, numbers in zip(arrays, self.others(group))]


def swap_core(array):
    return lax.ppermute(array, "core", [(0, 1), (1, 0)])


def swap_x(array):
    return lax.ppermute(array, "x", [(0, 1), (1, 0)])


def add(a, b):
    return (a.astype(F32) + b.astype(F32)).astype(BF16)


def total_of(terms):
    total = terms[0].astype(F32)
    for term in terms[1:]:
        total = total + term.astype(F32)
    return total.astype(BF16)


def divide_kernel(place, *refs, terms, pieces):
    for n in range(pieces):
        refs[terms * pieces + n][...] = total_of([refs[t * pieces + n][...] for t in range(terms)])


def divide(bits, terms, deps=()):
    place = bits[0] if len(bits) == 1 else bits[0] * 2 + bits[1]
    pieces = 2 ** len(bits)
    rows, width = terms[0].shape
    rows = rows // pieces
    if rows % 16:
        return [
            total_of([lax.dynamic_slice_in_dim(t, (place ^ n) * rows, rows, 0) for t in terms])
            for n in range(pieces)
        ]
    tile = min(rows, 384)
    steps = rows // tile
    source = lambda n: pl.BlockSpec((tile, width), lambda t, p: ((p[0] ^ n) * steps + t, 0))
    kernel = functools.partial(divide_kernel, terms=len(terms), pieces=pieces)
    return pl.pallas_call(
        after(kernel, 1 + len(terms) * pieces, len(deps)),
        out_shape=(shaped((rows, width), BF16),) * pieces,
        grid_spec=pltpu.PrefetchScalarGridSpec(
            num_scalar_prefetch=1,
            grid=(steps,),
            in_specs=[source(n) for n in range(pieces)] * len(terms) + [ANYWHERE] * len(deps),
            out_specs=(pl.BlockSpec((tile, width), lambda t, p: (t, 0)),) * pieces,
        ),
        cost_estimate=lasting(1),
        compiler_params=params(),
    )(place.astype(jnp.int32).reshape(1), *[t for t in terms for _ in range(pieces)], *deps)


def in_order(bits, pieces):
    if len(pieces) == 2:
        mine, other = pieces
        forward, back = jnp.concatenate([mine, other], axis=0), jnp.concatenate([other, mine], axis=0)
        return jnp.where(bits[-1] == 0, forward, back)
    low, high = in_order(bits[1:], pieces[:2]), in_order(bits[1:], pieces[2:])
    return in_order(bits[:1], [low, high])


def two_parts(vector):
    high = lax.reduce_precision(vector, 8, 7)
    low = lax.reduce_precision(vector - high, 8, 7)
    return jnp.concatenate([high, low], axis=0).astype(BF16), high + low


def one_part(pair):
    rows = pair.shape[0] // 2
    return pair[:rows].astype(F32) + pair[rows:].astype(F32)


def spread_kernel(*refs, parts):
    contract, expand = refs[2 * parts :]
    rows = contract.shape[0] // parts
    for q in range(parts):
        contract[q * rows : (q + 1) * rows, :] = refs[q][...].astype(F32)
        expand[q * rows : (q + 1) * rows, :] = refs[parts + q][...].astype(F32)


def spread(gathered, links, features, units, deps=()):
    piece = features >> (links.rounds - 2)
    parts = features // piece

    def rank(core, half, which, quarter):
        def one(order):
            place = 0
            bits = {order[0]: half, order[1]: which}
            for n, dim in enumerate(order[2:]):
                bits[dim] = (quarter >> (links.rounds - 3 - n)) & 1
            for dim, value in bits.items():
                place = place + (value * 2 if dim == "x" else value * (4 << dim))
            return place

        return jnp.where(core == 0, one(links.orders[0]), one(links.orders[1])) + core

    source = lambda which, q: pl.BlockSpec((piece, features), lambda c, h: (rank(c, h, which, q), 0))
    return pl.pallas_call(
        after(functools.partial(spread_kernel, parts=parts), 2 * parts, len(deps)),
        out_shape=(shaped((4 * units, features), F32), shaped((features, 4 * units), F32)),
        grid=(2, 2),
        in_specs=[source(which, q) for which in range(2) for q in range(parts)] + [ANYWHERE] * len(deps),
        out_specs=(
            pl.BlockSpec((features, features), lambda c, h: (c * 2 + h, 0)),
            pl.BlockSpec((features, features), lambda c, h: (0, c * 2 + h)),
        ),
        cost_estimate=lasting(12),
        compiler_params=params(),
    )(*[gathered] * (2 * parts), *deps)


def spread_joint_kernel(places, own, sib, *refs, which, offset):
    joint, dense, wide, arrived = refs[-4:]
    count, part = own.shape[0], own.shape[1] // 4
    copies = []
    for g, ref in enumerate((own, sib)):
        core = places[2] ^ g
        half = pl.multiple_of(places[4 + 2 * g + which] * part, part)
        for n in range(4):
            wide[g, n] = ref[:, n * part : (n + 1) * part].astype(F32)
            if n < 3:
                columns = pl.ds(pl.multiple_of((2 * n + core) * part, part), part)
                there = joint.at[pl.ds(pl.multiple_of(half + offset, 8), count), columns]
            else:
                rows = pl.ds(pl.multiple_of(core * part + offset, 8), count)
                there = dense.at[rows, pl.ds(half, part)]
            copies.append(pltpu.make_async_copy(wide.at[g, n], there, arrived.at[g, n]))
            copies[-1].start()
    for copy in copies:
        copy.wait()


def spread_joint(places, own, sib, features, which, into=(), offset=0):
    part = features // 2
    return pl.pallas_call(
        functools.partial(spread_joint_kernel, which=which, offset=offset),
        out_shape=(shaped((features, 3 * features), F32), shaped((features, features), F32)),
        grid_spec=pltpu.PrefetchScalarGridSpec(
            num_scalar_prefetch=1,
            grid=(1,),
            in_specs=[whole(own.shape), whole(sib.shape)] + [ANYWHERE] * len(into),
            out_specs=(ANYWHERE, ANYWHERE),
            scratch_shapes=[
                pltpu.VMEM((2, 4, own.shape[0], part), F32), pltpu.SemaphoreType.DMA((2, 4)),
            ],
        ),
        input_output_aliases={3: 0, 4: 1} if into else {},
        cost_estimate=lasting(3),
        compiler_params=params(),
    )(places, own, sib, *into)


def per_device(
    links, joint_links, block_in, lengths, attn_gain, attn_bias, feed_gain, feed_bias, joint_weight, joint_bias,
    dense_weight, dense_bias, expand_weight, expand_bias, contract_weight, contract_bias, out_cotangent,
):
    rows_here, chunk, features = block_in.shape
    tokens = rows_here * chunk
    total = 2 * tokens
    segs = lengths.shape[1]
    heads = H // 2
    part = features // 2
    units = expand_weight.shape[1] // 4
    x_at, core_at = lax.axis_index("x"), lax.axis_index("core")
    chunk_at = x_at * 2 + core_at

    x_own, dy_own = block_in.reshape(tokens, features), out_cotangent.reshape(tokens, features)
    x_sib, dy_sib = swap_core(x_own), swap_core(dy_own)
    away = jnp.stack([
        lax.dynamic_index_in_dim(block_in, 1 - x_at, 0, keepdims=False),
        lax.dynamic_index_in_dim(out_cotangent, 1 - x_at, 0, keepdims=False),
    ])
    near = swap_x(away)

    mine = lax.dynamic_index_in_dim(lengths, x_at, 0, keepdims=False)
    before = jnp.tril(jnp.ones((segs, segs), jnp.int32))
    bounds = jnp.sum(before * mine[None, :], axis=1)
    bounds = jnp.where(jnp.arange(segs) == segs - 1, chunk_at, bounds).astype(jnp.int32)
    slots = jnp.arange(4, dtype=jnp.int32)
    starts = (((slots & 1) * 2 + (slots >> 1)) ^ chunk_at) * chunk
    pos = (starts[:, None] + jnp.arange(chunk, dtype=jnp.int32)[None, :]).reshape(1, total)
    inverse = BASE_FREQ ** (-2.0 * jnp.arange(HALF).astype(F32) / RD)
    angles = inverse[:, None] * pos.astype(F32)
    cos, sin = jnp.cos(angles), jnp.sin(angles)

    pack = jnp.concatenate([
        attn_gain, attn_bias, feed_gain, feed_bias, dense_bias + contract_bias, expand_bias, joint_bias,
    ]).reshape(-1, features)
    pack = jnp.pad(pack, ((0, 16 - pack.shape[0]), (0, 0)))

    bits = [links.bit(n) for n in range(links.rounds)]
    of = lambda group: [bits[n] for n in group]
    sib_bit = links.bit(0, True)
    places = jnp.stack(
        [core_at * 2 + 1 - bits[0], core_at * 2 + bits[0], core_at, x_at, 1 - bits[0], bits[0],
         1 - sib_bit, sib_bit]
    ).astype(jnp.int32)

    joint_bit, joint_sib_bit = joint_links.bit(0), joint_links.bit(0, True)
    joint_places = jnp.concatenate([
        places[:4], jnp.stack([1 - joint_bit, joint_bit, 1 - joint_sib_bit, joint_sib_bit]).astype(jnp.int32),
    ])

    def feed(number, x, deps):
        base = (places[number] * (units // 256)).reshape(1)
        return feed_part(base, x, dy_own, dy_sib, pack, expand_weight, contract_weight, units, deps)

    sent = feed(0, (x_own, x_sib), (away,))
    arrived = links.swap(sent[0], 0)
    kept = feed(1, sent[5:], (sent[0],))
    near = once(near, (kept[0],))
    far = swap_core(near)

    flat = lambda a: a.reshape(2 * units, features)
    first, second, *rest = links.groups
    stay, outgoing = divide(of(second), [flat(kept[0]), flat(arrived)])
    terms = [stay, links.swap(outgoing, *second)]
    normed_t, qkv, mix_t = project(
        places, x_own, x_sib, dy_own, dy_sib, near, far, pack, joint_weight, dense_weight, cos, sin,
        heads, (outgoing,),
    )
    ready = normed_t
    for number, group in enumerate(rest):
        stay, *outgoing = divide(of(group), terms, (ready,))
        terms = [stay, *links.swap_group(outgoing, group)]
        ready = stay
        if number == 0:
            out_sib, back_sib = products(places, sent, kept, contract_weight, expand_weight, True, (stay,))
            ready = out_sib
    out_own, back_own = products(places, sent, kept, contract_weight, expand_weight, False, (stay,))
    out_sib, back_sib = swap_core(out_sib), swap_core(back_sib)
    terms[-1] = once(terms[-1], (out_own,))
    last = total_of(terms)
    gathered = lax.all_gather(last, CHIP, axis=0, tiled=True)
    mixed_own, mixed_far, *grads = attention(bounds, qkv, mix_t, pos, cos, sin, chunk, segs, (last,))
    mixed_own, mixed_far = mixed_own.reshape(part, tokens), mixed_far.reshape(part, tokens)
    grads = [g.reshape(3, part, tokens) for g in grads]
    bits = [joint_links.bit(n) for n in range(joint_links.rounds)]
    grads_sib = swap_core(grads[1])
    mixed = (mixed_own, mixed_far)
    outgoing, current, joint_b = joint_grads(
        joint_places, normed_t, grads, mixed, dy_own, dy_sib, near, far
    )
    arrived = joint_links.swap(outgoing, *first)
    mixed_sib = swap_core(once(mixed_far, (grads[0],)))
    mixed_near = swap_x(jnp.concatenate([mixed_own[:, chunk:], mixed_sib[:, chunk:]], axis=0))
    dx_own, dx_far, gain_attn, bias_attn = norm_back(
        places, grads[0], grads_sib, joint_weight, x_own, near, pack, (current,)
    )
    dx_near = swap_x(dx_far)
    stay, outgoing = divide(of(second), [current, arrived], (dx_own,))
    terms = [stay, joint_links.swap(outgoing, *second)]
    block_out = block_result(
        places, x_own, out_own, out_sib, mixed_own, mixed_sib, mixed_near, dense_weight, pack, (stay,)
    )
    ready = block_out
    for number, group in enumerate(rest):
        stay, *outgoing = divide(of(group), terms, (ready,))
        terms = [stay, *joint_links.swap_group(outgoing, group)]
        ready = stay
        if number == 0:
            grad_contract_w, grad_expand_w = spread(gathered, links, features, units, (stay,))
            ready = grad_contract_w
    input_grad, small = input_result(
        places, x_own, dy_own, back_own, back_sib, dx_own, dx_near, pack,
        (gain_attn, bias_attn, sent[4], sent[3], kept[3]), joint_b, (ready,),
    )
    terms[-1] = once(terms[-1], (input_grad,))
    current = total_of(terms)

    shared = 5 * features

    def summed(group, small):
        pair, small = two_parts(small)
        outgoing = jnp.concatenate([current, pair], axis=0)
        rows_now = current.shape[0]
        arrived = [joint_links.swap(outgoing, *numbers) for numbers in joint_links.others(group)]
        parts = [small] + [one_part(array[rows_now:]) for array in arrived]
        while len(parts) > 1:
            parts = [a + b for a, b in zip(parts[::2], parts[1::2])]
        return in_order(of(group), [current] + [array[:rows_now] for array in arrived]), parts[0]

    for group in reversed(rest):
        current, small = summed(group, small)
    pair, small = two_parts(small)
    rows_now = current.shape[0]
    outgoing = jnp.concatenate([current, pair], axis=0)
    arrived = joint_links.swap(outgoing, *second)
    one, both = joint_links.swap(pair, *first), joint_links.swap(pair, *first, *second)
    small = (small + one_part(arrived[rows_now:])) + (one_part(one) + one_part(both))
    current = in_order(of(second), [current, arrived[:rows_now]])
    arrived = joint_links.swap(current, *first)
    sib_current = swap_core(current)
    pair, small = two_parts(small)
    small_sib = one_part(swap_core(pair)).reshape(-1)
    small = small.reshape(-1)
    sums = (small + small_sib)[:shared].reshape(5, features)
    ordered = lambda a, b: jnp.where(core_at == 0, jnp.stack([a, b]), jnp.stack([b, a]))
    single = ordered(small[shared:], small_sib[shared:])
    grad_expand_b = single[:, : 2 * units].reshape(-1)
    grad_joint_b = single[:, 2 * units : 2 * units + 3 * part].reshape(2, 3, part).transpose(1, 0, 2).reshape(-1)
    into = spread_joint(joint_places, current, sib_current, features, 1)
    arrived = once(arrived, (into[0], sums, grad_joint_b, grad_expand_b))
    grad_joint_w, grad_dense_w = spread_joint(
        joint_places, arrived, swap_core(arrived), features, 0, into
    )
    return (
        block_out.reshape(block_in.shape),
        input_grad.reshape(block_in.shape),
        sums[0],
        sums[1],
        sums[2],
        sums[3],
        grad_joint_w,
        grad_joint_b,
        grad_dense_w,
        sums[4],
        grad_expand_w,
        grad_expand_b,
        grad_contract_w,
        sums[4],
    )


def solution(mesh):
    row_count, seq_count = mesh.devices.shape
    chips = Mesh(mesh.devices.reshape(row_count, seq_count // 2, 2), CHIP)
    links = Links(row_count)
    tokens = P("rows", ("x", "core"), None)
    in_specs = (tokens, P("rows", None)) + (P(),) * 12 + (tokens,)
    out_specs = (tokens, tokens) + (P(),) * 12
    return jax.shard_map(
        functools.partial(per_device, links, Links(row_count, True)), mesh=chips, in_specs=in_specs, out_specs=out_specs,
        check_vma=False,
    )
```

```python
import functools

import jax
import jax.numpy as jnp
from jax import lax
from jax.experimental import pallas as pl
from jax.experimental.pallas import tpu as pltpu
from jax.sharding import Mesh, PartitionSpec as P

H = 12
RD = 16
HALF = RD // 2
EPSILON = 1e-05
BASE_FREQ = 10000.0
NEGATIVE = -1e30
F32 = jnp.float32
BF16 = jnp.bfloat16
VMEM_BYTES = 63 * 2**20
CHIP = ("rows", "x", "core")
NT = (((1,), (1,)), ((), ()))


def dot(a, b):
    return jnp.dot(a, b, preferred_element_type=F32)


def dot_nt(a, b):
    return lax.dot_general(a, b, NT, preferred_element_type=F32)


def params():
    return pltpu.CompilerParams(vmem_limit_bytes=VMEM_BYTES)


def lasting(microseconds):
    return pl.CostEstimate(flops=int(microseconds * 1e9), bytes_accessed=0, transcendentals=0)


def whole(shape):
    return pl.BlockSpec(shape, lambda *_: (0,) * len(shape))


def shaped(shape, dtype):
    return jax.ShapeDtypeStruct(shape, dtype)


def after(kernel, inputs, deps):
    return lambda *refs: kernel(*refs[:inputs], *refs[inputs + deps :])


ANYWHERE = pl.BlockSpec(memory_space=pl.ANY)


def once(array, deps):
    return pl.pallas_call(
        lambda *refs: None,
        out_shape=shaped(array.shape, array.dtype),
        in_specs=[ANYWHERE] * (1 + len(deps)),
        out_specs=ANYWHERE,
        input_output_aliases={0: 0},
        cost_estimate=lasting(0.1),
    )(array, *deps)


def norm_stats(x):
    centered = x - jnp.mean(x, axis=-1, keepdims=True)
    spread = jnp.mean(centered * centered, axis=-1, keepdims=True)
    inverse = lax.rsqrt(spread + EPSILON)
    return centered * inverse, inverse


def gelu_both(h):
    e = jnp.exp2(h * h * (-0.5 * 1.4426950408889634))
    t = pl.reciprocal(1.0 + jnp.abs(h) * (0.3275911 * 0.7071067811865476), approx=False)
    poly = t * (
        0.5 * 0.254829592
        + t * (0.5 * -0.284496736 + t * (0.5 * 1.421413741 + t * (0.5 * -1.453152027 + t * (0.5 * 1.061405429))))
    )
    tail = poly * e
    phi = jnp.where(h >= 0.0, 1.0 - tail, tail)
    return h * phi, phi + h * e * 0.3989422804014327


def feed_kernel(
    base, x_own, x_sib, dy_own, dy_sib, pack, we, wc,
    grads, act, hid, be_grad, out_bias, normed, nf, act_t, hid_t, x_here, dy_here, gone, arrived,
):
    tokens, features = dy_own.shape
    copy = pltpu.make_async_copy(nf, normed, gone)

    @pl.when(pl.program_id(0) == 0)
    def _():
        tile = 256
        sources = (x_own, x_sib, dy_own, dy_sib)
        places = (x_here.at[0], x_here.at[1], dy_here.at[0], dy_here.at[1])
        copies = [
            pltpu.make_async_copy(a, b, arrived.at[n]) for n, (a, b) in enumerate(zip(sources, places))
        ]
        for one in copies:
            one.start()
        for half in range(2):
            copies[half].wait()

            def norm(i, _):
                here = pl.ds(pl.multiple_of(i * tile, tile), tile)
                there = pl.ds(pl.multiple_of(half * tokens + i * tile, tile), tile)
                hat, _ = norm_stats(x_here[half, here, :].astype(F32))
                nf[there, :] = (hat * pack[2:3, :] + pack[3:4, :]).astype(BF16)
                return 0

            lax.fori_loop(0, tokens // tile, norm, 0)
        copy.start()
        copies[2].wait()
        copies[3].wait()

        def add_up(i, total):
            here = pl.ds(pl.multiple_of(i * tile, tile), tile)
            return total + jnp.sum(dy_here[0, here, :].astype(F32), axis=0, keepdims=True)

        out_bias[...] = lax.fori_loop(0, tokens // tile, add_up, jnp.zeros((1, features), F32))

    feed_tile(base, nf, dy_here.at[0], dy_here.at[1], pack, we, wc, grads, act, hid, be_grad, act_t, hid_t)

    @pl.when(pl.program_id(0) == pl.num_programs(0) - 1)
    def _():
        copy.wait()


def feed_tile(base, nf, dy_own, dy_sib, pack, we, wc, grads, act, hid, be_grad, act_t, hid_t):
    step = pl.program_id(0)
    tokens, features = dy_own.shape
    width = we.shape[1]
    first = (base[0] + step) * width
    be = pack[
        pl.ds(5 + first // features, 1), pl.ds(pl.multiple_of(first % features, width), width)
    ]
    tile = 512
    per = tokens // tile
    count = 2 * per
    hidden, back = [None] * count, [None] * count

    def finish(n):
        value, slope = gelu_both(hidden[n])
        rows = slice(n * tile, (n + 1) * tile)
        value, slope = value.astype(BF16), (back[n] * slope).astype(BF16)
        act[rows, :] = value
        hid[rows, :] = slope
        act_t[:, rows] = value.T
        hid_t[:, rows] = slope.T

    for n in range(count):
        dy_ref = dy_own if n < per else dy_sib
        hidden[n] = dot(nf[n * tile : (n + 1) * tile, :], we[...]) + be
        back[n] = dot_nt(dy_ref[(n % per) * tile : (n % per + 1) * tile, :], wc[...])
        if n > 0:
            finish(n - 1)
    finish(count - 1)
    there = pl.ds(pl.multiple_of(step * width, width), width)
    grads[0, there, :] = (
        dot(act_t[:, :tokens], dy_own[...]) + dot(act_t[:, tokens:], dy_sib[...])
    ).astype(BF16)
    grads[1, :, there] = dot(hid_t[...], nf[...]).T.astype(BF16)
    be_grad[...] = jnp.sum(hid[...].astype(F32), axis=0, keepdims=True)


def feed_part(base, x, dy_own, dy_sib, pack, we, wc, units, deps=()):
    tokens, features = dy_own.shape
    width = 256
    prepared = len(x) == 1
    token = pl.BlockSpec((2 * tokens, width), lambda t, b: (0, t))
    out_shape = (
        shaped((2, units, features), BF16), shaped((2 * tokens, units), BF16),
        shaped((2 * tokens, units), BF16), shaped((1, units), F32),
    )
    out_specs = (whole((2, units, features)), token, token, pl.BlockSpec((1, width), lambda t, b: (0, t)))
    scratch = [pltpu.VMEM((width, 2 * tokens), BF16), pltpu.VMEM((width, 2 * tokens), BF16)]
    if not prepared:
        out_shape += (shaped((1, features), F32), shaped((2 * tokens, features), BF16))
        out_specs += (whole((1, features)), ANYWHERE)
        both = pltpu.VMEM((2, tokens, features), BF16)
        scratch = [pltpu.VMEM((2 * tokens, features), BF16), *scratch, both, both,
                   pltpu.SemaphoreType.DMA, pltpu.SemaphoreType.DMA((4,))]
    return pl.pallas_call(
        after(feed_tile if prepared else feed_kernel, 6 + len(x), len(deps)),
        out_shape=out_shape,
        grid_spec=pltpu.PrefetchScalarGridSpec(
            num_scalar_prefetch=1,
            grid=(units // width,),
            in_specs=([whole(a.shape) for a in (*x, dy_own, dy_sib)] if prepared else [ANYWHERE] * 4)
            + [
                whole(pack.shape),
                pl.BlockSpec((features, width), lambda t, b: (0, b[0] + t)),
                pl.BlockSpec((width, features), lambda t, b: (b[0] + t, 0)),
            ]
            + [ANYWHERE] * len(deps),
            out_specs=out_specs,
            scratch_shapes=scratch,
        ),
        cost_estimate=lasting(22),
        compiler_params=params(),
    )(base, *x, dy_own, dy_sib, pack, we, wc, *deps)


def row_pieces(places, own, sib, near, far, number, tile):
    rows = pl.ds(pl.multiple_of(places[3] * tile, tile), tile)
    return own.at[rows], near.at[number], sib.at[rows], far.at[number]


def project_kernel(
    places, x_own, x_sib, dy_own, dy_sib, near, far, pack, wq, wk, wv, wd,
    cos, sin, normed_t, qkv, mix_t, w_t, jb, x_here, dy_here, arrived,
):
    step = pl.program_id(0)
    part = wq.shape[1]
    heads, size = qkv.shape[1], qkv.shape[2]
    tile = x_here.shape[1]
    copies = [
        [pltpu.make_async_copy(piece, there.at[n], arrived.at[which, n]) for n, piece in enumerate(pieces)]
        for which, (there, pieces) in enumerate((
            (x_here, row_pieces(places, x_own, x_sib, near, far, 0, tile)),
            (dy_here, row_pieces(places, dy_own, dy_sib, near, far, 1, tile)),
        ))
    ]

    @pl.when(step == 0)
    def _():
        for pair in zip(*copies):
            for copy in pair:
                copy.start()
        lanes = pl.ds(pl.multiple_of(places[2] * part, 128), part)
        for n, w in enumerate((wq, wk, wv)):
            rows = slice(n * part, (n + 1) * part)
            w_t[rows, :] = w[...].T
            jb[rows, :] = jnp.broadcast_to(pack[9 + n : 10 + n, lanes], (128, part)).T

    for number in range(4):

        @pl.when(step == number)
        def _():
            copies[0][number].wait()
            copies[1][number].wait()

    hat, _ = norm_stats(x_here[step].astype(F32))
    turned = (hat * pack[0:1, :] + pack[1:2, :]).astype(BF16).T
    normed_t[...] = turned
    mix = dot_nt(wd[...], dy_here[step])
    c, s = cos[...], sin[...]
    for n in range(3):
        rows = slice(n * part, (n + 1) * part)
        joint = dot(w_t[rows, :], turned) + jnp.concatenate([jb[rows, :]] * (c.shape[1] // 128), axis=1)
        for h in range(heads):
            one = joint[h * size : (h + 1) * size]
            if n < 2:
                a, b = one[:HALF], one[HALF:RD]
                one = jnp.concatenate([a * c - b * s, b * c + a * s, one[RD:]], axis=0)
            if n == 0:
                one = one * size**-0.5
            qkv[n, h] = one.astype(BF16)
    for h in range(heads):
        mix_t[h] = mix[h * size : (h + 1) * size].astype(BF16)


def project(places, x_own, x_sib, dy_own, dy_sib, near, far, pack, joint_w, dense_w, cos, sin,
            heads, deps=()):
    tokens, features = x_own.shape
    tile = tokens // 2
    part = features // 2
    size = part // heads
    weight = lambda n: pl.BlockSpec((features, part), lambda g, p: (0, 2 * n + p[2]))
    lane = pl.BlockSpec((HALF, tile), lambda g, p: (0, g))
    return pl.pallas_call(
        after(project_kernel, 14, len(deps)),
        out_shape=(
            shaped((features, 2 * tokens), BF16),
            shaped((3, heads, size, 2 * tokens), BF16),
            shaped((heads, size, 2 * tokens), BF16),
        ),
        grid_spec=pltpu.PrefetchScalarGridSpec(
            num_scalar_prefetch=1,
            grid=(4,),
            in_specs=[ANYWHERE] * 6
            + [whole(pack.shape), weight(0), weight(1), weight(2),
               pl.BlockSpec((part, features), lambda g, p: (p[2], 0)), lane, lane]
            + [ANYWHERE] * len(deps),
            out_specs=(
                pl.BlockSpec((features, tile), lambda g, p: (0, g)),
                pl.BlockSpec((3, heads, size, tile), lambda g, p: (0, 0, 0, g)),
                pl.BlockSpec((heads, size, tile), lambda g, p: (0, 0, g)),
            ),
            scratch_shapes=[pltpu.VMEM((3 * part, features), BF16), pltpu.VMEM((3 * part, 128), F32),
                            pltpu.VMEM((4, tile, features), BF16), pltpu.VMEM((4, tile, features), BF16),
                            pltpu.SemaphoreType.DMA((2, 4))],
        ),
        cost_estimate=lasting(12),
        compiler_params=params(),
    )(places, x_own, x_sib, dy_own, dy_sib, near, far, pack,
      joint_w, joint_w, joint_w, dense_w, cos, sin, *deps)


def placing(bounds, segs, block, chunk, total):
    per_chunk = chunk // block
    tag = bounds[segs - 1]

    def place(b):
        k = (b // per_chunk) ^ tag
        slot = 2 * (k & 1) + (k >> 1)
        return pl.multiple_of(slot * chunk + (b % per_chunk) * block, block)

    def halved(offset):
        half = offset // (total // 2)
        return half, pl.ds(pl.multiple_of(offset - half * (total // 2), block), block)

    def first_of(position):
        start = jnp.int32(0)
        for m in range(segs - 1):
            start = jnp.where(bounds[m] <= position, bounds[m], start)
        return start

    def last_of(position):
        end = jnp.int32(total)
        for m in range(segs - 2, -1, -1):
            end = jnp.where(bounds[m] > position, bounds[m], end)
        return end - 1

    return place, halved, first_of, last_of


def sentence_rows(bounds, segs, pos):
    seg = jnp.zeros_like(pos)
    for m in range(segs - 1):
        seg = seg + (pos >= bounds[m]).astype(jnp.int32)
    rows = lax.broadcasted_iota(jnp.int32, (16, pos.shape[1]), 0)
    same = rows == seg
    onehot = jnp.where(same, 1.0, 0.0).astype(BF16)
    away = jnp.where(same | (rows >= segs), 0.0, NEGATIVE).astype(BF16)
    return onehot, away


def causal_bias(block):
    key = lax.broadcasted_iota(jnp.int32, (block, block), 0)
    query = lax.broadcasted_iota(jnp.int32, (block, block), 1)
    return jnp.where(key <= query, 0.0, NEGATIVE)


def staged(heads, *steps):
    for turn in range(len(heads) + len(steps) - 1):
        for number, step in enumerate(steps):
            if 0 <= turn - number < len(heads):
                step(heads[turn - number])


def in_runs(start, end, body, run=2):
    runs = (end - start) // run

    def several(n, _):
        body([start + n * run + r for r in range(run)])
        return 0

    def single(n, _):
        body([n])
        return 0

    lax.fori_loop(0, runs, several, 0)
    if run > 1:
        lax.fori_loop(start + runs * run, end, single, 0)


def attention_kernel(
    bounds, qkv, mix_hbm, pos, cos, sin, out_near, out_far, grad_near, grad_far,
    here, mix, mixed, grads, stats, qa, kn, vn, acc, top, low, dq, dk, dv, came, gone, left,
    *, heads, block, chunk, segs,
):
    total = mix.shape[-1]
    size = mix.shape[1]
    place, halved, first_of, last_of = placing(bounds, segs, block, chunk, total)
    hs = range(heads)
    copy = pltpu.make_async_copy
    loads = [copy(qkv.at[n], here.at[n], came.at[n]) for n in range(3)] + [copy(mix_hbm, mix, came.at[3])]
    for n in (1, 0, 2, 3):
        loads[n].start()
    q, k, v = (here.at[pl.ds(n, 1)] for n in range(3))
    onehot, away = sentence_rows(bounds, segs, pos[...])
    loads[1].wait()
    for h in hs:
        kn[h] = jnp.concatenate([k[0, h], onehot], axis=0).T
    loads[0].wait()
    for h in hs:
        qa[h, :size, :] = q[0, h]
        qa[h, size:, :] = away
    loads[2].wait()
    for h in hs:
        vn[h] = v[0, h].T
    loads[3].wait()
    bias = causal_bias(block)

    def queries(i, _):
        half, lanes = halved(place(i))
        qs = pl.ds(place(i), block)
        s = [dot(kn[h, qs, :], qa[h, :, qs]) + bias for h in hs]
        m = [jnp.max(s[h], axis=0, keepdims=True) for h in hs]
        p = [jnp.exp(s[h] - m[h]) for h in hs]
        o = [dot(v[0, h, :, qs], p[h].astype(BF16)) for h in hs]
        l = [jnp.sum(p[h], axis=0, keepdims=True) for h in hs]
        for h in hs:
            top[h] = m[h]
            low[h] = l[h]
            acc[h] = o[h]

        def keys(blocks):
            parts = [pl.ds(place(j), block) for j in blocks]
            s, p, f = {}, {}, {}

            def score(h):
                s[h] = [dot(kn[h, ks, :], qa[h, :, qs]) for ks in parts]

            def soften(h):
                m_old = top[h]
                m = m_old
                for one in s[h]:
                    m = jnp.maximum(m, jnp.max(one, axis=0, keepdims=True))
                e = [jnp.exp(one - m) for one in s[h]]
                f[h] = jnp.exp(m_old - m)
                top[h] = m
                low[h] = low[h] * f[h] + sum(jnp.sum(one, axis=0, keepdims=True) for one in e)
                p[h] = [one.astype(BF16) for one in e]

            def gather(h):
                acc[h] = acc[h] * f[h] + sum(dot(v[0, h, :, ks], one) for ks, one in zip(parts, p[h]))

            staged(hs, score, soften, gather)

        in_runs(first_of(i * block) // block, i, keys)
        result = [acc[h] / low[h] for h in hs]
        for h in hs:
            mixed[half, h, :, lanes] = result[h].astype(BF16)
        for h in hs:
            o = result[h]
            stats[h, 0:1, qs] = top[h] + jnp.log(low[h])
            stats[h, 1:2, qs] = jnp.sum(o * mix[h, :, qs].astype(F32), axis=0, keepdims=True)
        return 0

    lax.fori_loop(0, total // block, queries, 0)

    early = [copy(mixed.at[n], out, left.at[n]) for n, out in enumerate((out_near, out_far))]
    for one in early:
        one.start()
    dq[...] = jnp.zeros_like(dq)

    def pairs(parts, ks, add, fresh):
        p, ds, s, dp = {}, {}, {}, {}

        def score(h):
            s[h] = [dot(kn[h, ks, :], qa[h, :, qs]) for qs in parts]
            dp[h] = [dot(vn[h, ks, :], mix[h, :, qs]) for qs in parts]

        def soften(h):
            p[h], ds[h] = [], []
            for qs, one, back in zip(parts, s[h], dp[h]):
                e = jnp.exp((one if add is None else one + add) - stats[h, 0:1, qs])
                p[h].append(e.astype(BF16))
                ds[h].append((e * (back - stats[h, 1:2, qs])).astype(BF16))

        def gather(h):
            a = sum(dot_nt(mix[h, :, qs], one) for qs, one in zip(parts, p[h]))
            b = sum(dot_nt(q[0, h, :, qs], one) for qs, one in zip(parts, ds[h]))
            dv[h] = a if fresh else dv[h] + a
            dk[h] = b if fresh else dk[h] + b
            for qs, one in zip(parts, ds[h]):
                dq[h, :, qs] += dot(k[0, h, :, ks], one)

        staged(hs, score, soften, gather)

    def turned_back(g, c, s):
        a, b = g[:HALF], g[HALF:RD]
        return jnp.concatenate([a * c + b * s, b * c - a * s, g[RD:]], axis=0).astype(BF16)

    def key_block(j, _):
        ks = pl.ds(place(j), block)
        pairs([ks], ks, bias, True)
        in_runs(
            j + 1,
            last_of((j + 1) * block - 1) // block + 1,
            lambda blocks: pairs([pl.ds(place(i), block) for i in blocks], ks, None, False),
            1,
        )
        half, lanes = halved(place(j))
        c, s = cos[:, ks], sin[:, ks]
        g = [(turned_back(dk[h], c, s), dv[h].astype(BF16)) for h in hs]
        for h in hs:
            grads[half, 1, h, :, lanes] = g[h][0]
            grads[half, 2, h, :, lanes] = g[h][1]
        for number, out in enumerate((grad_near, grad_far)):

            @pl.when(half == number)
            def _():
                copy(grads.at[number, 1:, :, :, lanes], out.at[1:, :, :, lanes], gone.at[j]).start()

        return 0

    lax.fori_loop(0, total // block, key_block, 0)
    c, s = cos[...], sin[...]
    for h in hs:
        g = turned_back(dq[h] * size**-0.5, c, s)
        grads[0, 0, h] = g[:, : total // 2]
        grads[1, 0, h] = g[:, total // 2 :]
    last = [copy(grads.at[n, 0], out.at[0], left.at[2 + n]) for n, out in enumerate((grad_near, grad_far))]
    for one in last:
        one.start()
    for j in range(total // block):
        copy(grads.at[0, 1:, :, :, :block], grad_near.at[1:, :, :, :block], gone.at[j]).wait()
    for one in early + last:
        one.wait()


def attention(bounds, qkv, mix, pos, cos, sin, chunk, segs, deps=(), block=256):
    _, heads, size, total = qkv.shape
    kernel = functools.partial(attention_kernel, heads=heads, block=block, chunk=chunk, segs=segs)
    mixed, grads = (heads, size, total // 2), (3, heads, size, total // 2)
    return pl.pallas_call(
        after(kernel, 6, len(deps)),
        out_shape=(shaped(mixed, BF16),) * 2 + (shaped(grads, BF16),) * 2,
        grid_spec=pltpu.PrefetchScalarGridSpec(
            num_scalar_prefetch=1,
            grid=(1,),
            in_specs=[ANYWHERE, ANYWHERE, whole((1, total)),
                      whole((HALF, total)), whole((HALF, total))] + [ANYWHERE] * len(deps),
            out_specs=(ANYWHERE,) * 4,
            scratch_shapes=[
                pltpu.VMEM((3, heads, size, total), BF16),
                pltpu.VMEM((heads, size, total), BF16),
                pltpu.VMEM((2, *mixed), BF16),
                pltpu.VMEM((2, *grads), BF16),
                pltpu.VMEM((heads, 2, total), F32),
                pltpu.VMEM((heads, size + 16, total), BF16),
                pltpu.VMEM((heads, total, size + 16), BF16),
                pltpu.VMEM((heads, total, size), BF16),
                pltpu.VMEM((heads, size, block), F32),
                pltpu.VMEM((heads, 1, block), F32),
                pltpu.VMEM((heads, 1, block), F32),
                pltpu.VMEM((heads, size, total), F32),
                pltpu.VMEM((heads, size, block), F32),
                pltpu.VMEM((heads, size, block), F32),
                pltpu.SemaphoreType.DMA((4,)),
                pltpu.SemaphoreType.DMA((total // block,)),
                pltpu.SemaphoreType.DMA((4,)),
            ],
        ),
        cost_estimate=lasting(60),
        compiler_params=params(),
    )(bounds, qkv, mix, pos, cos, sin, *deps)


def joint_grads_kernel(
    places, normed_t, near, far, mixed, mixed_far, dy_own, dy_sib, dy_near, dy_far, going, staying, bias,
    nt, g, mx, dy, made, arrived, gone,
):
    part, tokens = mixed.shape
    tile = tokens // 2
    copy = pltpu.make_async_copy
    first = copy(normed_t, nt, arrived.at[3, 0])
    first.start()
    later = []
    for n in range(3):
        later.append([copy(near.at[n], g.at[n, 0], arrived.at[n, 0]), copy(far.at[n], g.at[n, 1], arrived.at[n, 1])])
    last = [copy(mixed, mx.at[0], arrived.at[3, 1]), copy(mixed_far, mx.at[1], arrived.at[3, 2])]
    pieces = row_pieces(places, dy_own, dy_sib, dy_near, dy_far, 1, tile)
    last += [copy(piece, dy.at[n], arrived.at[4, n]) for n, piece in enumerate(pieces)]
    later.append(last)
    for copies in later:
        for one in copies:
            one.start()
    first.wait()
    leaving = []
    for n in range(4):
        for one in later[n]:
            one.wait()
        for which, out in enumerate((going, staying)):
            half = pl.ds(pl.multiple_of(places[4 + which] * part, 128), part)
            if n < 3:
                value = dot_nt(nt[half, :tokens], g[n, 0]) + dot_nt(nt[half, tokens:], g[n, 1])
            else:
                value = (
                    dot(mx[0, :, :tile], dy[0, :, half]) + dot(mx[0, :, tile:], dy[1, :, half])
                    + dot(mx[1, :, :tile], dy[2, :, half]) + dot(mx[1, :, tile:], dy[3, :, half])
                )
            made[which, n] = value.astype(BF16)
            there = out.at[:, n * part : (n + 1) * part]
            leaving.append(copy(made.at[which, n], there, gone.at[which, n]))
            leaving[-1].start()
        if n < 3:
            total = None
            for half in range(2):
                for at in range(0, tokens, 128):
                    one = g[n, half, :, at : at + 128].astype(F32)
                    total = one if total is None else total + one
            bias[n] = jnp.sum(total.T, axis=0, keepdims=True)
    for one in leaving:
        one.wait()


def joint_grads(places, normed_t, grads, mixed, dy_own, dy_sib, near, far, deps=()):
    features, total = normed_t.shape
    part = features // 2
    tokens = total // 2
    return pl.pallas_call(
        after(joint_grads_kernel, 10, len(deps)),
        out_shape=(shaped((part, 4 * part), BF16),) * 2 + (shaped((3, 1, part), F32),),
        grid_spec=pltpu.PrefetchScalarGridSpec(
            num_scalar_prefetch=1,
            grid=(1,),
            in_specs=[ANYWHERE] * (9 + len(deps)),
            out_specs=(ANYWHERE, ANYWHERE, whole((3, 1, part))),
            scratch_shapes=[
                pltpu.VMEM((features, total), BF16), pltpu.VMEM((3, 2, part, tokens), BF16),
                pltpu.VMEM((2, part, tokens), BF16), pltpu.VMEM((4, tokens // 2, features), BF16),
                pltpu.VMEM((2, 4, part, part), BF16), pltpu.SemaphoreType.DMA((5, 4)),
                pltpu.SemaphoreType.DMA((2, 4)),
            ],
        ),
        cost_estimate=lasting(11),
        compiler_params=params(),
    )(places, normed_t, grads[0], grads[1], mixed[0], mixed[1], dy_own, dy_sib, near, far, *deps)


def norm_back_of(grad, x, gain):
    hat, inverse = norm_stats(x)
    scaled = grad * gain
    dx = inverse * (
        scaled
        - jnp.mean(scaled, axis=-1, keepdims=True)
        - hat * jnp.mean(scaled * hat, axis=-1, keepdims=True)
    )
    return dx, jnp.sum(grad * hat, axis=0, keepdims=True), jnp.sum(grad, axis=0, keepdims=True)


def norm_back_kernel(places, own, sib, w, x, x_near, pack, dx_own, dx_far, gain_grad, bias_grad, x_here):
    step = pl.program_id(0)
    part = own.shape[1]
    core = places[2]

    @pl.when(step == 0)
    def _():
        x_here[...] = x_near[0]

    @pl.when(step == 1)
    def _():
        x_here[...] = x[...]

    total = None
    for n in range(3):
        mine = pl.ds(pl.multiple_of((2 * n + core) * part, 128), part)
        other = pl.ds(pl.multiple_of((2 * n + 1 - core) * part, 128), part)
        one = dot(w[:, mine], own[n]) + dot(w[:, other], sib[n])
        total = one if n == 0 else total + one
    dx, g, b = norm_back_of(total.T, x_here[...].astype(F32), pack[0:1, :])

    @pl.when(step == 0)
    def _():
        dx_far[...] = dx.astype(BF16)
        gain_grad[...] = g
        bias_grad[...] = b

    @pl.when(step == 1)
    def _():
        dx_own[...] = dx
        gain_grad[...] += g
        bias_grad[...] += b


def norm_back(places, own, sib, w, x, near, pack, deps=()):
    part = own.shape[1]
    tokens, features = x.shape
    tile = tokens // 2
    piece = pl.BlockSpec((3, part, tile), lambda g, p: (0, 0, 1 - g))
    return pl.pallas_call(
        after(norm_back_kernel, 7, len(deps)),
        out_shape=(shaped((tile, features), F32), shaped((tile, features), BF16),
                   shaped((1, features), F32), shaped((1, features), F32)),
        grid_spec=pltpu.PrefetchScalarGridSpec(
            num_scalar_prefetch=1,
            grid=(2,),
            in_specs=[piece, piece, whole(w.shape),
                      pl.BlockSpec((tile, features), lambda g, p: (p[3], 0)),
                      pl.BlockSpec((1, tile, features), lambda g, p: (0, 0, 0)),
                      whole(pack.shape)] + [ANYWHERE] * len(deps),
            out_specs=(whole((tile, features)), whole((tile, features)),
                       whole((1, features)), whole((1, features))),
            scratch_shapes=[pltpu.VMEM((tile, features), BF16)],
        ),
        cost_estimate=lasting(12),
        compiler_params=params(),
    )(places, own, sib, w, x, near, pack, *deps)


def products_kernel(places, act_a, act_b, hid_a, hid_b, wc_a, wc_b, we_a, we_b, out, back):
    out[...] = (dot(act_a[...], wc_a[...]) + dot(act_b[...], wc_b[...])).astype(out.dtype)
    back[...] = (dot_nt(hid_a[...], we_a[...]) + dot_nt(hid_b[...], we_b[...])).astype(back.dtype)


def products(places, sent, kept, wc, we, sibling, deps=()):
    tokens, units = sent[1].shape[0] // 2, sent[1].shape[1]
    features = wc.shape[1]
    tile = tokens // 2
    token = pl.BlockSpec((tile, units), lambda g, p: (2 * int(sibling) + g, 0))
    row = lambda n: pl.BlockSpec((units, features), lambda g, p: (p[n], 0))
    column = lambda n: pl.BlockSpec((features, units), lambda g, p: (0, p[n]))
    spec = pl.BlockSpec((tile, features), lambda g, p: (g, 0))
    return pl.pallas_call(
        after(products_kernel, 9, len(deps)),
        out_shape=(shaped((tokens, features), BF16 if sibling else F32),) * 2,
        grid_spec=pltpu.PrefetchScalarGridSpec(
            num_scalar_prefetch=1,
            grid=(2,),
            in_specs=[token] * 4 + [row(0), row(1), column(0), column(1)] + [ANYWHERE] * len(deps),
            out_specs=(spec, spec),
        ),
        cost_estimate=lasting(10),
        compiler_params=params(),
    )(places, sent[1], kept[1], sent[2], kept[2], wc, wc, we, we, *deps)


def block_out_kernel(places, x, out, out_sib, mixed, mixed_sib, mixed_near, wd, pack, block_out):
    step = pl.program_id(0)
    part, tile = mixed.shape[0], x.shape[0]
    core = places[2]
    mine = pl.ds(pl.multiple_of(core * part, 128), part)
    other = pl.ds(pl.multiple_of((1 - core) * part, 128), part)

    def finish(ours, siblings):
        attn = dot(ours.T, wd[mine, :]) + dot(siblings.T, wd[other, :])
        feed = out[...] + out_sib[...].astype(F32)
        block_out[...] = (x[...].astype(F32) + attn + feed + pack[4:5, :]).astype(BF16)

    @pl.when(step == 0)
    def _():
        finish(mixed[:, :tile], mixed_sib[:, :tile])

    @pl.when(step == 1)
    def _():
        finish(mixed_near[:part, :], mixed_near[part:, :])


def block_result(places, x, out, out_sib, mixed, mixed_sib, mixed_near, wd, pack, deps=()):
    tokens, features = out.shape
    tile = tokens // 2
    part = features // 2
    token = pl.BlockSpec((tile, features), lambda g, p: (p[3] ^ g, 0))
    return pl.pallas_call(
        after(block_out_kernel, 9, len(deps)),
        out_shape=shaped((tokens, features), BF16),
        grid_spec=pltpu.PrefetchScalarGridSpec(
            num_scalar_prefetch=1,
            grid=(2,),
            in_specs=[token] * 3 + [whole((part, tokens)), whole((part, tokens)), whole((features, tile)),
                      whole((features, features)), whole(pack.shape)] + [ANYWHERE] * len(deps),
            out_specs=token,
        ),
        cost_estimate=lasting(8),
        compiler_params=params(),
    )(places, x, out, out_sib, mixed, mixed_sib, mixed_near, wd, pack, *deps)


def input_grad_kernel(
    places, x, dy, back, back_sib, dx_own, dx_near, pack, gain_attn, bias_attn, out_bias, be_sent, be_kept,
    joint_b, input_grad, small, gain_sum, bias_sum,
):
    step = pl.program_id(0)
    features = x.shape[1]
    dx_feed, g, b = norm_back_of(
        back[...] + back_sib[...].astype(F32), x[...].astype(F32), pack[2:3, :]
    )

    @pl.when(step == 0)
    def _():
        input_grad[...] = (dy[...].astype(F32) + dx_own[...] + dx_feed).astype(BF16)
        gain_sum[...] = g
        bias_sum[...] = b

    @pl.when(step == 1)
    def _():
        input_grad[...] = (dy[...].astype(F32) + dx_near[...].astype(F32) + dx_feed).astype(BF16)
        small[...] = jnp.zeros_like(small)
        small[0:1, :features] = gain_attn[...]
        small[0:1, features:] = bias_attn[...]
        small[1:2, :features] = gain_sum[...] + g
        small[1:2, features:] = bias_sum[...] + b
        small[2:3, :features] = out_bias[...]
        first = places[5] == 0
        small[2:3, features:] = jnp.where(first, be_kept[...], be_sent[...])
        small[3:4, :features] = jnp.where(first, be_sent[...], be_kept[...])
        half = features // 2
        small[3:4, features : features + half] = joint_b[0]
        small[3:4, features + half :] = joint_b[1]
        small[4:5, :half] = joint_b[2]


def input_result(places, x, dy, back, back_sib, dx_own, dx_near, pack, sums, joint_b, deps=()):
    tokens, features = x.shape
    tile = tokens // 2
    token = pl.BlockSpec((tile, features), lambda g, p: (p[3] ^ g, 0))
    return pl.pallas_call(
        after(input_grad_kernel, 14, len(deps)),
        out_shape=(shaped((tokens, features), BF16), shaped((8, 2 * features), F32)),
        grid_spec=pltpu.PrefetchScalarGridSpec(
            num_scalar_prefetch=1,
            grid=(2,),
            in_specs=[token] * 4 + [whole((tile, features))] * 2 + [whole(pack.shape)]
            + [whole((1, features))] * 5 + [whole(joint_b.shape)] + [ANYWHERE] * len(deps),
            out_specs=(token, whole((8, 2 * features))),
            scratch_shapes=[pltpu.VMEM((1, features), F32), pltpu.VMEM((1, features), F32)],
        ),
        cost_estimate=lasting(8),
        compiler_params=params(),
    )(places, x, dy, back, back_sib, dx_own, dx_near, pack, *sums, joint_b, *deps)


class Links:
    def __init__(self, row_count, x_together=False):
        self.row_count = row_count
        self.row_bits = row_count.bit_length() - 1
        rest = range(2, self.row_bits)
        if x_together:
            self.orders = ([0, 1, "x", *rest], [1, 0, "x", *rest])
        else:
            dims = [0, 1, "x", *rest]
            other = list(dims)
            for n in range(0, len(dims) - 1, 2):
                other[n], other[n + 1] = other[n + 1], other[n]
            self.orders = (dims, other)
        dims = self.orders[0]
        self.rounds = len(dims)
        self.groups = [(n,) for n in range(self.rounds)]

    def bit(self, number, sibling=False):
        def of(dim):
            if dim == "x":
                return lax.axis_index("x")
            return (lax.axis_index("rows") >> dim) & 1

        return jnp.where(
            lax.axis_index("core") == int(sibling), of(self.orders[0][number]), of(self.orders[1][number])
        )

    def swap(self, array, *numbers):
        pairs = []
        for row in range(self.row_count):
            for x in range(2):
                for core in range(2):
                    there = [row, x]
                    for number in numbers:
                        dim = self.orders[core][number]
                        if dim == "x":
                            there[1] = 1 - there[1]
                        else:
                            there[0] ^= 1 << dim
                    pairs.append(((row * 2 + x) * 2 + core, (there[0] * 2 + there[1]) * 2 + core))
        return lax.ppermute(array, CHIP, pairs)

    def others(self, group):
        return [group] if len(group) == 1 else [group[1:], group[:1], group]

    def swap_group(self, arrays, group):
        return [self.swap(array, *numbers) for array, numbers in zip(arrays, self.others(group))]


def swap_core(array):
    return lax.ppermute(array, "core", [(0, 1), (1, 0)])


def swap_x(array):
    return lax.ppermute(array, "x", [(0, 1), (1, 0)])


def add(a, b):
    return (a.astype(F32) + b.astype(F32)).astype(BF16)


def total_of(terms):
    total = terms[0].astype(F32)
    for term in terms[1:]:
        total = total + term.astype(F32)
    return total.astype(BF16)


def divide_kernel(place, *refs, terms, pieces):
    for n in range(pieces):
        refs[terms * pieces + n][...] = total_of([refs[t * pieces + n][...] for t in range(terms)])


def divide(bits, terms, deps=()):
    place = bits[0] if len(bits) == 1 else bits[0] * 2 + bits[1]
    pieces = 2 ** len(bits)
    rows, width = terms[0].shape
    rows = rows // pieces
    if rows % 16:
        return [
            total_of([lax.dynamic_slice_in_dim(t, (place ^ n) * rows, rows, 0) for t in terms])
            for n in range(pieces)
        ]
    tile = min(rows, 384)
    steps = rows // tile
    source = lambda n: pl.BlockSpec((tile, width), lambda t, p: ((p[0] ^ n) * steps + t, 0))
    kernel = functools.partial(divide_kernel, terms=len(terms), pieces=pieces)
    return pl.pallas_call(
        after(kernel, 1 + len(terms) * pieces, len(deps)),
        out_shape=(shaped((rows, width), BF16),) * pieces,
        grid_spec=pltpu.PrefetchScalarGridSpec(
            num_scalar_prefetch=1,
            grid=(steps,),
            in_specs=[source(n) for n in range(pieces)] * len(terms) + [ANYWHERE] * len(deps),
            out_specs=(pl.BlockSpec((tile, width), lambda t, p: (t, 0)),) * pieces,
        ),
        cost_estimate=lasting(1),
        compiler_params=params(),
    )(place.astype(jnp.int32).reshape(1), *[t for t in terms for _ in range(pieces)], *deps)


def in_order(bits, pieces):
    if len(pieces) == 2:
        mine, other = pieces
        forward, back = jnp.concatenate([mine, other], axis=0), jnp.concatenate([other, mine], axis=0)
        return jnp.where(bits[-1] == 0, forward, back)
    low, high = in_order(bits[1:], pieces[:2]), in_order(bits[1:], pieces[2:])
    return in_order(bits[:1], [low, high])


def two_parts(vector):
    high = lax.reduce_precision(vector, 8, 7)
    low = lax.reduce_precision(vector - high, 8, 7)
    return jnp.concatenate([high, low], axis=0).astype(BF16), high + low


def one_part(pair):
    rows = pair.shape[0] // 2
    return pair[:rows].astype(F32) + pair[rows:].astype(F32)


def spread_kernel(*refs, parts):
    contract, expand = refs[2 * parts :]
    rows = contract.shape[0] // parts
    for q in range(parts):
        contract[q * rows : (q + 1) * rows, :] = refs[q][...].astype(F32)
        expand[q * rows : (q + 1) * rows, :] = refs[parts + q][...].astype(F32)


def spread(gathered, links, features, units, deps=()):
    piece = features >> (links.rounds - 2)
    parts = features // piece

    def rank(core, half, which, quarter):
        def one(order):
            place = 0
            bits = {order[0]: half, order[1]: which}
            for n, dim in enumerate(order[2:]):
                bits[dim] = (quarter >> (links.rounds - 3 - n)) & 1
            for dim, value in bits.items():
                place = place + (value * 2 if dim == "x" else value * (4 << dim))
            return place

        return jnp.where(core == 0, one(links.orders[0]), one(links.orders[1])) + core

    source = lambda which, q: pl.BlockSpec((piece, features), lambda c, h: (rank(c, h, which, q), 0))
    return pl.pallas_call(
        after(functools.partial(spread_kernel, parts=parts), 2 * parts, len(deps)),
        out_shape=(shaped((4 * units, features), F32), shaped((features, 4 * units), F32)),
        grid=(2, 2),
        in_specs=[source(which, q) for which in range(2) for q in range(parts)] + [ANYWHERE] * len(deps),
        out_specs=(
            pl.BlockSpec((features, features), lambda c, h: (c * 2 + h, 0)),
            pl.BlockSpec((features, features), lambda c, h: (0, c * 2 + h)),
        ),
        cost_estimate=lasting(12),
        compiler_params=params(),
    )(*[gathered] * (2 * parts), *deps)


def spread_joint_kernel(places, own, sib, *refs, which, offset):
    joint, dense, wide, arrived = refs[-4:]
    count, part = own.shape[0], own.shape[1] // 4
    copies = []
    for g, ref in enumerate((own, sib)):
        core = places[2] ^ g
        half = pl.multiple_of(places[4 + 2 * g + which] * part, part)
        for n in range(4):
            wide[g, n] = ref[:, n * part : (n + 1) * part].astype(F32)
            if n < 3:
                columns = pl.ds(pl.multiple_of((2 * n + core) * part, part), part)
                there = joint.at[pl.ds(pl.multiple_of(half + offset, 8), count), columns]
            else:
                rows = pl.ds(pl.multiple_of(core * part + offset, 8), count)
                there = dense.at[rows, pl.ds(half, part)]
            copies.append(pltpu.make_async_copy(wide.at[g, n], there, arrived.at[g, n]))
            copies[-1].start()
    for copy in copies:
        copy.wait()


def spread_joint(places, own, sib, features, which, into=(), offset=0):
    part = features // 2
    return pl.pallas_call(
        functools.partial(spread_joint_kernel, which=which, offset=offset),
        out_shape=(shaped((features, 3 * features), F32), shaped((features, features), F32)),
        grid_spec=pltpu.PrefetchScalarGridSpec(
            num_scalar_prefetch=1,
            grid=(1,),
            in_specs=[whole(own.shape), whole(sib.shape)] + [ANYWHERE] * len(into),
            out_specs=(ANYWHERE, ANYWHERE),
            scratch_shapes=[
                pltpu.VMEM((2, 4, own.shape[0], part), F32), pltpu.SemaphoreType.DMA((2, 4)),
            ],
        ),
        input_output_aliases={3: 0, 4: 1} if into else {},
        cost_estimate=lasting(3),
        compiler_params=params(),
    )(places, own, sib, *into)


def per_device(
    links, joint_links, block_in, lengths, attn_gain, attn_bias, feed_gain, feed_bias, joint_weight, joint_bias,
    dense_weight, dense_bias, expand_weight, expand_bias, contract_weight, contract_bias, out_cotangent,
):
    rows_here, chunk, features = block_in.shape
    tokens = rows_here * chunk
    total = 2 * tokens
    segs = lengths.shape[1]
    heads = H // 2
    part = features // 2
    units = expand_weight.shape[1] // 4
    x_at, core_at = lax.axis_index("x"), lax.axis_index("core")
    chunk_at = x_at * 2 + core_at

    x_own, dy_own = block_in.reshape(tokens, features), out_cotangent.reshape(tokens, features)
    x_sib, dy_sib = swap_core(x_own), swap_core(dy_own)
    away = jnp.stack([
        lax.dynamic_index_in_dim(block_in, 1 - x_at, 0, keepdims=False),
        lax.dynamic_index_in_dim(out_cotangent, 1 - x_at, 0, keepdims=False),
    ])
    near = swap_x(away)

    mine = lax.dynamic_index_in_dim(lengths, x_at, 0, keepdims=False)
    before = jnp.tril(jnp.ones((segs, segs), jnp.int32))
    bounds = jnp.sum(before * mine[None, :], axis=1)
    bounds = jnp.where(jnp.arange(segs) == segs - 1, chunk_at, bounds).astype(jnp.int32)
    slots = jnp.arange(4, dtype=jnp.int32)
    starts = (((slots & 1) * 2 + (slots >> 1)) ^ chunk_at) * chunk
    pos = (starts[:, None] + jnp.arange(chunk, dtype=jnp.int32)[None, :]).reshape(1, total)
    inverse = BASE_FREQ ** (-2.0 * jnp.arange(HALF).astype(F32) / RD)
    angles = inverse[:, None] * pos.astype(F32)
    cos, sin = jnp.cos(angles), jnp.sin(angles)

    pack = jnp.concatenate([
        attn_gain, attn_bias, feed_gain, feed_bias, dense_bias + contract_bias, expand_bias, joint_bias,
    ]).reshape(-1, features)
    pack = jnp.pad(pack, ((0, 16 - pack.shape[0]), (0, 0)))

    bits = [links.bit(n) for n in range(links.rounds)]
    of = lambda group: [bits[n] for n in group]
    sib_bit = links.bit(0, True)
    places = jnp.stack(
        [core_at * 2 + 1 - bits[0], core_at * 2 + bits[0], core_at, x_at, 1 - bits[0], bits[0],
         1 - sib_bit, sib_bit]
    ).astype(jnp.int32)

    joint_bit, joint_sib_bit = joint_links.bit(0), joint_links.bit(0, True)
    joint_places = jnp.concatenate([
        places[:4], jnp.stack([1 - joint_bit, joint_bit, 1 - joint_sib_bit, joint_sib_bit]).astype(jnp.int32),
    ])

    def feed(number, x, deps):
        base = (places[number] * (units // 256)).reshape(1)
        return feed_part(base, x, dy_own, dy_sib, pack, expand_weight, contract_weight, units, deps)

    sent = feed(0, (x_own, x_sib), (away,))
    arrived = links.swap(sent[0], 0)
    kept = feed(1, sent[5:], (sent[0],))
    near = once(near, (kept[0],))
    far = swap_core(near)

    flat = lambda a: a.reshape(2 * units, features)
    first, second, *rest = links.groups
    stay, outgoing = divide(
        of(second), [flat(kept[0]), flat(arrived)], (cos, sin, pos, bounds, joint_places)
    )
    terms = [stay, links.swap(outgoing, *second)]
    normed_t, qkv, mix_t = project(
        places, x_own, x_sib, dy_own, dy_sib, near, far, pack, joint_weight, dense_weight, cos, sin,
        heads, (outgoing,),
    )
    ready = normed_t
    for number, group in enumerate(rest):
        stay, *outgoing = divide(of(group), terms, (ready,))
        terms = [stay, *links.swap_group(outgoing, group)]
        ready = stay
        if number == 0:
            out_sib, back_sib = products(places, sent, kept, contract_weight, expand_weight, True, (stay,))
            ready = out_sib
    out_own, back_own = products(places, sent, kept, contract_weight, expand_weight, False, (stay,))
    out_sib, back_sib = swap_core(out_sib), swap_core(back_sib)
    terms[-1] = once(terms[-1], (out_own,))
    last = total_of(terms)
    gathered = lax.all_gather(last, CHIP, axis=0, tiled=True)
    mixed_own, mixed_far, *grads = attention(bounds, qkv, mix_t, pos, cos, sin, chunk, segs, (last,))
    mixed_own, mixed_far = mixed_own.reshape(part, tokens), mixed_far.reshape(part, tokens)
    grads = [g.reshape(3, part, tokens) for g in grads]
    bits = [joint_links.bit(n) for n in range(joint_links.rounds)]
    grads_sib = swap_core(grads[1])
    mixed = (mixed_own, mixed_far)
    outgoing, current, joint_b = joint_grads(
        joint_places, normed_t, grads, mixed, dy_own, dy_sib, near, far
    )
    arrived = joint_links.swap(outgoing, *first)
    mixed_sib = swap_core(once(mixed_far, (grads[0],)))
    mixed_near = swap_x(jnp.concatenate([mixed_own[:, chunk:], mixed_sib[:, chunk:]], axis=0))
    dx_own, dx_far, gain_attn, bias_attn = norm_back(
        places, grads[0], grads_sib, joint_weight, x_own, near, pack, (current,)
    )
    dx_near = swap_x(dx_far)
    stay, outgoing = divide(of(second), [current, arrived], (dx_own,))
    terms = [stay, joint_links.swap(outgoing, *second)]
    block_out = block_result(
        places, x_own, out_own, out_sib, mixed_own, mixed_sib, mixed_near, dense_weight, pack, (stay,)
    )
    ready = block_out
    for number, group in enumerate(rest):
        stay, *outgoing = divide(of(group), terms, (ready,))
        terms = [stay, *joint_links.swap_group(outgoing, group)]
        ready = stay
        if number == 0:
            grad_contract_w, grad_expand_w = spread(gathered, links, features, units, (stay,))
            ready = grad_contract_w
    input_grad, small = input_result(
        places, x_own, dy_own, back_own, back_sib, dx_own, dx_near, pack,
        (gain_attn, bias_attn, sent[4], sent[3], kept[3]), joint_b, (ready,),
    )
    terms[-1] = once(terms[-1], (input_grad,))
    current = total_of(terms)

    shared = 5 * features

    def summed(group, small):
        pair, small = two_parts(small)
        outgoing = jnp.concatenate([current, pair], axis=0)
        rows_now = current.shape[0]
        arrived = [joint_links.swap(outgoing, *numbers) for numbers in joint_links.others(group)]
        parts = [small] + [one_part(array[rows_now:]) for array in arrived]
        while len(parts) > 1:
            parts = [a + b for a, b in zip(parts[::2], parts[1::2])]
        return in_order(of(group), [current] + [array[:rows_now] for array in arrived]), parts[0]

    for group in reversed(rest):
        current, small = summed(group, small)
    pair, small = two_parts(small)
    rows_now = current.shape[0]
    outgoing = jnp.concatenate([current, pair], axis=0)
    arrived = joint_links.swap(outgoing, *second)
    one, both = joint_links.swap(pair, *first), joint_links.swap(pair, *first, *second)
    small = (small + one_part(arrived[rows_now:])) + (one_part(one) + one_part(both))
    current = in_order(of(second), [current, arrived[:rows_now]])
    arrived = joint_links.swap(current, *first)
    sib_current = swap_core(current)
    pair, small = two_parts(small)
    small_sib = one_part(swap_core(pair)).reshape(-1)
    small = small.reshape(-1)
    sums = (small + small_sib)[:shared].reshape(5, features)
    ordered = lambda a, b: jnp.where(core_at == 0, jnp.stack([a, b]), jnp.stack([b, a]))
    single = ordered(small[shared:], small_sib[shared:])
    grad_expand_b = single[:, : 2 * units].reshape(-1)
    grad_joint_b = single[:, 2 * units : 2 * units + 3 * part].reshape(2, 3, part).transpose(1, 0, 2).reshape(-1)
    into = spread_joint(joint_places, current, sib_current, features, 1)
    arrived = once(arrived, (into[0], sums, grad_joint_b, grad_expand_b))
    grad_joint_w, grad_dense_w = spread_joint(
        joint_places, arrived, swap_core(arrived), features, 0, into
    )
    return (
        block_out.reshape(block_in.shape),
        input_grad.reshape(block_in.shape),
        sums[0],
        sums[1],
        sums[2],
        sums[3],
        grad_joint_w,
        grad_joint_b,
        grad_dense_w,
        sums[4],
        grad_expand_w,
        grad_expand_b,
        grad_contract_w,
        sums[4],
    )


def solution(mesh):
    row_count, seq_count = mesh.devices.shape
    chips = Mesh(mesh.devices.reshape(row_count, seq_count // 2, 2), CHIP)
    links = Links(row_count)
    tokens = P("rows", ("x", "core"), None)
    in_specs = (tokens, P("rows", None)) + (P(),) * 12 + (tokens,)
    out_specs = (tokens, tokens) + (P(),) * 12
    return jax.shard_map(
        functools.partial(per_device, links, Links(row_count, True)), mesh=chips, in_specs=in_specs, out_specs=out_specs,
        check_vma=False,
    )
```

```python
import functools

import jax
import jax.numpy as jnp
from jax import lax
from jax.experimental import pallas as pl
from jax.experimental.pallas import tpu as pltpu
from jax.sharding import Mesh, PartitionSpec as P

H = 12
RD = 16
HALF = RD // 2
EPSILON = 1e-05
BASE_FREQ = 10000.0
NEGATIVE = -1e30
F32 = jnp.float32
BF16 = jnp.bfloat16
VMEM_BYTES = 64 * 2**20
CHIP = ("rows", "x", "core")
NT = (((1,), (1,)), ((), ()))


def dot(a, b):
    return jnp.dot(a, b, preferred_element_type=F32)


def dot_nt(a, b):
    return lax.dot_general(a, b, NT, preferred_element_type=F32)


def params():
    return pltpu.CompilerParams(vmem_limit_bytes=VMEM_BYTES)


def lasting(microseconds):
    return pl.CostEstimate(flops=int(microseconds * 1e9), bytes_accessed=0, transcendentals=0)


def whole(shape):
    return pl.BlockSpec(shape, lambda *_: (0,) * len(shape))


def shaped(shape, dtype):
    return jax.ShapeDtypeStruct(shape, dtype)


def after(kernel, inputs, deps):
    return lambda *refs: kernel(*refs[:inputs], *refs[inputs + deps :])


ANYWHERE = pl.BlockSpec(memory_space=pl.ANY)


def once(array, deps):
    return pl.pallas_call(
        lambda *refs: None,
        out_shape=shaped(array.shape, array.dtype),
        in_specs=[ANYWHERE] * (1 + len(deps)),
        out_specs=ANYWHERE,
        input_output_aliases={0: 0},
        cost_estimate=lasting(0.1),
    )(array, *deps)


def norm_stats(x):
    centered = x - jnp.mean(x, axis=-1, keepdims=True)
    spread = jnp.mean(centered * centered, axis=-1, keepdims=True)
    inverse = lax.rsqrt(spread + EPSILON)
    return centered * inverse, inverse


def gelu_both(h):
    e = jnp.exp2(h * h * (-0.5 * 1.4426950408889634))
    t = pl.reciprocal(1.0 + jnp.abs(h) * (0.3275911 * 0.7071067811865476), approx=False)
    poly = t * (
        0.5 * 0.254829592
        + t * (0.5 * -0.284496736 + t * (0.5 * 1.421413741 + t * (0.5 * -1.453152027 + t * (0.5 * 1.061405429))))
    )
    tail = poly * e
    phi = jnp.where(h >= 0.0, 1.0 - tail, tail)
    return h * phi, phi + h * e * 0.3989422804014327


def feed_kernel(
    base, x_own, x_sib, dy_own, dy_sib, pack, we, wc,
    grads, act, hid, be_grad, out_bias, normed, nf, act_t, hid_t, x_here, dy_here, gone, arrived,
):
    tokens, features = dy_own.shape
    copy = pltpu.make_async_copy(nf, normed, gone)

    @pl.when(pl.program_id(0) == 0)
    def _():
        tile = 256
        sources = (x_own, x_sib, dy_own, dy_sib)
        places = (x_here.at[0], x_here.at[1], dy_here.at[0], dy_here.at[1])
        copies = [
            pltpu.make_async_copy(a, b, arrived.at[n]) for n, (a, b) in enumerate(zip(sources, places))
        ]
        for one in copies:
            one.start()
        for half in range(2):
            copies[half].wait()

            def norm(i, _):
                here = pl.ds(pl.multiple_of(i * tile, tile), tile)
                there = pl.ds(pl.multiple_of(half * tokens + i * tile, tile), tile)
                hat, _ = norm_stats(x_here[half, here, :].astype(F32))
                nf[there, :] = (hat * pack[2:3, :] + pack[3:4, :]).astype(BF16)
                return 0

            lax.fori_loop(0, tokens // tile, norm, 0)
        copy.start()
        copies[2].wait()
        copies[3].wait()

        def add_up(i, total):
            here = pl.ds(pl.multiple_of(i * tile, tile), tile)
            return total + jnp.sum(dy_here[0, here, :].astype(F32), axis=0, keepdims=True)

        out_bias[...] = lax.fori_loop(0, tokens // tile, add_up, jnp.zeros((1, features), F32))

    feed_tile(base, nf, dy_here.at[0], dy_here.at[1], pack, we, wc, grads, act, hid, be_grad, act_t, hid_t)

    @pl.when(pl.program_id(0) == pl.num_programs(0) - 1)
    def _():
        copy.wait()


def feed_tile(base, nf, dy_own, dy_sib, pack, we, wc, grads, act, hid, be_grad, act_t, hid_t):
    step = pl.program_id(0)
    tokens, features = dy_own.shape
    width = we.shape[1]
    first = (base[0] + step) * width
    be = pack[
        pl.ds(5 + first // features, 1), pl.ds(pl.multiple_of(first % features, width), width)
    ]
    tile = 512
    per = tokens // tile
    count = 2 * per
    hidden, back = [None] * count, [None] * count

    def finish(n):
        value, slope = gelu_both(hidden[n])
        rows = slice(n * tile, (n + 1) * tile)
        value, slope = value.astype(BF16), (back[n] * slope).astype(BF16)
        act[rows, :] = value
        hid[rows, :] = slope
        act_t[:, rows] = value.T
        hid_t[:, rows] = slope.T

    for n in range(count):
        dy_ref = dy_own if n < per else dy_sib
        hidden[n] = dot(nf[n * tile : (n + 1) * tile, :], we[...]) + be
        back[n] = dot_nt(dy_ref[(n % per) * tile : (n % per + 1) * tile, :], wc[...])
        if n > 0:
            finish(n - 1)
    finish(count - 1)
    there = pl.ds(pl.multiple_of(step * width, width), width)
    grads[0, there, :] = (
        dot(act_t[:, :tokens], dy_own[...]) + dot(act_t[:, tokens:], dy_sib[...])
    ).astype(BF16)
    grads[1, :, there] = dot(hid_t[...], nf[...]).T.astype(BF16)
    be_grad[...] = jnp.sum(hid[...].astype(F32), axis=0, keepdims=True)


def feed_part(base, x, dy_own, dy_sib, pack, we, wc, units, deps=()):
    tokens, features = dy_own.shape
    width = 256
    prepared = len(x) == 1
    token = pl.BlockSpec((2 * tokens, width), lambda t, b: (0, t))
    out_shape = (
        shaped((2, units, features), BF16), shaped((2 * tokens, units), BF16),
        shaped((2 * tokens, units), BF16), shaped((1, units), F32),
    )
    out_specs = (whole((2, units, features)), token, token, pl.BlockSpec((1, width), lambda t, b: (0, t)))
    scratch = [pltpu.VMEM((width, 2 * tokens), BF16), pltpu.VMEM((width, 2 * tokens), BF16)]
    if not prepared:
        out_shape += (shaped((1, features), F32), shaped((2 * tokens, features), BF16))
        out_specs += (whole((1, features)), ANYWHERE)
        both = pltpu.VMEM((2, tokens, features), BF16)
        scratch = [pltpu.VMEM((2 * tokens, features), BF16), *scratch, both, both,
                   pltpu.SemaphoreType.DMA, pltpu.SemaphoreType.DMA((4,))]
    return pl.pallas_call(
        after(feed_tile if prepared else feed_kernel, 6 + len(x), len(deps)),
        out_shape=out_shape,
        grid_spec=pltpu.PrefetchScalarGridSpec(
            num_scalar_prefetch=1,
            grid=(units // width,),
            in_specs=([whole(a.shape) for a in (*x, dy_own, dy_sib)] if prepared else [ANYWHERE] * 4)
            + [
                whole(pack.shape),
                pl.BlockSpec((features, width), lambda t, b: (0, b[0] + t)),
                pl.BlockSpec((width, features), lambda t, b: (b[0] + t, 0)),
            ]
            + [ANYWHERE] * len(deps),
            out_specs=out_specs,
            scratch_shapes=scratch,
        ),
        cost_estimate=lasting(22),
        compiler_params=params(),
    )(base, *x, dy_own, dy_sib, pack, we, wc, *deps)


def row_pieces(places, own, sib, near, far, number, tile):
    rows = pl.ds(pl.multiple_of(places[3] * tile, tile), tile)
    return own.at[rows], near.at[number], sib.at[rows], far.at[number]


def project_kernel(
    places, x_own, x_sib, dy_own, dy_sib, near, far, pack, wq, wk, wv, wd,
    cos, sin, normed_t, qkv, mix_t, w_t, jb, x_here, dy_here, arrived,
):
    step = pl.program_id(0)
    part = wq.shape[1]
    heads, size = qkv.shape[1], qkv.shape[2]
    tile = x_here.shape[1]
    copies = [
        [pltpu.make_async_copy(piece, there.at[n], arrived.at[which, n]) for n, piece in enumerate(pieces)]
        for which, (there, pieces) in enumerate((
            (x_here, row_pieces(places, x_own, x_sib, near, far, 0, tile)),
            (dy_here, row_pieces(places, dy_own, dy_sib, near, far, 1, tile)),
        ))
    ]

    @pl.when(step == 0)
    def _():
        for pair in zip(*copies):
            for copy in pair:
                copy.start()
        lanes = pl.ds(pl.multiple_of(places[2] * part, 128), part)
        for n, w in enumerate((wq, wk, wv)):
            rows = slice(n * part, (n + 1) * part)
            w_t[rows, :] = w[...].T
            jb[rows, :] = jnp.broadcast_to(pack[9 + n : 10 + n, lanes], (128, part)).T

    for number in range(4):

        @pl.when(step == number)
        def _():
            copies[0][number].wait()
            copies[1][number].wait()

    hat, _ = norm_stats(x_here[step].astype(F32))
    turned = (hat * pack[0:1, :] + pack[1:2, :]).astype(BF16).T
    normed_t[...] = turned
    mix = dot_nt(wd[...], dy_here[step])
    c, s = cos[...], sin[...]
    for n in range(3):
        rows = slice(n * part, (n + 1) * part)
        joint = dot(w_t[rows, :], turned) + jnp.concatenate([jb[rows, :]] * (c.shape[1] // 128), axis=1)
        for h in range(heads):
            one = joint[h * size : (h + 1) * size]
            if n < 2:
                a, b = one[:HALF], one[HALF:RD]
                one = jnp.concatenate([a * c - b * s, b * c + a * s, one[RD:]], axis=0)
            if n == 0:
                one = one * size**-0.5
            qkv[n, h] = one.astype(BF16)
    for h in range(heads):
        mix_t[h] = mix[h * size : (h + 1) * size].astype(BF16)


def project(places, x_own, x_sib, dy_own, dy_sib, near, far, pack, joint_w, dense_w, cos, sin,
            heads, deps=()):
    tokens, features = x_own.shape
    tile = tokens // 2
    part = features // 2
    size = part // heads
    weight = lambda n: pl.BlockSpec((features, part), lambda g, p: (0, 2 * n + p[2]))
    lane = pl.BlockSpec((HALF, tile), lambda g, p: (0, g))
    return pl.pallas_call(
        after(project_kernel, 14, len(deps)),
        out_shape=(
            shaped((features, 2 * tokens), BF16),
            shaped((3, heads, size, 2 * tokens), BF16),
            shaped((heads, size, 2 * tokens), BF16),
        ),
        grid_spec=pltpu.PrefetchScalarGridSpec(
            num_scalar_prefetch=1,
            grid=(4,),
            in_specs=[ANYWHERE] * 6
            + [whole(pack.shape), weight(0), weight(1), weight(2),
               pl.BlockSpec((part, features), lambda g, p: (p[2], 0)), lane, lane]
            + [ANYWHERE] * len(deps),
            out_specs=(
                pl.BlockSpec((features, tile), lambda g, p: (0, g)),
                pl.BlockSpec((3, heads, size, tile), lambda g, p: (0, 0, 0, g)),
                pl.BlockSpec((heads, size, tile), lambda g, p: (0, 0, g)),
            ),
            scratch_shapes=[pltpu.VMEM((3 * part, features), BF16), pltpu.VMEM((3 * part, 128), F32),
                            pltpu.VMEM((4, tile, features), BF16), pltpu.VMEM((4, tile, features), BF16),
                            pltpu.SemaphoreType.DMA((2, 4))],
        ),
        cost_estimate=lasting(12),
        compiler_params=params(),
    )(places, x_own, x_sib, dy_own, dy_sib, near, far, pack,
      joint_w, joint_w, joint_w, dense_w, cos, sin, *deps)


def placing(bounds, segs, block, chunk, total):
    per_chunk = chunk // block
    tag = bounds[segs - 1]

    def place(b):
        k = (b // per_chunk) ^ tag
        slot = 2 * (k & 1) + (k >> 1)
        return pl.multiple_of(slot * chunk + (b % per_chunk) * block, block)

    def halved(offset):
        half = offset // (total // 2)
        return half, pl.ds(pl.multiple_of(offset - half * (total // 2), block), block)

    def first_of(position):
        start = jnp.int32(0)
        for m in range(segs - 1):
            start = jnp.where(bounds[m] <= position, bounds[m], start)
        return start

    def last_of(position):
        end = jnp.int32(total)
        for m in range(segs - 2, -1, -1):
            end = jnp.where(bounds[m] > position, bounds[m], end)
        return end - 1

    return place, halved, first_of, last_of


def sentence_rows(bounds, segs, pos):
    seg = jnp.zeros_like(pos)
    for m in range(segs - 1):
        seg = seg + (pos >= bounds[m]).astype(jnp.int32)
    rows = lax.broadcasted_iota(jnp.int32, (16, pos.shape[1]), 0)
    same = rows == seg
    onehot = jnp.where(same, 1.0, 0.0).astype(BF16)
    away = jnp.where(same | (rows >= segs), 0.0, NEGATIVE).astype(BF16)
    return onehot, away


def causal_bias(block):
    key = lax.broadcasted_iota(jnp.int32, (block, block), 0)
    query = lax.broadcasted_iota(jnp.int32, (block, block), 1)
    return jnp.where(key <= query, 0.0, NEGATIVE)


def staged(heads, *steps):
    for turn in range(len(heads) + len(steps) - 1):
        for number, step in enumerate(steps):
            if 0 <= turn - number < len(heads):
                step(heads[turn - number])


def in_runs(start, end, body, run=2):
    runs = (end - start) // run

    def several(n, _):
        body([start + n * run + r for r in range(run)])
        return 0

    def single(n, _):
        body([n])
        return 0

    lax.fori_loop(0, runs, several, 0)
    if run > 1:
        lax.fori_loop(start + runs * run, end, single, 0)


def attention_kernel(
    bounds, qkv, mix_hbm, pos, cos, sin, out_near, out_far, grad_near, grad_far,
    here, mix, mixed, grads, stats, qa, kn, vn, acc, top, low, dq, dk, dv, came, gone, left,
    *, heads, block, chunk, segs,
):
    total = mix.shape[-1]
    size = mix.shape[1]
    place, halved, first_of, last_of = placing(bounds, segs, block, chunk, total)
    hs = range(heads)
    copy = pltpu.make_async_copy
    loads = [copy(qkv.at[n], here.at[n], came.at[n]) for n in range(3)] + [copy(mix_hbm, mix, came.at[3])]
    for n in (1, 0, 2, 3):
        loads[n].start()
    q, k, v = (here.at[pl.ds(n, 1)] for n in range(3))
    onehot, away = sentence_rows(bounds, segs, pos[...])
    loads[1].wait()
    for h in hs:
        kn[h] = jnp.concatenate([k[0, h], onehot], axis=0).T
    loads[0].wait()
    for h in hs:
        qa[h, :size, :] = q[0, h]
        qa[h, size:, :] = away
    loads[2].wait()
    for h in hs:
        vn[h] = v[0, h].T
    loads[3].wait()
    bias = causal_bias(block)

    def queries(i, _):
        half, lanes = halved(place(i))
        qs = pl.ds(place(i), block)
        s = [dot(kn[h, qs, :], qa[h, :, qs]) + bias for h in hs]
        m = [jnp.max(s[h], axis=0, keepdims=True) for h in hs]
        p = [jnp.exp(s[h] - m[h]) for h in hs]
        o = [dot(v[0, h, :, qs], p[h].astype(BF16)) for h in hs]
        l = [jnp.sum(p[h], axis=0, keepdims=True) for h in hs]
        for h in hs:
            top[h] = m[h]
            low[h] = l[h]
            acc[h] = o[h]

        def keys(blocks):
            parts = [pl.ds(place(j), block) for j in blocks]
            s, p, f = {}, {}, {}

            def score(h):
                s[h] = [dot(kn[h, ks, :], qa[h, :, qs]) for ks in parts]

            def soften(h):
                m_old = top[h]
                m = m_old
                for one in s[h]:
                    m = jnp.maximum(m, jnp.max(one, axis=0, keepdims=True))
                e = [jnp.exp(one - m) for one in s[h]]
                f[h] = jnp.exp(m_old - m)
                top[h] = m
                low[h] = low[h] * f[h] + sum(jnp.sum(one, axis=0, keepdims=True) for one in e)
                p[h] = [one.astype(BF16) for one in e]

            def gather(h):
                acc[h] = acc[h] * f[h] + sum(dot(v[0, h, :, ks], one) for ks, one in zip(parts, p[h]))

            staged(hs, score, soften, gather)

        in_runs(first_of(i * block) // block, i, keys)
        result = [acc[h] / low[h] for h in hs]
        for h in hs:
            mixed[half, h, :, lanes] = result[h].astype(BF16)
        for h in hs:
            o = result[h]
            stats[h, 0:1, qs] = top[h] + jnp.log(low[h])
            stats[h, 1:2, qs] = jnp.sum(o * mix[h, :, qs].astype(F32), axis=0, keepdims=True)
        return 0

    lax.fori_loop(0, total // block, queries, 0)

    early = [copy(mixed.at[n], out, left.at[n]) for n, out in enumerate((out_near, out_far))]
    for one in early:
        one.start()
    dq[...] = jnp.zeros_like(dq)

    def pairs(parts, ks, add, fresh):
        p, ds, s, dp = {}, {}, {}, {}

        def score(h):
            s[h] = [dot(kn[h, ks, :], qa[h, :, qs]) for qs in parts]
            dp[h] = [dot(vn[h, ks, :], mix[h, :, qs]) for qs in parts]

        def soften(h):
            p[h], ds[h] = [], []
            for qs, one, back in zip(parts, s[h], dp[h]):
                e = jnp.exp((one if add is None else one + add) - stats[h, 0:1, qs])
                p[h].append(e.astype(BF16))
                ds[h].append((e * (back - stats[h, 1:2, qs])).astype(BF16))

        def gather(h):
            a = sum(dot_nt(mix[h, :, qs], one) for qs, one in zip(parts, p[h]))
            b = sum(dot_nt(q[0, h, :, qs], one) for qs, one in zip(parts, ds[h]))
            dv[h] = a if fresh else dv[h] + a
            dk[h] = b if fresh else dk[h] + b
            for qs, one in zip(parts, ds[h]):
                dq[h, :, qs] += dot(k[0, h, :, ks], one)

        staged(hs, score, soften, gather)

    def turned_back(g, c, s):
        a, b = g[:HALF], g[HALF:RD]
        return jnp.concatenate([a * c + b * s, b * c - a * s, g[RD:]], axis=0).astype(BF16)

    def key_block(j, _):
        ks = pl.ds(place(j), block)
        pairs([ks], ks, bias, True)
        in_runs(
            j + 1,
            last_of((j + 1) * block - 1) // block + 1,
            lambda blocks: pairs([pl.ds(place(i), block) for i in blocks], ks, None, False),
            1,
        )
        half, lanes = halved(place(j))
        c, s = cos[:, ks], sin[:, ks]
        g = [(turned_back(dk[h], c, s), dv[h].astype(BF16)) for h in hs]
        for h in hs:
            grads[half, 1, h, :, lanes] = g[h][0]
            grads[half, 2, h, :, lanes] = g[h][1]
        for number, out in enumerate((grad_near, grad_far)):

            @pl.when(half == number)
            def _():
                copy(grads.at[number, 1:, :, :, lanes], out.at[1:, :, :, lanes], gone.at[j]).start()

        return 0

    lax.fori_loop(0, total // block, key_block, 0)
    c, s = cos[...], sin[...]
    for h in hs:
        g = turned_back(dq[h] * size**-0.5, c, s)
        grads[0, 0, h] = g[:, : total // 2]
        grads[1, 0, h] = g[:, total // 2 :]
    last = [copy(grads.at[n, 0], out.at[0], left.at[2 + n]) for n, out in enumerate((grad_near, grad_far))]
    for one in last:
        one.start()
    for j in range(total // block):
        copy(grads.at[0, 1:, :, :, :block], grad_near.at[1:, :, :, :block], gone.at[j]).wait()
    for one in early + last:
        one.wait()


def attention(bounds, qkv, mix, pos, cos, sin, chunk, segs, deps=(), block=256):
    _, heads, size, total = qkv.shape
    kernel = functools.partial(attention_kernel, heads=heads, block=block, chunk=chunk, segs=segs)
    mixed, grads = (heads, size, total // 2), (3, heads, size, total // 2)
    return pl.pallas_call(
        after(kernel, 6, len(deps)),
        out_shape=(shaped(mixed, BF16),) * 2 + (shaped(grads, BF16),) * 2,
        grid_spec=pltpu.PrefetchScalarGridSpec(
            num_scalar_prefetch=1,
            grid=(1,),
            in_specs=[ANYWHERE, ANYWHERE, whole((1, total)),
                      whole((HALF, total)), whole((HALF, total))] + [ANYWHERE] * len(deps),
            out_specs=(ANYWHERE,) * 4,
            scratch_shapes=[
                pltpu.VMEM((3, heads, size, total), BF16),
                pltpu.VMEM((heads, size, total), BF16),
                pltpu.VMEM((2, *mixed), BF16),
                pltpu.VMEM((2, *grads), BF16),
                pltpu.VMEM((heads, 2, total), F32),
                pltpu.VMEM((heads, size + 16, total), BF16),
                pltpu.VMEM((heads, total, size + 16), BF16),
                pltpu.VMEM((heads, total, size), BF16),
                pltpu.VMEM((heads, size, block), F32),
                pltpu.VMEM((heads, 1, block), F32),
                pltpu.VMEM((heads, 1, block), F32),
                pltpu.VMEM((heads, size, total), F32),
                pltpu.VMEM((heads, size, block), F32),
                pltpu.VMEM((heads, size, block), F32),
                pltpu.SemaphoreType.DMA((4,)),
                pltpu.SemaphoreType.DMA((total // block,)),
                pltpu.SemaphoreType.DMA((4,)),
            ],
        ),
        cost_estimate=lasting(60),
        compiler_params=params(),
    )(bounds, qkv, mix, pos, cos, sin, *deps)


def joint_grads_kernel(
    places, normed_t, near, far, mixed, mixed_far, dy_own, dy_sib, dy_near, dy_far, going, staying, bias,
    nt, g, mx, dy, made, arrived, gone,
):
    part, tokens = mixed.shape
    tile = tokens // 2
    copy = pltpu.make_async_copy
    first = copy(normed_t, nt, arrived.at[3, 0])
    first.start()
    later = []
    for n in range(3):
        later.append([copy(near.at[n], g.at[n, 0], arrived.at[n, 0]), copy(far.at[n], g.at[n, 1], arrived.at[n, 1])])
    last = [copy(mixed, mx.at[0], arrived.at[3, 1]), copy(mixed_far, mx.at[1], arrived.at[3, 2])]
    pieces = row_pieces(places, dy_own, dy_sib, dy_near, dy_far, 1, tile)
    last += [copy(piece, dy.at[n], arrived.at[4, n]) for n, piece in enumerate(pieces)]
    later.append(last)
    for copies in later:
        for one in copies:
            one.start()
    first.wait()
    leaving = []
    for n in range(4):
        for one in later[n]:
            one.wait()
        for which, out in enumerate((going, staying)):
            half = pl.ds(pl.multiple_of(places[4 + which] * part, 128), part)
            if n < 3:
                value = dot_nt(nt[half, :tokens], g[n, 0]) + dot_nt(nt[half, tokens:], g[n, 1])
            else:
                value = (
                    dot(mx[0, :, :tile], dy[0, :, half]) + dot(mx[0, :, tile:], dy[1, :, half])
                    + dot(mx[1, :, :tile], dy[2, :, half]) + dot(mx[1, :, tile:], dy[3, :, half])
                )
            made[which, n] = value.astype(BF16)
            there = out.at[:, n * part : (n + 1) * part]
            leaving.append(copy(made.at[which, n], there, gone.at[which, n]))
            leaving[-1].start()
        if n < 3:
            total = None
            for half in range(2):
                for at in range(0, tokens, 128):
                    one = g[n, half, :, at : at + 128].astype(F32)
                    total = one if total is None else total + one
            bias[n] = jnp.sum(total.T, axis=0, keepdims=True)
    for one in leaving:
        one.wait()


def joint_grads(places, normed_t, grads, mixed, dy_own, dy_sib, near, far, deps=()):
    features, total = normed_t.shape
    part = features // 2
    tokens = total // 2
    return pl.pallas_call(
        after(joint_grads_kernel, 10, len(deps)),
        out_shape=(shaped((part, 4 * part), BF16),) * 2 + (shaped((3, 1, part), F32),),
        grid_spec=pltpu.PrefetchScalarGridSpec(
            num_scalar_prefetch=1,
            grid=(1,),
            in_specs=[ANYWHERE] * (9 + len(deps)),
            out_specs=(ANYWHERE, ANYWHERE, whole((3, 1, part))),
            scratch_shapes=[
                pltpu.VMEM((features, total), BF16), pltpu.VMEM((3, 2, part, tokens), BF16),
                pltpu.VMEM((2, part, tokens), BF16), pltpu.VMEM((4, tokens // 2, features), BF16),
                pltpu.VMEM((2, 4, part, part), BF16), pltpu.SemaphoreType.DMA((5, 4)),
                pltpu.SemaphoreType.DMA((2, 4)),
            ],
        ),
        cost_estimate=lasting(11),
        compiler_params=params(),
    )(places, normed_t, grads[0], grads[1], mixed[0], mixed[1], dy_own, dy_sib, near, far, *deps)


def norm_back_of(grad, x, gain):
    hat, inverse = norm_stats(x)
    scaled = grad * gain
    dx = inverse * (
        scaled
        - jnp.mean(scaled, axis=-1, keepdims=True)
        - hat * jnp.mean(scaled * hat, axis=-1, keepdims=True)
    )
    return dx, jnp.sum(grad * hat, axis=0, keepdims=True), jnp.sum(grad, axis=0, keepdims=True)


def norm_back_kernel(places, own, sib, w, x, x_near, pack, dx_own, dx_far, gain_grad, bias_grad, x_here):
    step = pl.program_id(0)
    part = own.shape[1]
    core = places[2]

    @pl.when(step == 0)
    def _():
        x_here[...] = x_near[0]

    @pl.when(step == 1)
    def _():
        x_here[...] = x[...]

    total = None
    for n in range(3):
        mine = pl.ds(pl.multiple_of((2 * n + core) * part, 128), part)
        other = pl.ds(pl.multiple_of((2 * n + 1 - core) * part, 128), part)
        one = dot(w[:, mine], own[n]) + dot(w[:, other], sib[n])
        total = one if n == 0 else total + one
    dx, g, b = norm_back_of(total.T, x_here[...].astype(F32), pack[0:1, :])

    @pl.when(step == 0)
    def _():
        dx_far[...] = dx.astype(BF16)
        gain_grad[...] = g
        bias_grad[...] = b

    @pl.when(step == 1)
    def _():
        dx_own[...] = dx
        gain_grad[...] += g
        bias_grad[...] += b


def norm_back(places, own, sib, w, x, near, pack, deps=()):
    part = own.shape[1]
    tokens, features = x.shape
    tile = tokens // 2
    piece = pl.BlockSpec((3, part, tile), lambda g, p: (0, 0, 1 - g))
    return pl.pallas_call(
        after(norm_back_kernel, 7, len(deps)),
        out_shape=(shaped((tile, features), F32), shaped((tile, features), BF16),
                   shaped((1, features), F32), shaped((1, features), F32)),
        grid_spec=pltpu.PrefetchScalarGridSpec(
            num_scalar_prefetch=1,
            grid=(2,),
            in_specs=[piece, piece, whole(w.shape),
                      pl.BlockSpec((tile, features), lambda g, p: (p[3], 0)),
                      pl.BlockSpec((1, tile, features), lambda g, p: (0, 0, 0)),
                      whole(pack.shape)] + [ANYWHERE] * len(deps),
            out_specs=(whole((tile, features)), whole((tile, features)),
                       whole((1, features)), whole((1, features))),
            scratch_shapes=[pltpu.VMEM((tile, features), BF16)],
        ),
        cost_estimate=lasting(12),
        compiler_params=params(),
    )(places, own, sib, w, x, near, pack, *deps)


def products_kernel(places, act_a, act_b, hid_a, hid_b, wc_a, wc_b, we_a, we_b, out, back):
    out[...] = (dot(act_a[...], wc_a[...]) + dot(act_b[...], wc_b[...])).astype(out.dtype)
    back[...] = (dot_nt(hid_a[...], we_a[...]) + dot_nt(hid_b[...], we_b[...])).astype(back.dtype)


def products(places, sent, kept, wc, we, sibling, deps=()):
    tokens, units = sent[1].shape[0] // 2, sent[1].shape[1]
    features = wc.shape[1]
    tile = tokens // 2
    token = pl.BlockSpec((tile, units), lambda g, p: (2 * int(sibling) + g, 0))
    row = lambda n: pl.BlockSpec((units, features), lambda g, p: (p[n], 0))
    column = lambda n: pl.BlockSpec((features, units), lambda g, p: (0, p[n]))
    spec = pl.BlockSpec((tile, features), lambda g, p: (g, 0))
    return pl.pallas_call(
        after(products_kernel, 9, len(deps)),
        out_shape=(shaped((tokens, features), BF16 if sibling else F32),) * 2,
        grid_spec=pltpu.PrefetchScalarGridSpec(
            num_scalar_prefetch=1,
            grid=(2,),
            in_specs=[token] * 4 + [row(0), row(1), column(0), column(1)] + [ANYWHERE] * len(deps),
            out_specs=(spec, spec),
        ),
        cost_estimate=lasting(10),
        compiler_params=params(),
    )(places, sent[1], kept[1], sent[2], kept[2], wc, wc, we, we, *deps)


def block_out_kernel(places, x, out, out_sib, mixed, mixed_sib, mixed_near, wd, pack, block_out):
    step = pl.program_id(0)
    part, tile = mixed.shape[0], x.shape[0]
    core = places[2]
    mine = pl.ds(pl.multiple_of(core * part, 128), part)
    other = pl.ds(pl.multiple_of((1 - core) * part, 128), part)

    def finish(ours, siblings):
        attn = dot(ours.T, wd[mine, :]) + dot(siblings.T, wd[other, :])
        feed = out[...] + out_sib[...].astype(F32)
        block_out[...] = (x[...].astype(F32) + attn + feed + pack[4:5, :]).astype(BF16)

    @pl.when(step == 0)
    def _():
        finish(mixed[:, :tile], mixed_sib[:, :tile])

    @pl.when(step == 1)
    def _():
        finish(mixed_near[:part, :], mixed_near[part:, :])


def block_result(places, x, out, out_sib, mixed, mixed_sib, mixed_near, wd, pack, deps=()):
    tokens, features = out.shape
    tile = tokens // 2
    part = features // 2
    token = pl.BlockSpec((tile, features), lambda g, p: (p[3] ^ g, 0))
    return pl.pallas_call(
        after(block_out_kernel, 9, len(deps)),
        out_shape=shaped((tokens, features), BF16),
        grid_spec=pltpu.PrefetchScalarGridSpec(
            num_scalar_prefetch=1,
            grid=(2,),
            in_specs=[token] * 3 + [whole((part, tokens)), whole((part, tokens)), whole((features, tile)),
                      whole((features, features)), whole(pack.shape)] + [ANYWHERE] * len(deps),
            out_specs=token,
        ),
        cost_estimate=lasting(8),
        compiler_params=params(),
    )(places, x, out, out_sib, mixed, mixed_sib, mixed_near, wd, pack, *deps)


def input_grad_kernel(
    places, x, dy, back, back_sib, dx_own, dx_near, pack, gain_attn, bias_attn, out_bias, be_sent, be_kept,
    joint_b, input_grad, small, gain_sum, bias_sum,
):
    step = pl.program_id(0)
    features = x.shape[1]
    dx_feed, g, b = norm_back_of(
        back[...] + back_sib[...].astype(F32), x[...].astype(F32), pack[2:3, :]
    )

    @pl.when(step == 0)
    def _():
        input_grad[...] = (dy[...].astype(F32) + dx_own[...] + dx_feed).astype(BF16)
        gain_sum[...] = g
        bias_sum[...] = b

    @pl.when(step == 1)
    def _():
        input_grad[...] = (dy[...].astype(F32) + dx_near[...].astype(F32) + dx_feed).astype(BF16)
        small[...] = jnp.zeros_like(small)
        small[0:1, :features] = gain_attn[...]
        small[0:1, features:] = bias_attn[...]
        small[1:2, :features] = gain_sum[...] + g
        small[1:2, features:] = bias_sum[...] + b
        small[2:3, :features] = out_bias[...]
        first = places[5] == 0
        small[2:3, features:] = jnp.where(first, be_kept[...], be_sent[...])
        small[3:4, :features] = jnp.where(first, be_sent[...], be_kept[...])
        half = features // 2
        small[3:4, features : features + half] = joint_b[0]
        small[3:4, features + half :] = joint_b[1]
        small[4:5, :half] = joint_b[2]


def input_result(places, x, dy, back, back_sib, dx_own, dx_near, pack, sums, joint_b, deps=()):
    tokens, features = x.shape
    tile = tokens // 2
    token = pl.BlockSpec((tile, features), lambda g, p: (p[3] ^ g, 0))
    return pl.pallas_call(
        after(input_grad_kernel, 14, len(deps)),
        out_shape=(shaped((tokens, features), BF16), shaped((8, 2 * features), F32)),
        grid_spec=pltpu.PrefetchScalarGridSpec(
            num_scalar_prefetch=1,
            grid=(2,),
            in_specs=[token] * 4 + [whole((tile, features))] * 2 + [whole(pack.shape)]
            + [whole((1, features))] * 5 + [whole(joint_b.shape)] + [ANYWHERE] * len(deps),
            out_specs=(token, whole((8, 2 * features))),
            scratch_shapes=[pltpu.VMEM((1, features), F32), pltpu.VMEM((1, features), F32)],
        ),
        cost_estimate=lasting(8),
        compiler_params=params(),
    )(places, x, dy, back, back_sib, dx_own, dx_near, pack, *sums, joint_b, *deps)


class Links:
    def __init__(self, row_count, x_together=False):
        self.row_count = row_count
        self.row_bits = row_count.bit_length() - 1
        rest = range(2, self.row_bits)
        if x_together:
            self.orders = ([0, 1, "x", *rest], [1, 0, "x", *rest])
        else:
            dims = [0, 1, "x", *rest]
            other = list(dims)
            for n in range(0, len(dims) - 1, 2):
                other[n], other[n + 1] = other[n + 1], other[n]
            self.orders = (dims, other)
        dims = self.orders[0]
        self.rounds = len(dims)
        self.groups = [(n,) for n in range(self.rounds)]

    def bit(self, number, sibling=False):
        def of(dim):
            if dim == "x":
                return lax.axis_index("x")
            return (lax.axis_index("rows") >> dim) & 1

        return jnp.where(
            lax.axis_index("core") == int(sibling), of(self.orders[0][number]), of(self.orders[1][number])
        )

    def swap(self, array, *numbers):
        pairs = []
        for row in range(self.row_count):
            for x in range(2):
                for core in range(2):
                    there = [row, x]
                    for number in numbers:
                        dim = self.orders[core][number]
                        if dim == "x":
                            there[1] = 1 - there[1]
                        else:
                            there[0] ^= 1 << dim
                    pairs.append(((row * 2 + x) * 2 + core, (there[0] * 2 + there[1]) * 2 + core))
        return lax.ppermute(array, CHIP, pairs)

    def others(self, group):
        return [group] if len(group) == 1 else [group[1:], group[:1], group]

    def swap_group(self, arrays, group):
        return [self.swap(array, *numbers) for array, numbers in zip(arrays, self.others(group))]


def swap_core(array):
    return lax.ppermute(array, "core", [(0, 1), (1, 0)])


def swap_x(array):
    return lax.ppermute(array, "x", [(0, 1), (1, 0)])


def add(a, b):
    return (a.astype(F32) + b.astype(F32)).astype(BF16)


def total_of(terms):
    total = terms[0].astype(F32)
    for term in terms[1:]:
        total = total + term.astype(F32)
    return total.astype(BF16)


def divide_kernel(place, *refs, terms, pieces):
    for n in range(pieces):
        refs[terms * pieces + n][...] = total_of([refs[t * pieces + n][...] for t in range(terms)])


def divide(bits, terms, deps=()):
    place = bits[0] if len(bits) == 1 else bits[0] * 2 + bits[1]
    pieces = 2 ** len(bits)
    rows, width = terms[0].shape
    rows = rows // pieces
    if rows % 16:
        return [
            total_of([lax.dynamic_slice_in_dim(t, (place ^ n) * rows, rows, 0) for t in terms])
            for n in range(pieces)
        ]
    tile = min(rows, 384)
    steps = rows // tile
    source = lambda n: pl.BlockSpec((tile, width), lambda t, p: ((p[0] ^ n) * steps + t, 0))
    kernel = functools.partial(divide_kernel, terms=len(terms), pieces=pieces)
    return pl.pallas_call(
        after(kernel, 1 + len(terms) * pieces, len(deps)),
        out_shape=(shaped((rows, width), BF16),) * pieces,
        grid_spec=pltpu.PrefetchScalarGridSpec(
            num_scalar_prefetch=1,
            grid=(steps,),
            in_specs=[source(n) for n in range(pieces)] * len(terms) + [ANYWHERE] * len(deps),
            out_specs=(pl.BlockSpec((tile, width), lambda t, p: (t, 0)),) * pieces,
        ),
        cost_estimate=lasting(1),
        compiler_params=params(),
    )(place.astype(jnp.int32).reshape(1), *[t for t in terms for _ in range(pieces)], *deps)


def in_order(bits, pieces):
    if len(pieces) == 2:
        mine, other = pieces
        forward, back = jnp.concatenate([mine, other], axis=0), jnp.concatenate([other, mine], axis=0)
        return jnp.where(bits[-1] == 0, forward, back)
    low, high = in_order(bits[1:], pieces[:2]), in_order(bits[1:], pieces[2:])
    return in_order(bits[:1], [low, high])


def two_parts(vector):
    high = lax.reduce_precision(vector, 8, 7)
    low = lax.reduce_precision(vector - high, 8, 7)
    return jnp.concatenate([high, low], axis=0).astype(BF16), high + low


def one_part(pair):
    rows = pair.shape[0] // 2
    return pair[:rows].astype(F32) + pair[rows:].astype(F32)


def spread_kernel(*refs, parts):
    contract, expand = refs[2 * parts :]
    rows = contract.shape[0] // parts
    for q in range(parts):
        contract[q * rows : (q + 1) * rows, :] = refs[q][...].astype(F32)
        expand[q * rows : (q + 1) * rows, :] = refs[parts + q][...].astype(F32)


def spread(gathered, links, features, units, deps=()):
    piece = features >> (links.rounds - 2)
    parts = features // piece

    def rank(core, half, which, quarter):
        def one(order):
            place = 0
            bits = {order[0]: half, order[1]: which}
            for n, dim in enumerate(order[2:]):
                bits[dim] = (quarter >> (links.rounds - 3 - n)) & 1
            for dim, value in bits.items():
                place = place + (value * 2 if dim == "x" else value * (4 << dim))
            return place

        return jnp.where(core == 0, one(links.orders[0]), one(links.orders[1])) + core

    source = lambda which, q: pl.BlockSpec((piece, features), lambda c, h: (rank(c, h, which, q), 0))
    return pl.pallas_call(
        after(functools.partial(spread_kernel, parts=parts), 2 * parts, len(deps)),
        out_shape=(shaped((4 * units, features), F32), shaped((features, 4 * units), F32)),
        grid=(2, 2),
        in_specs=[source(which, q) for which in range(2) for q in range(parts)] + [ANYWHERE] * len(deps),
        out_specs=(
            pl.BlockSpec((features, features), lambda c, h: (c * 2 + h, 0)),
            pl.BlockSpec((features, features), lambda c, h: (0, c * 2 + h)),
        ),
        cost_estimate=lasting(12),
        compiler_params=params(),
    )(*[gathered] * (2 * parts), *deps)


def spread_joint_kernel(places, own, sib, *refs, which, offset):
    joint, dense, wide, arrived = refs[-4:]
    count, part = own.shape[0], own.shape[1] // 4
    copies = []
    for g, ref in enumerate((own, sib)):
        core = places[2] ^ g
        half = pl.multiple_of(places[4 + 2 * g + which] * part, part)
        for n in range(4):
            wide[g, n] = ref[:, n * part : (n + 1) * part].astype(F32)
            if n < 3:
                columns = pl.ds(pl.multiple_of((2 * n + core) * part, part), part)
                there = joint.at[pl.ds(pl.multiple_of(half + offset, 8), count), columns]
            else:
                rows = pl.ds(pl.multiple_of(core * part + offset, 8), count)
                there = dense.at[rows, pl.ds(half, part)]
            copies.append(pltpu.make_async_copy(wide.at[g, n], there, arrived.at[g, n]))
            copies[-1].start()
    for copy in copies:
        copy.wait()


def spread_joint(places, own, sib, features, which, into=(), offset=0):
    part = features // 2
    return pl.pallas_call(
        functools.partial(spread_joint_kernel, which=which, offset=offset),
        out_shape=(shaped((features, 3 * features), F32), shaped((features, features), F32)),
        grid_spec=pltpu.PrefetchScalarGridSpec(
            num_scalar_prefetch=1,
            grid=(1,),
            in_specs=[whole(own.shape), whole(sib.shape)] + [ANYWHERE] * len(into),
            out_specs=(ANYWHERE, ANYWHERE),
            scratch_shapes=[
                pltpu.VMEM((2, 4, own.shape[0], part), F32), pltpu.SemaphoreType.DMA((2, 4)),
            ],
        ),
        input_output_aliases={3: 0, 4: 1} if into else {},
        cost_estimate=lasting(3),
        compiler_params=params(),
    )(places, own, sib, *into)


def per_device(
    links, joint_links, block_in, lengths, attn_gain, attn_bias, feed_gain, feed_bias, joint_weight, joint_bias,
    dense_weight, dense_bias, expand_weight, expand_bias, contract_weight, contract_bias, out_cotangent,
):
    rows_here, chunk, features = block_in.shape
    tokens = rows_here * chunk
    total = 2 * tokens
    segs = lengths.shape[1]
    heads = H // 2
    part = features // 2
    units = expand_weight.shape[1] // 4
    x_at, core_at = lax.axis_index("x"), lax.axis_index("core")
    chunk_at = x_at * 2 + core_at

    x_own, dy_own = block_in.reshape(tokens, features), out_cotangent.reshape(tokens, features)
    x_sib, dy_sib = swap_core(x_own), swap_core(dy_own)
    away = jnp.stack([
        lax.dynamic_index_in_dim(block_in, 1 - x_at, 0, keepdims=False),
        lax.dynamic_index_in_dim(out_cotangent, 1 - x_at, 0, keepdims=False),
    ])
    near = swap_x(away)

    mine = lax.dynamic_index_in_dim(lengths, x_at, 0, keepdims=False)
    before = jnp.tril(jnp.ones((segs, segs), jnp.int32))
    bounds = jnp.sum(before * mine[None, :], axis=1)
    bounds = jnp.where(jnp.arange(segs) == segs - 1, chunk_at, bounds).astype(jnp.int32)
    slots = jnp.arange(4, dtype=jnp.int32)
    starts = (((slots & 1) * 2 + (slots >> 1)) ^ chunk_at) * chunk
    pos = (starts[:, None] + jnp.arange(chunk, dtype=jnp.int32)[None, :]).reshape(1, total)
    inverse = BASE_FREQ ** (-2.0 * jnp.arange(HALF).astype(F32) / RD)
    angles = inverse[:, None] * pos.astype(F32)
    cos, sin = jnp.cos(angles), jnp.sin(angles)

    pack = jnp.concatenate([
        attn_gain, attn_bias, feed_gain, feed_bias, dense_bias + contract_bias, expand_bias, joint_bias,
    ]).reshape(-1, features)
    pack = jnp.pad(pack, ((0, 16 - pack.shape[0]), (0, 0)))

    bits = [links.bit(n) for n in range(links.rounds)]
    of = lambda group: [bits[n] for n in group]
    sib_bit = links.bit(0, True)
    places = jnp.stack(
        [core_at * 2 + 1 - bits[0], core_at * 2 + bits[0], core_at, x_at, 1 - bits[0], bits[0],
         1 - sib_bit, sib_bit]
    ).astype(jnp.int32)

    joint_bit, joint_sib_bit = joint_links.bit(0), joint_links.bit(0, True)
    joint_places = jnp.concatenate([
        places[:4], jnp.stack([1 - joint_bit, joint_bit, 1 - joint_sib_bit, joint_sib_bit]).astype(jnp.int32),
    ])

    def feed(number, x, deps):
        base = (places[number] * (units // 256)).reshape(1)
        return feed_part(base, x, dy_own, dy_sib, pack, expand_weight, contract_weight, units, deps)

    sent = feed(0, (x_own, x_sib), (away,))
    arrived = links.swap(sent[0], 0)
    kept = feed(1, sent[5:], (sent[0],))
    near = once(near, (kept[0],))
    far = swap_core(near)

    flat = lambda a: a.reshape(2 * units, features)
    first, second, *rest = links.groups
    stay, outgoing = divide(
        of(second), [flat(kept[0]), flat(arrived)], (cos, sin, pos, bounds, joint_places)
    )
    terms = [stay, links.swap(outgoing, *second)]
    normed_t, qkv, mix_t = project(
        places, x_own, x_sib, dy_own, dy_sib, near, far, pack, joint_weight, dense_weight, cos, sin,
        heads, (outgoing,),
    )
    ready = normed_t
    for number, group in enumerate(rest):
        stay, *outgoing = divide(of(group), terms, (ready,))
        terms = [stay, *links.swap_group(outgoing, group)]
        ready = stay
        if number == 0:
            out_sib, back_sib = products(places, sent, kept, contract_weight, expand_weight, True, (stay,))
            ready = out_sib
    out_own, back_own = products(places, sent, kept, contract_weight, expand_weight, False, (stay,))
    out_sib, back_sib = swap_core(out_sib), swap_core(back_sib)
    terms[-1] = once(terms[-1], (out_own,))
    last = total_of(terms)
    gathered = lax.all_gather(last, CHIP, axis=0, tiled=True)
    mixed_own, mixed_far, *grads = attention(bounds, qkv, mix_t, pos, cos, sin, chunk, segs, (last,))
    mixed_own, mixed_far = mixed_own.reshape(part, tokens), mixed_far.reshape(part, tokens)
    grads = [g.reshape(3, part, tokens) for g in grads]
    bits = [joint_links.bit(n) for n in range(joint_links.rounds)]
    grads_sib = swap_core(grads[1])
    mixed = (mixed_own, mixed_far)
    outgoing, current, joint_b = joint_grads(
        joint_places, normed_t, grads, mixed, dy_own, dy_sib, near, far
    )
    arrived = joint_links.swap(outgoing, *first)
    mixed_sib = swap_core(once(mixed_far, (grads[0],)))
    mixed_near = swap_x(jnp.concatenate([mixed_own[:, chunk:], mixed_sib[:, chunk:]], axis=0))
    dx_own, dx_far, gain_attn, bias_attn = norm_back(
        places, grads[0], grads_sib, joint_weight, x_own, near, pack, (current,)
    )
    dx_near = swap_x(dx_far)
    stay, outgoing = divide(of(second), [current, arrived], (dx_own,))
    terms = [stay, joint_links.swap(outgoing, *second)]
    block_out = block_result(
        places, x_own, out_own, out_sib, mixed_own, mixed_sib, mixed_near, dense_weight, pack, (stay,)
    )
    ready = block_out
    for number, group in enumerate(rest):
        stay, *outgoing = divide(of(group), terms, (ready,))
        terms = [stay, *joint_links.swap_group(outgoing, group)]
        ready = stay
        if number == 0:
            grad_contract_w, grad_expand_w = spread(gathered, links, features, units, (stay,))
            ready = grad_contract_w
    input_grad, small = input_result(
        places, x_own, dy_own, back_own, back_sib, dx_own, dx_near, pack,
        (gain_attn, bias_attn, sent[4], sent[3], kept[3]), joint_b, (ready,),
    )
    terms[-1] = once(terms[-1], (input_grad,))
    current = total_of(terms)

    shared = 5 * features

    def summed(group, small):
        pair, small = two_parts(small)
        outgoing = jnp.concatenate([current, pair], axis=0)
        rows_now = current.shape[0]
        arrived = [joint_links.swap(outgoing, *numbers) for numbers in joint_links.others(group)]
        parts = [small] + [one_part(array[rows_now:]) for array in arrived]
        while len(parts) > 1:
            parts = [a + b for a, b in zip(parts[::2], parts[1::2])]
        return in_order(of(group), [current] + [array[:rows_now] for array in arrived]), parts[0]

    for group in reversed(rest):
        current, small = summed(group, small)
    pair, small = two_parts(small)
    rows_now = current.shape[0]
    outgoing = jnp.concatenate([current, pair], axis=0)
    arrived = joint_links.swap(outgoing, *second)
    one, both = joint_links.swap(pair, *first), joint_links.swap(pair, *first, *second)
    small = (small + one_part(arrived[rows_now:])) + (one_part(one) + one_part(both))
    current = in_order(of(second), [current, arrived[:rows_now]])
    arrived = joint_links.swap(current, *first)
    sib_current = swap_core(current)
    pair, small = two_parts(small)
    small_sib = one_part(swap_core(pair)).reshape(-1)
    small = small.reshape(-1)
    sums = (small + small_sib)[:shared].reshape(5, features)
    ordered = lambda a, b: jnp.where(core_at == 0, jnp.stack([a, b]), jnp.stack([b, a]))
    single = ordered(small[shared:], small_sib[shared:])
    grad_expand_b = single[:, : 2 * units].reshape(-1)
    grad_joint_b = single[:, 2 * units : 2 * units + 3 * part].reshape(2, 3, part).transpose(1, 0, 2).reshape(-1)
    into = spread_joint(joint_places, current, sib_current, features, 1)
    arrived = once(arrived, (into[0], sums, grad_joint_b, grad_expand_b))
    grad_joint_w, grad_dense_w = spread_joint(
        joint_places, arrived, swap_core(arrived), features, 0, into
    )
    return (
        block_out.reshape(block_in.shape),
        input_grad.reshape(block_in.shape),
        sums[0],
        sums[1],
        sums[2],
        sums[3],
        grad_joint_w,
        grad_joint_b,
        grad_dense_w,
        sums[4],
        grad_expand_w,
        grad_expand_b,
        grad_contract_w,
        sums[4],
    )


def solution(mesh):
    row_count, seq_count = mesh.devices.shape
    chips = Mesh(mesh.devices.reshape(row_count, seq_count // 2, 2), CHIP)
    links = Links(row_count)
    tokens = P("rows", ("x", "core"), None)
    in_specs = (tokens, P("rows", None)) + (P(),) * 12 + (tokens,)
    out_specs = (tokens, tokens) + (P(),) * 12
    return jax.shard_map(
        functools.partial(per_device, links, Links(row_count, True)), mesh=chips, in_specs=in_specs, out_specs=out_specs,
        check_vma=False,
    )
```
